512 devices in a mesh: bank: 16 (over x, z_hi), blk: 32 (over z_lo, y, core).
Axes of the slice: x: 4, y: 8, z: 8 (z_hi: 4, z_lo: 2; z = z_hi * 2 + z_lo), core: 2. Of those that a mesh axis runs over, the one named last changes fastest.
Arguments:
- k_store: bfloat16 [512, 512, 1024], P(('bank', 'blk')), may hold values from -6 to 6
- v_store: bfloat16 [512, 512, 1024], P(('bank', 'blk')), may hold values from -6 to 6
- pos_offset: int32 [512], replicated, may hold values from 0 to 8191
- owner_map: int32 [512], replicated, may hold values from 0 to 511, as said below
- passage_ids: int32 [32], replicated, may hold values from 0 to 511, as said below
- rec_index: int32 [32, 128], P('blk'), may hold values from 0 to 511, as said below
- rec_count: int32 [32], P('blk'), may hold values from 42 to 128, as said below
- fresh_q: bfloat16 [4096, 12288], P('blk', 'bank'), may hold values from -6 to 6
- fresh_k: bfloat16 [4096, 1024], P('blk'), may hold values from -6 to 6
- fresh_v: bfloat16 [4096, 1024], P('blk'), may hold values from -6 to 6
- ques_q: bfloat16 [512, 12288], P('blk', 'bank'), may hold values from -8 to 8
- ques_k: bfloat16 [512, 1024], P('blk'), may hold values from -8 to 8
- ques_v: bfloat16 [512, 1024], P('blk'), may hold values from -6 to 6
Outputs:
- rec_out: bfloat16 [4096, 12288], P('blk', 'bank')
- ques_out: bfloat16 [512, 12288], P('blk', 'bank')
The draws below stay inside these ranges and needn't reach their ends.
Inputs may be any that keep to these rules, and one draw needn't show every extreme that they name: `owner_map`: a permutation of the 512 store slots; slot n lies on the device of flat index n over bank+blk. The slot owner_map[passage_ids[s]] equals o * 32 + s for some bank index o. `rec_index`: each row holds 128 distinct positions in rising order. `rec_count`: some passage uses all 128 slots in every draw.
All inputs are finite; a program needn't handle non-finite values.
Results may differ from the reference program's by a relative error of at most 0.017.
Values may be sent and summed in bfloat16 or wider, within the bound.
A program may use at most 64 MiB of HBM per device.

```python
import jax
import jax.numpy as jnp
from jax import lax

QH = 96
KVH = 8
HD = 128
PT = 512
RECP = 128
ST_DEV = 1
PASS = 32
QLEN = 512
STORE = 512


def shared_catalog(key):
    return jax.random.permutation(key, STORE).astype(jnp.int32)


def draw_owner_map(key, part):
    return shared_catalog(key)


def draw_passage_ids(key, part):
    placed = shared_catalog(key)
    key = jax.random.fold_in(key, 5)
    inverse = jnp.argsort(placed).astype(jnp.int32)
    first_key, second_key = jax.random.split(key)
    banks = STORE // (ST_DEV * PASS)
    owners = jax.random.randint(first_key, (PASS,), 0, banks)
    within = jax.random.randint(second_key, (PASS,), 0, ST_DEV)
    target = placed[STORE - 1]
    target_pass = target // ST_DEV % PASS
    target_owner = target // (ST_DEV * PASS)
    target_within = target % ST_DEV
    chosen = jnp.arange(PASS) == target_pass
    owners = jnp.where(chosen, target_owner, owners)
    within = jnp.where(chosen, target_within, within)
    slots = (owners * PASS + jnp.arange(PASS)) * ST_DEV + within
    return inverse[slots].astype(jnp.int32)


def draw_rec_index(key, part):
    key = jax.random.fold_in(key, 7)
    keys = jax.random.split(key, PASS)

    def one_row(row_key):
        return jnp.sort(jax.random.permutation(row_key, PT)[:RECP])
    return jax.vmap(one_row)(keys).astype(jnp.int32)


def draw_rec_count(key, part):
    key = jax.random.fold_in(key, 9)
    first_key, second_key = jax.random.split(key)
    counts = jax.random.randint(first_key, (PASS,), RECP // 3, RECP + 1)
    chosen = jax.random.randint(second_key, (), 0, PASS)
    return jnp.where(jnp.arange(PASS) == chosen, RECP, counts).astype(jnp.int32)


def draw_ques_k(key, part):
    own_key = jax.random.fold_in(key, 13)
    base = jnp.clip(jax.random.normal(own_key, (QLEN, KVH * HD), jnp.float32), -6.0, 6.0)
    return base.astype(jnp.bfloat16)


def draw_ques_q(key, part):
    own_key = jax.random.fold_in(key, 17)
    base = jnp.clip(jax.random.normal(own_key, (QLEN, QH * HD), jnp.float32), -6.0, 6.0)
    return base.astype(jnp.bfloat16)


def touch_ends(result, key, low, largest):
    shape = result.shape
    index_at = [jax.random.randint(jax.random.fold_in(key, axis), (), 0, shape[axis]) for axis in range(len(shape))]
    result = result.at[tuple(index_at)].set(low)
    longest = shape.index(max(shape))
    index_at[longest] = (index_at[longest] + 1) % shape[longest]
    return result.at[tuple(index_at)].set(largest)


def block_levels(key, extent, cuts, smallest, top_value):
    factor_of, own = 1.0, jax.random.fold_in(key, 6)
    for dim, blocks in cuts:
        draws = jnp.exp(jax.random.uniform(jax.random.fold_in(own, dim), (blocks,), jnp.float32, smallest / len(cuts), top_value / len(cuts)))
        factor_of = factor_of * jnp.repeat(draws, extent[dim] // blocks).reshape([-1 if axis == dim else 1 for axis in range(len(extent))])
    return factor_of


def normal_values(key, extent, deviation, bound, pieces=(), held_as=jnp.bfloat16):
    loudness = block_levels(key, extent, pieces, -0.22, 0.18) if pieces else 1.0
    drawn = jax.random.normal(key, extent, jnp.float32) * deviation * loudness
    return jnp.minimum(jnp.maximum(drawn, -bound), bound).astype(held_as)


def setup_inputs(seed: int = 0) -> dict:
    splits = jax.random.split(jax.random.key(seed), 14)
    k_store = normal_values(splits[0], (STORE, PT, KVH * HD), 1.0, 6.0, ((0, 512),))
    v_store = normal_values(splits[1], (STORE, PT, KVH * HD), 1.0, 6.0, ((0, 512),))
    pos_offset = touch_ends(jax.random.randint(splits[2], (STORE,), 0, 8192), jax.random.fold_in(splits[2], 1), 0, 8191).astype(jnp.int32)
    owner_map = draw_owner_map(jax.random.fold_in(splits[13], 71), 0)
    passage_ids = draw_passage_ids(jax.random.fold_in(splits[13], 71), 0)
    rec_index = draw_rec_index(jax.random.fold_in(splits[13], 71), 0)
    rec_count = draw_rec_count(jax.random.fold_in(splits[13], 71), 0)
    fresh_q = normal_values(splits[7], (PASS * RECP, QH * HD), 1.0, 6.0, ((0, 32), (1, 16)))
    fresh_k = normal_values(splits[8], (PASS * RECP, KVH * HD), 1.0, 6.0, ((0, 32),))
    fresh_v = normal_values(splits[9], (PASS * RECP, KVH * HD), 1.0, 6.0, ((0, 32),))
    ques_q = draw_ques_q(jax.random.fold_in(splits[13], 71), 0)
    ques_k = draw_ques_k(jax.random.fold_in(splits[13], 71), 0)
    ques_v = normal_values(splits[12], (QLEN, KVH * HD), 1.0, 6.0, ((0, 32),))
    return {"k_store": k_store, "v_store": v_store, "pos_offset": pos_offset, "owner_map": owner_map, "passage_ids": passage_ids, "rec_index": rec_index, "rec_count": rec_count, "fresh_q": fresh_q, "fresh_k": fresh_k, "fresh_v": fresh_v, "ques_q": ques_q, "ques_k": ques_k, "ques_v": ques_v}


rope_theta = 1000000.0
mask_floor = -1e+30

def rotate(values, positions):
    count = values.shape[0]
    heads = values.shape[1] // HD
    half = HD // 2
    parts = values.astype(jnp.float32).reshape(count, heads, HD)
    inverse = rope_theta ** (-jnp.arange(half).astype(jnp.float32) * 2.0 / HD)
    angles = positions.astype(jnp.float32)[:, None] * inverse[None, :]
    cosine = jnp.cos(angles)[:, None, :]
    sine = jnp.sin(angles)[:, None, :]
    first = parts[:, :, :half]
    second = parts[:, :, half:]
    turned = jnp.concatenate([first * cosine - second * sine, second * cosine + first * sine], axis=2)
    return turned.reshape(count, heads * HD).astype(jnp.bfloat16)

def pick_block(total, limit):
    size = min(total, limit)
    while total % size != 0:
        size = size - 1
    return size

def reference(k_store, v_store, pos_offset, owner_map, passage_ids, rec_index, rec_count, fresh_q, fresh_k, fresh_v, ques_q, ques_k, ques_v):
    slots = owner_map[passage_ids].astype(jnp.int32)
    starts = (jnp.arange(PASS) * PT).astype(jnp.int32)
    tokens = jnp.arange(PT).astype(jnp.int32)
    slot_rows = jnp.arange(RECP).astype(jnp.int32)

    def blend(items):
        slot, start, index, count, new_keys, new_values = items
        cached_k = rotate(k_store[slot], start - pos_offset[slot] + tokens)
        cached_v = v_store[slot]
        fresh_rot = rotate(new_keys, start + index)
        target = jnp.where(slot_rows < count, index, PT)
        return (cached_k.at[target].set(fresh_rot, mode='drop'), cached_v.at[target].set(new_values, mode='drop'))
    keys_pass, values_pass = lax.map(blend, (slots, starts, rec_index, rec_count, fresh_k.reshape(PASS, RECP, KVH * HD), fresh_v.reshape(PASS, RECP, KVH * HD)))
    ques_pos = (PASS * PT + jnp.arange(QLEN)).astype(jnp.int32)
    keys = jnp.concatenate([keys_pass.reshape(PASS * PT, KVH * HD), rotate(ques_k, ques_pos)], axis=0)
    values = jnp.concatenate([values_pass.reshape(PASS * PT, KVH * HD), ques_v], axis=0)
    key_pos = jnp.arange(PASS * PT + QLEN).astype(jnp.int32)
    rec_pos = (starts[:, None] + rec_index).reshape(PASS * RECP)
    queries = jnp.concatenate([rotate(fresh_q, rec_pos), rotate(ques_q, ques_pos)], axis=0)
    query_pos = jnp.concatenate([rec_pos, ques_pos], axis=0)
    rows = PASS * RECP + QLEN
    group = QH // KVH
    block = pick_block(rows, 512)
    scale = 1.0 / math_sqrt(HD)
    by_head = queries.reshape(rows, KVH, group, HD).transpose(1, 0, 2, 3)
    key_heads = keys.reshape(-1, KVH, HD).transpose(1, 0, 2)
    value_heads = values.reshape(-1, KVH, HD).transpose(1, 0, 2)

    def one_head(items):
        head_q, head_k, head_v = items
        key_f = head_k.astype(jnp.float32)
        value_f = head_v.astype(jnp.float32)

        def one_block(items2):
            block_q, block_pos = items2
            scores = jnp.einsum('rgd,nd->rgn', block_q.astype(jnp.float32), key_f) * scale
            allowed = key_pos[None, None, :] <= block_pos[:, None, None]
            scores = jnp.where(allowed, scores, mask_floor)
            top = lax.optimization_barrier(jnp.max(scores, axis=-1, keepdims=True))
            probs = jnp.where(allowed, jnp.exp(scores - top), 0.0)
            total = lax.optimization_barrier(jnp.sum(probs, axis=-1))
            weights = probs.astype(jnp.bfloat16).astype(jnp.float32)
            return jnp.einsum('rgn,nd->rgd', weights, value_f) / total[:, :, None]
        outs = lax.map(one_block, (head_q.reshape(rows // block, block, group, HD), query_pos.reshape(rows // block, block)))
        return outs.reshape(rows, group, HD)
    out = lax.map(one_head, (by_head, key_heads, value_heads))
    out = out.transpose(1, 0, 2, 3).reshape(rows, QH * HD)
    valid = (slot_rows[None, :] < rec_count[:, None]).reshape(PASS * RECP)
    rec_out = jnp.where(valid[:, None], out[:PASS * RECP], 0.0).astype(jnp.bfloat16)
    ques_out = out[PASS * RECP:].astype(jnp.bfloat16)
    return (rec_out, ques_out)

def math_sqrt(number):
    return float(number) ** 0.5
```

```python
import functools

import jax
import jax.numpy as jnp
import numpy as np
from jax import lax
from jax.experimental import pallas as pl
from jax.experimental.pallas import tpu as pltpu
from jax.sharding import PartitionSpec as P

HD = 128
PT = 512
RECP = 128
QDEV = 16
PASS = 32
HEADS = 6
ROWS = HEADS * RECP
QROWS = HEADS * QDEV
QSTART = PASS * PT
CHUNK = 512
FLOOR = -1e30
SCALE = float(np.log2(np.e) / np.sqrt(128.0))
MESH = pl.DeviceIdType.MESH
F32 = jnp.float32
BF16 = jnp.bfloat16

INV_2PI = float(1.0 / (2.0 * np.pi))
PI_A = 6.28125
PI_B = 0.0019350051879882812
PI_C = 3.0199159795074593e-07
SIN_C = [float((-1.0) ** k / np.prod(np.arange(1, 2 * k + 2, dtype=np.float64))) for k in range(9)]
COS_C = [float((-1.0) ** k / np.prod(np.arange(1, 2 * k + 1, dtype=np.float64))) for k in range(10)]


def freq_table():
    half = HD // 2
    freqs = 1000000.0 ** (-np.arange(half, dtype=np.float64) * 2.0 / HD)
    return np.concatenate([freqs, freqs])[None, :].astype(np.float32)


def cos_sin(pos, freq):
    angle = pos * freq
    turns = jnp.floor(angle * INV_2PI + 0.5)
    r = ((angle - turns * PI_A) - turns * PI_B) - turns * PI_C
    r2 = r * r
    s = jnp.full_like(r, SIN_C[8])
    for k in range(7, -1, -1):
        s = s * r2 + SIN_C[k]
    s = s * r
    c = jnp.full_like(r, COS_C[9])
    for k in range(8, -1, -1):
        c = c * r2 + COS_C[k]
    lane = lax.broadcasted_iota(jnp.int32, s.shape, 1)
    return c, jnp.where(lane < HD // 2, -s, s)


def turn(x, c, s):
    return x * c + pltpu.roll(x, HD // 2, 1) * s


def eye_mask(n, m):
    row = lax.broadcasted_iota(jnp.int32, (n, m), 0)
    col = lax.broadcasted_iota(jnp.int32, (n, m), 1)
    return row == col


def to_col(row, n):
    full = jnp.broadcast_to(row, (n, 128))
    return jnp.sum(jnp.where(eye_mask(n, 128), full, 0.0), axis=1, keepdims=True)


def to_row(col, n):
    return jnp.sum(jnp.where(eye_mask(n, 128), col, 0.0), axis=0, keepdims=True)


def nt_dot(a, b):
    return lax.dot_general(a, b, (((1,), (1,)), ((), ())), preferred_element_type=F32)


def kernel(
    pos_off, owner_map, pids, rec_count, rec_index, fresh_q, fresh_k, fresh_v,
    ques_q, ques_k, ques_v, freq_ref, k_store, v_store,
    rec_out, ques_out,
    xfin0, xfin1, mb00, mb01, mb10, mb11, msend, zsend, zin0, zin1, tab, hit, kall, vall, kq, vq,
    qrec, qques, qpos, sbuf, sq, osend, oqsend, orecv, oqrecv, lsend, lrecv,
    lsem, xs, xr, zs, zr, qs, qr, ps, pr, ns, nr, cs, cr, os_, or_,
):
    bank = lax.axis_index("bank")
    blk = lax.axis_index("blk")
    x = lax.div(bank, 4)
    z_hi = lax.rem(bank, 4)
    zh = lax.div(z_hi, 2)
    b1 = lax.rem(z_hi, 2)
    z_lo = lax.div(blk, 16)
    g = lax.rem(blk, 16)
    y = lax.div(g, 2)
    core = lax.rem(g, 2)
    zc = 2 * z_hi + z_lo
    z4 = 2 * b1 + z_lo
    head = 2 * x + zh

    def dev(xx, zz, gg):
        return (xx * 4 + lax.div(zz, 2), lax.rem(zz, 2) * 16 + gg)

    x_up = dev(lax.rem(x + 1, 4), zc, g)
    x_dn = dev(lax.rem(x + 3, 4), zc, g)
    y_up = dev(x, zc, lax.rem(y + 1, 8) * 2 + core)
    y_dn = dev(x, zc, lax.rem(y + 7, 8) * 2 + core)
    twin = dev(x, zc, y * 2 + 1 - core)

    def z_dev(i):
        return dev(x, lax.rem(zc + i, 8), g)

    def z4_dev(i):
        return dev(x, 4 * zh + lax.rem(z4 + i, 4), g)

    def rcopy(src, dst, ssem, rsem, where):
        return pltpu.make_async_remote_copy(
            src_ref=src, dst_ref=dst, send_sem=ssem, recv_sem=rsem,
            device_id=where, device_id_type=MESH,
        )

    xfin = (xfin0, xfin1)
    mbuf = ((mb00, mb01), (mb10, mb11))
    zin = (zin0, zin1)

    def slot_of(passage):
        return owner_map[pids[passage]]

    slot = slot_of(blk)
    owner_x = lax.div(slot, 128)
    off = pos_off[slot]
    count = rec_count[0]

    barrier = pltpu.get_barrier_semaphore()
    peers = [x_up, x_dn, y_up, y_dn, twin] + [z_dev(i) for i in range(1, 8)]
    for peer in peers:
        pl.semaphore_signal(barrier, inc=1, device_id=peer, device_id_type=MESH)
    pl.semaphore_wait(barrier, len(peers))

    stores = (k_store, v_store)

    def cols(xx):
        return pl.ds(pl.multiple_of(lax.rem(xx, 4) * 256, 256), 256)

    top = pl.ds(0, 256)
    low = pl.ds(256, 256)

    def x_first(part):
        st = stores[part].at[0]
        copies = [
            rcopy(st.at[top, cols(x + 2)], mbuf[part][0].at[1], xs.at[part, 0], xr.at[part, 0], x_up),
            rcopy(st.at[low, cols(x + 2)], mbuf[part][1].at[1], xs.at[part, 1], xr.at[part, 1], x_dn),
            rcopy(st.at[low, cols(x + 1)], xfin[part].at[1, 1], xs.at[part, 2], xr.at[part, 2], x_up),
            rcopy(st.at[top, cols(x + 3)], xfin[part].at[2, 0], xs.at[part, 3], xr.at[part, 3], x_dn),
        ]
        for c in copies:
            c.start()
        return copies

    def x_local(part):
        st = stores[part].at[0]
        copies = [
            pltpu.make_async_copy(st.at[top, cols(x + 1)], mbuf[part][0].at[0], lsem.at[part, 0]),
            pltpu.make_async_copy(st.at[low, cols(x + 3)], mbuf[part][1].at[0], lsem.at[part, 1]),
            pltpu.make_async_copy(st.at[top, cols(x)], xfin[part].at[0, 0], lsem.at[part, 2]),
            pltpu.make_async_copy(st.at[low, cols(x)], xfin[part].at[0, 1], lsem.at[part, 3]),
        ]
        for c in copies:
            c.start()
        return copies

    def x_second(part, first, local):
        local[0].wait()
        first[0].wait_recv()
        from_dn = jnp.where(owner_x == lax.rem(x + 3, 4), 1, 0)
        msend[part, 0] = mbuf[part][0][from_dn]
        c4 = rcopy(msend.at[part, 0], xfin[part].at[1, 0], xs.at[part, 4], xr.at[part, 4], x_up)
        c4.start()
        local[1].wait()
        first[1].wait_recv()
        from_up = jnp.where(owner_x == lax.rem(x + 1, 4), 1, 0)
        msend[part, 1] = mbuf[part][1][from_up]
        c5 = rcopy(msend.at[part, 1], xfin[part].at[2, 1], xs.at[part, 5], xr.at[part, 5], x_dn)
        c5.start()
        return [c4, c5]

    def x_finish(part, first, second, local):
        local[2].wait()
        local[3].wait()
        first[2].wait_recv()
        first[3].wait_recv()
        for c in second:
            c.wait_recv()
        is_own = owner_x == x
        idx_a = jnp.where(is_own, 0, jnp.where(owner_x == lax.rem(x + 1, 4), 2, 1))
        idx_b = jnp.where(is_own, 0, jnp.where(owner_x == lax.rem(x + 3, 4), 1, 2))
        fresh = (fresh_k, fresh_v)[part]
        fcols = fresh[:, cols(x)]
        for quarter in range(4):
            half, r0 = quarter // 2, (quarter % 2) * 128
            idx = idx_a if half == 0 else idx_b
            data = xfin[part][idx, half, r0:r0 + 128, :].astype(F32)
            onehot = hit[quarter]
            repl = jnp.dot(onehot, fcols, preferred_element_type=F32)
            found = jnp.sum(onehot.astype(F32), axis=1, keepdims=True) > 0.5
            data = jnp.where(found, repl, data)
            for hh in range(2):
                piece = data[:, hh * 128:(hh + 1) * 128]
                if part == 0:
                    piece = turn(piece, tab[quarter, 0], tab[quarter, 1])
                zsend[part, quarter, hh] = piece.astype(BF16)
        copies = []
        for i in range(1, 8):
            t = lax.rem(zc + i, 8)
            c = rcopy(
                zsend.at[part, lax.rem(t, 4), lax.div(t, 4)], zin[part].at[i],
                zs.at[part, i - 1], zr.at[part, i - 1], z_dev(i),
            )
            c.start()
            copies.append(c)
        zin[part][0] = zsend[part, z4, zh]
        return copies

    def z_finish(part, copies):
        for c in copies:
            c.wait_recv()
        for c in range(2):
            owner_z = lax.rem(lax.div(slot_of(c * 16 + g), 32), 4)
            idx = lax.rem(zc + 8 - (2 * owner_z + c), 8)
            block = zin[part][idx]
            rows = pl.ds(pl.multiple_of(g * 128, 128), 128)
            if part == 0:
                kall[c, rows, :] = block
            else:
                vall[c, rows, 0:128] = block

    def gather_slices(fam, gg):
        if fam == 0:
            return kall.at[:, pl.ds(pl.multiple_of(gg * 128, 128), 128), :]
        if fam == 1:
            return vall.at[:, pl.ds(pl.multiple_of(gg * 128, 128), 128), pl.ds(0, 128)]
        if fam == 2:
            return kq.at[pl.ds(pl.multiple_of(gg * 16, 16), 16), :]
        return vq.at[pl.ds(pl.multiple_of(gg * 16, 16), 16), pl.ds(0, 128)]

    def reach(fam):
        return (4, 3) if fam % 2 == 0 else (3, 4)

    def at_y(dy):
        return lax.rem(y + 8 + dy, 8) * 2 + core

    sent = []

    def g_send(fam, dy, which, hop):
        piece = gather_slices(fam, at_y(dy))
        if which == "up":
            c = rcopy(piece, piece, ps.at[fam, hop], pr.at[fam, hop], y_up)
        elif which == "dn":
            c = rcopy(piece, piece, ns.at[fam, hop], nr.at[fam, hop], y_dn)
        else:
            c = rcopy(piece, piece, cs.at[fam, hop], cr.at[fam, hop], twin)
        c.start()
        sent.append(c)

    def g_wait(fam, dy, which, hop):
        if which == "up":
            piece = gather_slices(fam, at_y(dy))
            rcopy(piece, piece, ps.at[fam, hop], pr.at[fam, hop], y_up).wait_recv()
        elif which == "dn":
            piece = gather_slices(fam, at_y(dy))
            rcopy(piece, piece, ns.at[fam, hop], nr.at[fam, hop], y_dn).wait_recv()
        else:
            piece = gather_slices(fam, lax.rem(y + 8 + dy, 8) * 2 + 1 - core)
            rcopy(piece, piece, cs.at[fam, hop], cr.at[fam, hop], twin).wait_recv()

    def g_start(fam):
        g_send(fam, 0, "up", 0)
        g_send(fam, 0, "dn", 0)
        g_send(fam, 0, "twin", 0)

    def g_step(fam, d):
        n_up, n_dn = reach(fam)
        if d <= n_up:
            g_wait(fam, -d, "up", d - 1)
            if d < n_up:
                g_send(fam, -d, "up", d)
            g_send(fam, -d, "twin", d)
        if d <= n_dn:
            g_wait(fam, d, "dn", d - 1)
            if d < n_dn:
                g_send(fam, d, "dn", d)
            g_send(fam, d, "twin", d if d == 4 else 4 + d)

    def g_end(fam):
        n_up, n_dn = reach(fam)
        g_wait(fam, 0, "twin", 0)
        for d in range(1, n_up + 1):
            g_wait(fam, -d, "twin", d)
        for d in range(1, n_dn + 1):
            g_wait(fam, d, "twin", d if d == 4 else 4 + d)

    loc_k = x_local(0)
    first_k = x_first(0)
    loc_v = x_local(1)

    freq = freq_ref[...]
    rec_row = rec_index[...].astype(F32)
    rec_pos_row = rec_row + (blk * PT).astype(F32)
    rec_pos = to_col(rec_pos_row, 128)
    c_rec, s_rec = cos_sin(rec_pos, freq)
    ques_pos = (
        lax.broadcasted_iota(jnp.int32, (QDEV, 1), 0) + (QSTART + blk * QDEV)
    ).astype(F32)
    c_q, s_q = cos_sin(ques_pos, freq)
    for hh in range(HEADS):
        lanes = slice(hh * 128, (hh + 1) * 128)
        q = turn(fresh_q[:, lanes].astype(F32), c_rec, s_rec) * SCALE
        qrec[z4, hh * 128:(hh + 1) * 128, :] = q.astype(BF16)
        q = turn(ques_q[:, lanes].astype(F32), c_q, s_q) * SCALE
        qques[z4, hh * 16:(hh + 1) * 16, :] = q.astype(BF16)
    qpos[z4] = jnp.broadcast_to(rec_pos_row, (8, 128))
    q_copies = []
    for i in range(1, 4):
        for j, ref in enumerate((qrec, qques, qpos)):
            c = rcopy(ref.at[z4], ref.at[z4], qs.at[i - 1, j], qr.at[i - 1, j], z4_dev(i))
            c.start()
            q_copies.append((i, j, c))

    vall[:, :, 128:256] = jnp.ones((2, 2048, 128), BF16)
    vq[:, 128:256] = jnp.ones((256, 128), BF16)
    hcol = pl.ds(pl.multiple_of(head * 128, 128), 128)
    my_rows = pl.ds(pl.multiple_of(g * 16, 16), 16)
    kq[my_rows, :] = turn(ques_k[:, hcol].astype(F32), c_q, s_q).astype(BF16)
    vq[my_rows, 0:128] = ques_v[:, hcol]

    second_k = x_second(0, first_k, loc_k)
    first_v = x_first(1)
    g_start(2)
    g_start(3)

    off_f = off.astype(F32)
    base_f = (blk * PT).astype(F32)
    slot_lane = lax.broadcasted_iota(jnp.int32, (128, 128), 1)
    for quarter in range(4):
        tok = lax.broadcasted_iota(jnp.int32, (128, 128), 0) + quarter * 128
        match = (tok.astype(F32) == jnp.broadcast_to(rec_row, (128, 128))) & (slot_lane < count)
        onehot = jnp.where(match, 1.0, 0.0)
        hit[quarter] = onehot.astype(BF16)
        found = jnp.sum(onehot, axis=1, keepdims=True) > 0.5
        tpos = (lax.broadcasted_iota(jnp.int32, (128, 1), 0) + quarter * 128).astype(F32) + base_f
        tpos = tpos - jnp.where(found, 0.0, off_f)
        c_t, s_t = cos_sin(tpos, freq)
        tab[quarter, 0] = c_t
        tab[quarter, 1] = s_t

    z_k = x_finish(0, first_k, second_k, loc_k)
    second_v = x_second(1, first_v, loc_v)
    for d in range(1, 5):
        g_step(2, d)
        g_step(3, d)
    z_finish(0, z_k)
    g_start(0)
    z_v = x_finish(1, first_v, second_v, loc_v)
    for d in range(1, 5):
        g_step(0, d)
    z_finish(1, z_v)
    g_start(1)
    for d in range(1, 5):
        g_step(1, d)
    for fam in range(4):
        g_end(fam)
    for i, j, c in q_copies:
        c.wait_recv()

    lsend[...] = jnp.zeros((4, 8, 128), F32)
    key_lane = lax.broadcasted_iota(jnp.int32, (1, CHUNK), 1)
    key_off = lax.div(key_lane, 128) * PT + lax.rem(key_lane, 128) + z4 * 128
    key_off = key_off.astype(F32)

    def k_chunk(ch):
        return kall[lax.div(ch, 4), pl.ds(pl.multiple_of(lax.rem(ch, 4) * CHUNK, CHUNK), CHUNK), :]

    def v_chunk(ch):
        return vall[lax.div(ch, 4), pl.ds(pl.multiple_of(lax.rem(ch, 4) * CHUNK, CHUNK), CHUNK), :]

    def fold(s):
        m = s[:, 0:128]
        for j in range(1, s.shape[1] // 128):
            m = jnp.maximum(m, s[:, j * 128:(j + 1) * 128])
        return m

    def scores(q, ch, rows, m):
        s = nt_dot(q, k_chunk(ch))
        sbuf[ch, 0:rows, :] = s
        return jnp.maximum(m, fold(s))

    def weigh(ch, rows, m, acc):
        p = jnp.exp2(sbuf[ch, 0:rows, :] - m).astype(BF16)
        return acc + jnp.dot(p, v_chunk(ch), preferred_element_type=F32)

    qq = qques[...].reshape(4 * QROWS, 128)
    m = jnp.full((4 * QROWS, 128), FLOOR, F32)
    m = lax.fori_loop(0, 8, lambda ch, mm: scores(qq, ch, 4 * QROWS, mm), m)
    s = nt_dot(qq, kq[...])
    row = lax.broadcasted_iota(jnp.int32, (4 * QROWS, 1), 0)
    row_src = lax.div(row, QROWS)
    row_pos = lax.rem(row_src, 2) * 256 + g * 16 + lax.rem(row, 16)
    col = lax.broadcasted_iota(jnp.int32, (1, 256), 1)
    col_pos = z_lo * 256 + col
    col_mine = lax.div(lax.rem(col, 16), 8) == b1
    col_pos = jnp.where(col_mine, col_pos, 100000)
    s = jnp.where(col_pos <= row_pos, s, FLOOR)
    sq[...] = s
    m = jnp.max(jnp.maximum(m, fold(s)), axis=1, keepdims=True)
    acc = jnp.zeros((4 * QROWS, 256), F32)
    acc = lax.fori_loop(0, 8, lambda ch, a: weigh(ch, 4 * QROWS, m, a), acc)
    p = jnp.exp2(sq[...] - m).astype(BF16)
    acc = acc + jnp.dot(p, vq[...], preferred_element_type=F32)
    total = acc[:, 128:256]
    o = (acc[:, 0:128] / total).astype(BF16)
    lse = m + jnp.log2(total)
    for src in range(4):
        rows = slice(src * QROWS, (src + 1) * QROWS)
        oqsend[src] = o[rows]
        lsend[src, 6:7, :] = to_row(lse[rows], QROWS)
    oqrecv[z4] = oqsend[z4]
    out_copies = []
    for i in range(1, 4):
        src = lax.rem(z4 + i, 4)
        c = rcopy(oqsend.at[src], oqrecv.at[z4], os_.at[i - 1, 1], or_.at[i - 1, 1], z4_dev(i))
        c.start()
        out_copies.append(c)

    def rec_tile(i):
        src = lax.rem(z4 + i, 4)
        c = lax.rem(src, 2)
        n_open = 4 * c + lax.div(g, 4)
        q = qrec[src]
        m = jnp.full((ROWS, 128), FLOOR, F32)
        m = lax.fori_loop(0, n_open, lambda ch, mm: scores(q, ch, ROWS, mm), m)
        pos_col = to_col(qpos[src, 0:1, :], 128)
        seen = (key_off + (n_open * (4 * PT)).astype(F32)) <= pos_col
        k_last = k_chunk(n_open)
        tops = []
        for hh in range(HEADS):
            s = nt_dot(q[hh * 128:(hh + 1) * 128], k_last)
            s = jnp.where(seen, s, FLOOR)
            sbuf[n_open, hh * 128:(hh + 1) * 128, :] = s
            tops.append(fold(s))
        m = jnp.max(jnp.maximum(m, jnp.concatenate(tops, axis=0)), axis=1, keepdims=True)
        acc = jnp.zeros((ROWS, 256), F32)
        acc = lax.fori_loop(0, n_open + 1, lambda ch, a: weigh(ch, ROWS, m, a), acc)
        total = acc[:, 128:256]
        o = (acc[:, 0:128] / total).astype(BF16)
        lse = m + jnp.log2(total)
        for hh in range(HEADS):
            lsend[src, hh:hh + 1, :] = to_row(lse[hh * 128:(hh + 1) * 128], 128)
        return src, o

    for i in range(1, 4):
        src, o = rec_tile(i)
        osend[i - 1] = o
        c = rcopy(osend.at[i - 1], orecv.at[z4], os_.at[i - 1, 0], or_.at[i - 1, 0], z4_dev(i))
        c.start()
        out_copies.append(c)
        c = rcopy(lsend.at[src], lrecv.at[z4], os_.at[i - 1, 2], or_.at[i - 1, 2], z4_dev(i))
        c.start()
        out_copies.append(c)
    src, o = rec_tile(0)
    orecv[z4] = o
    lrecv[z4] = lsend[z4]

    for c in out_copies:
        c.wait_recv()

    def join(parts, lses, n):
        cols_ = [to_col(l, n) for l in lses]
        top_ = functools.reduce(jnp.maximum, cols_)
        ws = [jnp.exp2(c - top_) for c in cols_]
        total = ws[0] + ws[1] + ws[2] + ws[3]
        acc = ws[0] * parts[0].astype(F32)
        for w, part in zip(ws[1:], parts[1:]):
            acc = acc + w * part.astype(F32)
        return acc / total

    used = lax.broadcasted_iota(jnp.int32, (128, 1), 0) < count
    for hh in range(HEADS):
        rows = slice(hh * 128, (hh + 1) * 128)
        o = join([orecv[j, rows, :] for j in range(4)], [lrecv[j, hh:hh + 1, :] for j in range(4)], 128)
        rec_out[:, rows] = jnp.where(used, o, 0.0).astype(BF16)
    o = join([oqrecv[j] for j in range(4)], [lrecv[j, 6:7, :] for j in range(4)], QROWS)
    for hh in range(HEADS):
        ques_out[:, hh * 128:(hh + 1) * 128] = o[hh * 16:(hh + 1) * 16].astype(BF16)

    for c in first_k + second_k + first_v + second_v + z_k + z_v:
        c.wait_send()
    for i, j, c in q_copies:
        c.wait_send()
    for c in sent + out_copies:
        c.wait_send()


def on_device(
    k_store, v_store, pos_offset, owner_map, passage_ids, rec_index, rec_count,
    fresh_q, fresh_k, fresh_v, ques_q, ques_k, ques_v,
):
    vmem = pl.BlockSpec(memory_space=pltpu.VMEM)
    smem = pl.BlockSpec(memory_space=pltpu.SMEM)
    anym = pl.BlockSpec(memory_space=pl.ANY)
    dma = pltpu.SemaphoreType.DMA
    v = pltpu.VMEM
    return pl.pallas_call(
        kernel,
        out_shape=(
            jax.ShapeDtypeStruct((RECP, HEADS * HD), BF16),
            jax.ShapeDtypeStruct((QDEV, HEADS * HD), BF16),
        ),
        in_specs=[smem] * 4 + [vmem] * 8 + [anym] * 2,
        out_specs=(vmem, vmem),
        scratch_shapes=[
            v((3, 2, 256, 256), BF16), v((3, 2, 256, 256), BF16),
            v((2, 256, 256), BF16), v((2, 256, 256), BF16),
            v((2, 256, 256), BF16), v((2, 256, 256), BF16),
            v((2, 2, 256, 256), BF16),
            v((2, 4, 2, 128, 128), BF16),
            v((8, 128, 128), BF16), v((8, 128, 128), BF16),
            v((4, 2, 128, 128), F32),
            v((4, 128, 128), BF16),
            v((2, 2048, 128), BF16),
            v((2, 2048, 256), BF16),
            v((256, 128), BF16),
            v((256, 256), BF16),
            v((4, ROWS, 128), BF16),
            v((4, QROWS, 128), BF16),
            v((4, 8, 128), F32),
            v((8, ROWS, CHUNK), F32),
            v((4 * QROWS, 256), F32),
            v((3, ROWS, 128), BF16),
            v((4, QROWS, 128), BF16),
            v((4, ROWS, 128), BF16),
            v((4, QROWS, 128), BF16),
            v((4, 8, 128), F32),
            v((4, 8, 128), F32),
            dma((2, 4)),
            dma((2, 6)), dma((2, 6)),
            dma((2, 7)), dma((2, 7)),
            dma((3, 3)), dma((3, 3)),
            dma((4, 4)), dma((4, 4)),
            dma((4, 4)), dma((4, 4)),
            dma((4, 8)), dma((4, 8)),
            dma((3, 3)), dma((3, 3)),
        ],
        compiler_params=pltpu.CompilerParams(
            collective_id=0, has_side_effects=True, vmem_limit_bytes=50 * 1024 * 1024
        ),
        cost_estimate=pl.CostEstimate(
            flops=8_000_000_000, bytes_accessed=4_000_000, transcendentals=15_000_000
        ),
        name="blend_attend",
    )(
        pos_offset, owner_map, passage_ids, rec_count, rec_index, fresh_q, fresh_k, fresh_v,
        ques_q, ques_k, ques_v, jnp.asarray(freq_table()), k_store, v_store,
    )


def solution(mesh):
    return jax.shard_map(
        on_device,
        mesh=mesh,
        in_specs=(
            P(("bank", "blk"), None, None),
            P(("bank", "blk"), None, None),
            P(),
            P(),
            P(),
            P("blk", None),
            P("blk"),
            P("blk", "bank"),
            P("blk", None),
            P("blk", None),
            P("blk", "bank"),
            P("blk", None),
            P("blk", None),
        ),
        out_specs=(P("blk", "bank"), P("blk", "bank")),
        check_vma=False,
    )
```

```python
import functools

import jax
import jax.numpy as jnp
import numpy as np
from jax import lax
from jax.experimental import pallas as pl
from jax.experimental.pallas import tpu as pltpu
from jax.sharding import PartitionSpec as P

HD = 128
PT = 512
RECP = 128
QDEV = 16
PASS = 32
HEADS = 6
ROWS = HEADS * RECP
QROWS = HEADS * QDEV
QSTART = PASS * PT
CHUNK = 512
NP = 2
TOK = 64
VMEM_LIMIT = 62 * 1024 * 1024
FLOOR = -1e30
SCALE = float(np.log2(np.e) / np.sqrt(128.0))
MESH = pl.DeviceIdType.MESH
F32 = jnp.float32
BF16 = jnp.bfloat16

INV_2PI = float(1.0 / (2.0 * np.pi))
PI_A = 6.28125
PI_B = 0.0019350051879882812
PI_C = 3.0199159795074593e-07
SIN_C = [float((-1.0) ** k / np.prod(np.arange(1, 2 * k + 2, dtype=np.float64))) for k in range(9)]
COS_C = [float((-1.0) ** k / np.prod(np.arange(1, 2 * k + 1, dtype=np.float64))) for k in range(10)]


def freq_table():
    half = HD // 2
    freqs = 1000000.0 ** (-np.arange(half, dtype=np.float64) * 2.0 / HD)
    return np.concatenate([freqs, freqs])[None, :].astype(np.float32)


def cos_sin(pos, freq):
    angle = pos * freq
    turns = jnp.floor(angle * INV_2PI + 0.5)
    r = ((angle - turns * PI_A) - turns * PI_B) - turns * PI_C
    r2 = r * r
    s = jnp.full_like(r, SIN_C[8])
    for k in range(7, -1, -1):
        s = s * r2 + SIN_C[k]
    s = s * r
    c = jnp.full_like(r, COS_C[9])
    for k in range(8, -1, -1):
        c = c * r2 + COS_C[k]
    lane = lax.broadcasted_iota(jnp.int32, s.shape, 1)
    return c, jnp.where(lane < HD // 2, -s, s)


def turn(x, c, s):
    return x * c + pltpu.roll(x, HD // 2, 1) * s


def eye_mask(n, m):
    row = lax.broadcasted_iota(jnp.int32, (n, m), 0)
    col = lax.broadcasted_iota(jnp.int32, (n, m), 1)
    return row == col


def to_col(row, n):
    full = jnp.broadcast_to(row, (n, 128))
    return jnp.sum(jnp.where(eye_mask(n, 128), full, 0.0), axis=1, keepdims=True)


def to_row(col, n):
    return jnp.sum(jnp.where(eye_mask(n, 128), col, 0.0), axis=0, keepdims=True)


def nt_dot(a, b):
    return lax.dot_general(a, b, (((1,), (1,)), ((), ())), preferred_element_type=F32)


def kernel(
    pos_off_h, owner_map_h, pids_h, rec_count_h, rec_index_h, freq_h, fresh_q_h, fresh_k_h,
    fresh_v_h, ques_q_h, ques_k_h, ques_v_h, k_store, v_store,
    rec_out, ques_out,
    pos_off, owner_map, pids, rec_count, rec_index, freq_ref, fresh_q, fresh_kv, ques_q, ques_kv,
    xfin0, xfin1, mb00, mb01, mb10, mb11, msend, zsend, zin0, zin1, tab, keep, repl, kall, vall, kq, vq,
    qrec, qques, qpos, mcur, mst, ast, mstq, astq,
    osend, oqsend, orecv, oqrecv, lsend, lrecv,
    isem, lsem, xs, xr, zs, zr, qs, qr, ps, pr, ns, nr, cs, cr, os_, or_,
):
    xfin = (xfin0, xfin1)
    mbuf = ((mb00, mb01), (mb10, mb11))
    zin = (zin0, zin1)
    bank = lax.axis_index("bank")
    blk = lax.axis_index("blk")
    x = lax.div(bank, 4)
    z_hi = lax.rem(bank, 4)
    zh = lax.div(z_hi, 2)
    b1 = lax.rem(z_hi, 2)
    z_lo = lax.div(blk, 16)
    g = lax.rem(blk, 16)
    y = lax.div(g, 2)
    core = lax.rem(g, 2)
    zc = 2 * z_hi + z_lo
    z4 = 2 * b1 + z_lo
    head = 2 * x + zh

    def dev(xx, zz, gg):
        return (xx * 4 + lax.div(zz, 2), lax.rem(zz, 2) * 16 + gg)

    x_up = dev(lax.rem(x + 1, 4), zc, g)
    x_dn = dev(lax.rem(x + 3, 4), zc, g)
    y_up = dev(x, zc, lax.rem(y + 1, 8) * 2 + core)
    y_dn = dev(x, zc, lax.rem(y + 7, 8) * 2 + core)
    y_up2 = dev(x, zc, lax.rem(y + 2, 8) * 2 + core)
    y_dn2 = dev(x, zc, lax.rem(y + 6, 8) * 2 + core)
    twin = dev(x, zc, y * 2 + 1 - core)

    def z_dev(i):
        return dev(x, lax.rem(zc + i, 8), g)

    def z4_dev(i):
        return dev(x, 4 * zh + lax.rem(z4 + i, 4), g)

    def rcopy(src, dst, ssem, rsem, where):
        return pltpu.make_async_remote_copy(
            src_ref=src, dst_ref=dst, send_sem=ssem, recv_sem=rsem,
            device_id=where, device_id_type=MESH,
        )

    def cols(xx):
        return pl.ds(pl.multiple_of(lax.rem(xx, 4) * 256, 256), 256)

    hcol = pl.ds(pl.multiple_of(head * 128, 128), 128)

    barrier = pltpu.get_barrier_semaphore()
    peers = [x_up, x_dn, y_up, y_dn, y_up2, y_dn2, twin] + [z_dev(i) for i in range(1, 8)]
    for peer in peers:
        pl.semaphore_signal(barrier, inc=1, device_id=peer, device_id_type=MESH)

    moves = [
        (fresh_q_h, fresh_q), (rec_index_h, rec_index), (freq_h, freq_ref), (ques_q_h, ques_q),
        (ques_k_h.at[:, hcol], ques_kv.at[0]), (ques_v_h.at[:, hcol], ques_kv.at[1]),
        (owner_map_h, owner_map), (pids_h, pids), (pos_off_h, pos_off), (rec_count_h, rec_count),
        (fresh_k_h.at[:, cols(x)], fresh_kv.at[0]), (fresh_v_h.at[:, cols(x)], fresh_kv.at[1]),
    ]
    moves = [pltpu.make_async_copy(a, b, isem.at[i]) for i, (a, b) in enumerate(moves)]
    for c in moves:
        c.start()

    stores = (k_store, v_store)
    top = pl.ds(0, 2)
    low = pl.ds(2, 2)

    def toks(part):
        return pl.ds(part * TOK, TOK)

    def x_local(part):
        copies = []
        for kv in range(2):
            st = stores[kv]
            for j, (src, dst) in enumerate((
                (st.at[top, toks(part), cols(x + 1)], mbuf[part][0].at[0, kv]),
                (st.at[low, toks(part), cols(x + 3)], mbuf[part][1].at[0, kv]),
                (st.at[top, toks(part), cols(x)], xfin[part].at[0, kv, 0]),
                (st.at[low, toks(part), cols(x)], xfin[part].at[0, kv, 1]),
            )):
                c = pltpu.make_async_copy(src, dst, lsem.at[part, kv, j])
                c.start()
                copies.append(c)
        return copies

    loc = [x_local(part) for part in range(NP)]
    pl.semaphore_wait(barrier, len(peers))

    def x_relay(part):
        copies = []
        for kv in range(2):
            st = stores[kv]
            copies += [
                rcopy(st.at[top, toks(part), cols(x + 2)], mbuf[part][0].at[1, kv],
                      xs.at[part, 0, kv], xr.at[part, 0, kv], x_up),
                rcopy(st.at[low, toks(part), cols(x + 2)], mbuf[part][1].at[1, kv],
                      xs.at[part, 1, kv], xr.at[part, 1, kv], x_dn),
            ]
        for c in copies:
            c.start()
        return copies

    def x_plain(part):
        copies = []
        for kv in range(2):
            st = stores[kv]
            copies += [
                rcopy(st.at[low, toks(part), cols(x + 1)], xfin[part].at[1, kv, 1],
                      xs.at[part, 2, kv], xr.at[part, 2, kv], x_up),
                rcopy(st.at[top, toks(part), cols(x + 3)], xfin[part].at[2, kv, 0],
                      xs.at[part, 3, kv], xr.at[part, 3, kv], x_dn),
            ]
        for c in copies:
            c.start()
        return copies

    def x_merge(part, relay, owner_x):
        copies = []
        for d in range(2):
            for kv in range(2):
                loc[part][kv * 4 + d].wait()
                relay[kv * 2 + d].wait_recv()
            near = lax.rem(x + (3 if d == 0 else 1), 4)
            pick = jnp.where(owner_x == near, 1, 0)
            msend[part, d] = mbuf[part][d][pick]
            c = rcopy(msend.at[part, d], xfin[part].at[1 + d, :, d],
                      xs.at[part, 4 + d, 0], xr.at[part, 4 + d, 0], x_up if d == 0 else x_dn)
            c.start()
            copies.append(c)
        return copies

    def x_finish(part, plain, merged, owner_x, between):
        for kv in range(2):
            loc[part][kv * 4 + 2].wait()
            loc[part][kv * 4 + 3].wait()
        for c in plain + merged:
            c.wait_recv()
        is_own = owner_x == x
        idx_a = jnp.where(is_own, 0, jnp.where(owner_x == lax.rem(x + 1, 4), 2, 1))
        idx_b = jnp.where(is_own, 0, jnp.where(owner_x == lax.rem(x + 3, 4), 1, 2))
        for kv in range(2):
            for quarter in range(4):
                half = quarter // 2
                idx = idx_a if half == 0 else idx_b
                data = xfin[part][idx, kv, half, quarter % 2].astype(F32)
                for hh in range(2):
                    lanes = slice(hh * 128, (hh + 1) * 128)
                    piece = data[:, lanes]
                    if kv == 0:
                        piece = turn(piece, tab[part, quarter, 0], tab[part, quarter, 1])
                    else:
                        piece = piece * keep[part, quarter]
                    piece = piece + repl[part, quarter, kv, :, lanes]
                    zsend[part, hh, quarter, kv] = piece.astype(BF16)
            if kv == 0 and between is not None:
                between()
        copies = []
        for i in (1, 7, 2, 6, 3, 5, 4):
            t = lax.rem(zc + i, 8)
            c = rcopy(
                zsend.at[part, lax.div(t, 4), lax.rem(t, 4)], zin[part].at[i],
                zs.at[part, i - 1], zr.at[part, i - 1], z_dev(i),
            )
            c.start()
            copies.append(c)
        zin[part][0] = zsend[part, zh, z4]
        return copies

    def z_finish(part, copies):
        for c in copies:
            c.wait_recv()
        rows = pl.ds(pl.multiple_of(g * TOK, TOK), TOK)
        for c in range(2):
            owner_z = lax.rem(lax.div(owner_map[pids[c * 16 + g]], 32), 4)
            idx = lax.rem(zc + 8 - (2 * owner_z + c), 8)
            kall[part, c, rows, :] = zin[part][idx, 0]
            vall[part, c, rows, 0:128] = zin[part][idx, 1]

    def gather_slices(fam, gg):
        if fam < 4:
            rows = pl.ds(pl.multiple_of(gg * TOK, TOK), TOK)
            if fam % 2 == 0:
                return kall.at[fam // 2, :, rows, :]
            return vall.at[fam // 2, :, rows, pl.ds(0, 128)]
        rows = pl.ds(pl.multiple_of(gg * 16, 16), 16)
        if fam == 4:
            return kq.at[rows, :]
        return vq.at[rows, pl.ds(0, 128)]

    def reach(fam):
        return (4, 3) if fam % 2 == 0 else (3, 4)

    def at_y(dy):
        return lax.rem(y + 8 + dy, 8) * 2 + core

    def g_copy(fam, dy, which, hop):
        piece = gather_slices(fam, at_y(dy))
        if which == "up":
            return rcopy(piece, piece, ps.at[fam, hop], pr.at[fam, hop], y_up2 if hop % 2 else y_up)
        if which == "dn":
            return rcopy(piece, piece, ns.at[fam, hop], nr.at[fam, hop], y_dn2 if hop % 2 else y_dn)
        return rcopy(piece, piece, cs.at[fam, hop], cr.at[fam, hop], twin)

    def g_send(fam, dy, which, hop):
        g_copy(fam, dy, which, hop).start()

    def g_arrived(fam, dy, which, hop):
        g_copy(fam, dy, which, hop).wait_recv()

    def g_start(fam):
        for hop in range(2):
            g_send(fam, 0, "up", hop)
            g_send(fam, 0, "dn", hop)
        g_send(fam, 0, "twin", 0)

    def g_first(fam):
        n_up, n_dn = reach(fam)
        g_arrived(fam, -2, "up", 1)
        for hop in range(2, n_up):
            g_send(fam, -2, "up", hop)
        g_arrived(fam, 2, "dn", 1)
        for hop in range(2, n_dn):
            g_send(fam, 2, "dn", hop)
        g_send(fam, -2, "twin", 2)
        g_send(fam, 2, "twin", 6)
        g_arrived(fam, -1, "up", 0)
        g_send(fam, -1, "twin", 1)
        g_arrived(fam, 1, "dn", 0)
        g_send(fam, 1, "twin", 5)

    def g_second(fam):
        n_up, n_dn = reach(fam)
        for d in range(3, n_up + 1):
            g_arrived(fam, -d, "up", d - 1)
            g_send(fam, -d, "twin", d)
        for d in range(3, n_dn + 1):
            g_arrived(fam, d, "dn", d - 1)
            g_send(fam, d, "twin", d if d == 4 else 4 + d)

    def twin_hops(fam):
        n_up, n_dn = reach(fam)
        return [(0, 0)] + [(-d, d) for d in range(1, n_up + 1)] + [
            (d, d if d == 4 else 4 + d) for d in range(1, n_dn + 1)
        ]

    def g_end(fam):
        for dy, hop in twin_hops(fam):
            piece = gather_slices(fam, lax.rem(y + 8 + dy, 8) * 2 + 1 - core)
            rcopy(piece, piece, cs.at[fam, hop], cr.at[fam, hop], twin).wait_recv()

    def g_sent(fam):
        n_up, n_dn = reach(fam)
        for hop in range(n_up):
            g_copy(fam, 0 if hop < 2 else -2, "up", hop).wait_send()
        for hop in range(n_dn):
            g_copy(fam, 0 if hop < 2 else 2, "dn", hop).wait_send()
        for dy, hop in twin_hops(fam):
            g_copy(fam, dy, "twin", hop).wait_send()

    relay0 = x_relay(0)
    for c in moves:
        c.wait()
    slot = owner_map[pids[blk]]
    owner_x = lax.div(slot, 128)
    off = pos_off[slot]
    count = rec_count[0]

    freq = freq_ref[...]
    rec_row = rec_index[...].astype(F32)
    rec_pos_row = rec_row + (blk * PT).astype(F32)
    rec_pos = to_col(rec_pos_row, 128)
    c_rec, s_rec = cos_sin(rec_pos, freq)

    @pl.loop(0, HEADS)
    def _(hh):
        at = pl.ds(pl.multiple_of(hh * 128, 128), 128)
        q = turn(fresh_q[:, at].astype(F32), c_rec, s_rec) * SCALE
        qrec[z4, at, :] = q.astype(BF16)

    qpos[z4] = jnp.broadcast_to(rec_pos_row, (8, 128))
    for c in relay0:
        c.wait_send()
    plain0 = x_plain(0)
    ques_pos = (
        lax.broadcasted_iota(jnp.int32, (QDEV, 1), 0) + (QSTART + blk * QDEV)
    ).astype(F32)
    c_q, s_q = cos_sin(ques_pos, freq)
    for hh in range(HEADS):
        lanes = slice(hh * 128, (hh + 1) * 128)
        q = turn(ques_q[:, lanes].astype(F32), c_q, s_q) * SCALE
        qques[pl.ds(pl.multiple_of(z4 * QROWS + hh * 16, 16), 16), :] = q.astype(BF16)
    def src_rows(src):
        return pl.ds(pl.multiple_of(src * QROWS, 16), QROWS)

    q_copies = []
    for i in (1, 3, 2):
        for j, ref in enumerate((qrec.at[z4], qques.at[src_rows(z4)], qpos.at[z4])):
            c = rcopy(ref, ref, qs.at[i - 1, j], qr.at[i - 1, j], z4_dev(i))
            c.start()
            q_copies.append(c)

    my_rows = pl.ds(pl.multiple_of(g * 16, 16), 16)
    kq[my_rows, :] = turn(ques_kv[0].astype(F32), c_q, s_q).astype(BF16)
    vq[my_rows, 0:128] = ques_kv[1]
    merged0 = x_merge(0, relay0, owner_x)
    g_start(4)
    g_start(5)

    off_f = off.astype(F32)
    base_f = (blk * PT).astype(F32)
    slot_lane = lax.broadcasted_iota(jnp.int32, (TOK, 128), 1)

    def tables(part):
        @pl.loop(0, 4)
        def _(quarter):
            first = quarter * 128 + part * TOK
            tok = lax.broadcasted_iota(jnp.int32, (TOK, 128), 0) + first
            match = (tok.astype(F32) == jnp.broadcast_to(rec_row, (TOK, 128))) & (slot_lane < count)
            onehot = jnp.where(match, 1.0, 0.0)
            found = jnp.sum(onehot, axis=1, keepdims=True) > 0.5
            onehot = onehot.astype(BF16)
            tpos = (lax.broadcasted_iota(jnp.int32, (TOK, 1), 0) + first).astype(F32) + base_f
            tpos = tpos - jnp.where(found, 0.0, off_f)
            c_t, s_t = cos_sin(tpos, freq)
            rk = jnp.dot(onehot, fresh_kv[0], preferred_element_type=F32)
            for hh in range(2):
                lanes = slice(hh * 128, (hh + 1) * 128)
                repl[part, quarter, 0, :, lanes] = turn(rk[:, lanes], c_t, s_t)
            repl[part, quarter, 1] = jnp.dot(onehot, fresh_kv[1], preferred_element_type=F32)
            stay = jnp.broadcast_to(jnp.where(found, 0.0, 1.0), (TOK, 128))
            keep[part, quarter] = stay
            tab[part, quarter, 0] = c_t * stay
            tab[part, quarter, 1] = s_t * stay

    tables(0)
    vall[:, :, :, 128:256] = jnp.ones((NP, 2, 16 * TOK, 128), BF16)
    vq[:, 128:256] = jnp.ones((256, 128), BF16)
    for c in merged0:
        c.wait_send()
    relay1 = x_relay(1)
    tables(1)
    plain1 = []

    def go_plain1():
        for c in relay1:
            c.wait_send()
        plain1.extend(x_plain(1))

    z0 = x_finish(0, plain0, merged0, owner_x, go_plain1)
    merged1 = x_merge(1, relay1, owner_x)
    for step in (g_first, g_second):
        step(4)
        step(5)
    z_finish(0, z0)
    g_start(0)
    g_start(1)
    z1 = x_finish(1, plain1, merged1, owner_x, None)
    for step in (g_first, g_second):
        step(0)
        step(1)
    z_finish(1, z1)
    g_start(2)
    g_start(3)
    for fam in (4, 5, 0, 1):
        g_end(fam)
    for c in q_copies:
        c.wait_recv()

    key_lane = lax.broadcasted_iota(jnp.int32, (1, CHUNK), 1)
    key_off = lax.div(key_lane, TOK) * PT + lax.rem(key_lane, TOK) + z4 * 128
    key_off = key_off.astype(F32)

    def chunk_rows(ch):
        return pl.ds(pl.multiple_of(lax.rem(ch, 2) * CHUNK, CHUNK), CHUNK)

    def k_chunk(part, ch):
        return kall[part, lax.div(ch, 2), chunk_rows(ch), :]

    def v_chunk(part, ch):
        return vall[part, lax.div(ch, 2), chunk_rows(ch), :]

    def fold(s):
        m = s[:, 0:128]
        for j in range(1, s.shape[1] // 128):
            m = jnp.maximum(m, s[:, j * 128:(j + 1) * 128])
        return m

    def wide(m, n):
        return jnp.concatenate([m] * (n // 128), axis=1)

    def blocks(n):
        return [(b, slice(b * 128, (b + 1) * 128)) for b in range(n)]

    def attend(n, q_of, open_chunks, keys, values, closing, first, m_ref, a_ref):
        for b, rows in blocks(n):
            mcur[rows, :] = jnp.full((128, 128), FLOOR, F32) if first else m_ref[rows, :]

        @pl.loop(0, open_chunks)
        def _(ch):
            k = keys(ch)
            for b, rows in blocks(n):
                mcur[rows, :] = jnp.maximum(mcur[rows, :], fold(nt_dot(q_of(rows), k)))

        if closing is not None:
            k_last, v_last, mask = closing
            for b, rows in blocks(n):
                s = jnp.where(mask(rows), nt_dot(q_of(rows), k_last()), FLOOR)
                mcur[rows, :] = jnp.maximum(mcur[rows, :], fold(s))
        for b, rows in blocks(n):
            m = jnp.broadcast_to(jnp.max(mcur[rows, :], axis=1, keepdims=True), (128, 128))
            if first:
                a_ref[rows, :] = jnp.zeros((128, 256), F32)
            else:
                a_ref[rows, :] = a_ref[rows, :] * wide(jnp.exp2(m_ref[rows, :] - m), 256)
            m_ref[rows, :] = m

        def add(rows, s, v):
            p = jnp.exp2(s - wide(m_ref[rows, :], s.shape[1])).astype(BF16)
            a_ref[rows, :] = a_ref[rows, :] + jnp.dot(p, v, preferred_element_type=F32)

        @pl.loop(0, open_chunks)
        def _(ch):
            k = keys(ch)
            v = values(ch)
            for b, rows in blocks(n):
                add(rows, nt_dot(q_of(rows), k), v)

        if closing is not None:
            for b, rows in blocks(n):
                add(rows, jnp.where(mask(rows), nt_dot(q_of(rows), k_last()), FLOOR), v_last())

    def log_sum(m, total, n):
        return to_row(m, n) + jnp.log2(jnp.maximum(to_row(total, n), 1e-30))

    lsend[...] = jnp.zeros((4, 8, 128), F32)

    def out_copy(i, j):
        src = lax.rem(z4 + i, 4)
        a, b = (
            (osend.at[i], orecv.at[z4]),
            (oqsend.at[src_rows(src)], oqrecv.at[z4]),
            (lsend.at[src], lrecv.at[z4]),
        )[j]
        return rcopy(a, b, os_.at[i, j], or_.at[i, j], z4_dev(i))

    def ques_mask(rows):
        row = lax.broadcasted_iota(jnp.int32, (128, 1), 0) + rows.start
        row_pos = lax.rem(lax.div(row, QROWS), 2) * 256 + g * 16 + lax.rem(row, 16)
        col = lax.broadcasted_iota(jnp.int32, (1, 256), 1)
        col_mine = lax.div(lax.rem(col, 16), 8) == b1
        return jnp.where(col_mine, z_lo * 256 + col, 100000) <= row_pos

    def ques_pass(part):
        closing = (lambda: kq[...], lambda: vq[...], ques_mask) if part == 0 else None
        attend(
            3, lambda rows: qques[rows, :], 4, lambda ch: k_chunk(part, ch),
            lambda ch: v_chunk(part, ch), closing, part == 0, mstq, astq,
        )
        if part < NP - 1:
            return
        for src in range(4):
            rows = slice(src * QROWS, (src + 1) * QROWS)
            total = astq[rows, 128:256]
            oqsend[rows, :] = (astq[rows, 0:128] / total).astype(BF16)
            lsend[src, 6:7, :] = log_sum(mstq[rows, :], total, QROWS)
        oqrecv[z4] = oqsend[src_rows(z4), :]
        for i in range(1, 4):
            out_copy(i, 1).start()

    def rec_pass(part, i):
        src = lax.rem(z4 + i, 4)
        n_open = 2 * lax.rem(src, 2) + lax.div(g, 8)
        pos_col = to_col(qpos[src, 0:1, :], 128)
        key_pos = key_off + (n_open * (8 * PT) + part * TOK).astype(F32)
        closing = (
            lambda: k_chunk(part, n_open), lambda: v_chunk(part, n_open),
            lambda rows: key_pos <= pos_col,
        )
        m_ref, a_ref = mst.at[i], ast.at[i]
        attend(
            HEADS, lambda rows: qrec[src, rows, :], n_open, lambda ch: k_chunk(part, ch),
            lambda ch: v_chunk(part, ch), closing, part == 0, m_ref, a_ref,
        )
        if part < NP - 1:
            return
        for hh in range(HEADS):
            rows = slice(hh * 128, (hh + 1) * 128)
            total = a_ref[rows, 128:256]
            osend[i, rows, :] = (a_ref[rows, 0:128] / total).astype(BF16)
            lsend[src, hh:hh + 1, :] = log_sum(m_ref[rows, :], total, 128)

        @pl.when(i == 0)
        def _():
            orecv[z4] = osend[0]
            lrecv[z4] = lsend[z4]

        @pl.when(i > 0)
        def _():
            out_copy(i, 0).start()
            out_copy(i, 2).start()

    ques_pass(0)

    @pl.loop(0, 4)
    def _(it):
        @pl.when(it == 1)
        def _():
            g_first(2)
            g_first(3)

        @pl.when(it == 3)
        def _():
            g_second(2)
            g_second(3)

        rec_pass(0, lax.rem(it + 1, 4))

    g_end(2)
    g_end(3)
    ques_pass(1)

    @pl.loop(0, 4)
    def _(it):
        rec_pass(1, lax.rem(it + 1, 4))

    out_copies = [out_copy(i, j) for i in range(1, 4) for j in range(3)]
    for c in out_copies:
        c.wait_recv()

    def join(parts, lses, n):
        cols_ = [to_col(l, n) for l in lses]
        top_ = functools.reduce(jnp.maximum, cols_)
        ws = [jnp.exp2(c - top_) for c in cols_]
        total = ws[0] + ws[1] + ws[2] + ws[3]
        acc = ws[0] * parts[0].astype(F32)
        for w, part in zip(ws[1:], parts[1:]):
            acc = acc + w * part.astype(F32)
        return acc / total

    used = lax.broadcasted_iota(jnp.int32, (128, 1), 0) < count

    @pl.loop(0, HEADS)
    def _(hh):
        rows = pl.ds(pl.multiple_of(hh * 128, 128), 128)
        o = join([orecv[j, rows, :] for j in range(4)], [lrecv[j, pl.ds(hh, 1), :] for j in range(4)], 128)
        rec_out[:, rows] = jnp.where(used, o, 0.0).astype(BF16)

    o = join([oqrecv[j] for j in range(4)], [lrecv[j, 6:7, :] for j in range(4)], QROWS)
    for hh in range(HEADS):
        ques_out[:, hh * 128:(hh + 1) * 128] = o[hh * 16:(hh + 1) * 16].astype(BF16)

    for c in plain0 + plain1 + merged1 + z0 + z1 + q_copies + out_copies:
        c.wait_send()
    for fam in range(6):
        g_sent(fam)


def on_device(
    k_store, v_store, pos_offset, owner_map, passage_ids, rec_index, rec_count,
    fresh_q, fresh_k, fresh_v, ques_q, ques_k, ques_v,
):
    vmem = pl.BlockSpec(memory_space=pltpu.VMEM)
    anym = pl.BlockSpec(memory_space=pl.ANY)
    dma = pltpu.SemaphoreType.DMA
    v = pltpu.VMEM
    smem = pltpu.SMEM
    i32 = jnp.int32
    return pl.pallas_call(
        kernel,
        out_shape=(
            jax.ShapeDtypeStruct((RECP, HEADS * HD), BF16),
            jax.ShapeDtypeStruct((QDEV, HEADS * HD), BF16),
        ),
        in_specs=[anym] * 14,
        out_specs=(vmem, vmem),
        scratch_shapes=[
            smem((512,), i32), smem((512,), i32), smem((32,), i32), smem((1,), i32),
            v((1, 128), i32), v((1, 128), F32), v((RECP, HEADS * HD), BF16),
            v((2, RECP, 256), BF16), v((QDEV, HEADS * HD), BF16), v((2, QDEV, 128), BF16),
            v((3, 2, 2, 2, TOK, 256), BF16), v((3, 2, 2, 2, TOK, 256), BF16),
            v((2, 2, 2, TOK, 256), BF16), v((2, 2, 2, TOK, 256), BF16),
            v((2, 2, 2, TOK, 256), BF16), v((2, 2, 2, TOK, 256), BF16),
            v((NP, 2, 2, 2, TOK, 256), BF16),
            v((NP, 2, 4, 2, TOK, 128), BF16),
            v((8, 2, TOK, 128), BF16), v((8, 2, TOK, 128), BF16),
            v((NP, 4, 2, TOK, 128), F32),
            v((NP, 4, TOK, 128), F32),
            v((NP, 4, 2, TOK, 256), F32),
            v((NP, 2, 16 * TOK, 128), BF16),
            v((NP, 2, 16 * TOK, 256), BF16),
            v((256, 128), BF16),
            v((256, 256), BF16),
            v((4, ROWS, 128), BF16),
            v((4 * QROWS, 128), BF16),
            v((4, 8, 128), F32),
            v((ROWS, 128), F32),
            v((4, ROWS, 128), F32), v((4, ROWS, 256), F32),
            v((4 * QROWS, 128), F32), v((4 * QROWS, 256), F32),
            v((4, ROWS, 128), BF16),
            v((4 * QROWS, 128), BF16),
            v((4, ROWS, 128), BF16),
            v((4, QROWS, 128), BF16),
            v((4, 8, 128), F32),
            v((4, 8, 128), F32),
            dma((12,)),
            dma((NP, 2, 4)),
            dma((NP, 6, 2)), dma((NP, 6, 2)),
            dma((NP, 7)), dma((NP, 7)),
            dma((3, 3)), dma((3, 3)),
            dma((6, 4)), dma((6, 4)),
            dma((6, 4)), dma((6, 4)),
            dma((6, 8)), dma((6, 8)),
            dma((4, 3)), dma((4, 3)),
        ],
        compiler_params=pltpu.CompilerParams(
            collective_id=0, has_side_effects=True, vmem_limit_bytes=VMEM_LIMIT
        ),
        cost_estimate=pl.CostEstimate(
            flops=8_000_000_000, bytes_accessed=4_000_000, transcendentals=15_000_000
        ),
        name="blend_attend",
    )(
        pos_offset, owner_map, passage_ids, rec_count, rec_index, jnp.asarray(freq_table()),
        fresh_q, fresh_k, fresh_v, ques_q, ques_k, ques_v,
        k_store.reshape(4, 128, 1024), v_store.reshape(4, 128, 1024),
    )


def solution(mesh):
    return jax.shard_map(
        on_device,
        mesh=mesh,
        in_specs=(
            P(("bank", "blk"), None, None),
            P(("bank", "blk"), None, None),
            P(),
            P(),
            P(),
            P("blk", None),
            P("blk"),
            P("blk", "bank"),
            P("blk", None),
            P("blk", None),
            P("blk", "bank"),
            P("blk", None),
            P("blk", None),
        ),
        out_specs=(P("blk", "bank"), P("blk", "bank")),
        check_vma=False,
    )
```

```python
import functools

import jax
import jax.numpy as jnp
import numpy as np
from jax import lax
from jax.experimental import pallas as pl
from jax.experimental.pallas import tpu as pltpu
from jax.sharding import PartitionSpec as P

HD = 128
PT = 512
RECP = 128
QDEV = 16
PASS = 32
HEADS = 6
ROWS = HEADS * RECP
QROWS = HEADS * QDEV
QSTART = PASS * PT
CHUNK = 512
NP = 2
TOK = 64
VMEM_LIMIT = 62 * 1024 * 1024
FLOOR = -1e30
SCALE = float(1.0 / np.sqrt(128.0))
MESH = pl.DeviceIdType.MESH
F32 = jnp.float32
BF16 = jnp.bfloat16

INV_2PI = float(1.0 / (2.0 * np.pi))
PI_A = 6.28125
PI_B = 0.0019350051879882812
PI_C = 3.0199159795074593e-07
SIN_C = [float((-1.0) ** k / np.prod(np.arange(1, 2 * k + 2, dtype=np.float64))) for k in range(9)]
COS_C = [float((-1.0) ** k / np.prod(np.arange(1, 2 * k + 1, dtype=np.float64))) for k in range(10)]


def freq_table():
    half = HD // 2
    freqs = 1000000.0 ** (-np.arange(half, dtype=np.float64) * 2.0 / HD)
    return np.concatenate([freqs, freqs])[None, :].astype(np.float32)


def cos_sin(pos, freq):
    angle = pos * freq
    turns = jnp.floor(angle * INV_2PI + 0.5)
    r = ((angle - turns * PI_A) - turns * PI_B) - turns * PI_C
    r2 = r * r
    s = jnp.full_like(r, SIN_C[8])
    for k in range(7, -1, -1):
        s = s * r2 + SIN_C[k]
    s = s * r
    c = jnp.full_like(r, COS_C[9])
    for k in range(8, -1, -1):
        c = c * r2 + COS_C[k]
    lane = lax.broadcasted_iota(jnp.int32, s.shape, 1)
    return c, jnp.where(lane < HD // 2, -s, s)


def turn(x, c, s):
    return x * c + pltpu.roll(x, HD // 2, 1) * s


def eye_mask(n, m):
    row = lax.broadcasted_iota(jnp.int32, (n, m), 0)
    col = lax.broadcasted_iota(jnp.int32, (n, m), 1)
    return row == col


def to_col(row, n):
    full = jnp.broadcast_to(row, (n, 128))
    return jnp.sum(jnp.where(eye_mask(n, 128), full, 0.0), axis=1, keepdims=True)


def to_row(col, n):
    return jnp.sum(jnp.where(eye_mask(n, 128), col, 0.0), axis=0, keepdims=True)


def nt_dot(a, b):
    return lax.dot_general(a, b, (((1,), (1,)), ((), ())), preferred_element_type=F32)


def kernel(
    pos_off_h, owner_map_h, pids_h, rec_count_h, rec_index_h, freq_h, fresh_q_h, fresh_k_h,
    fresh_v_h, ques_q_h, ques_k_h, ques_v_h, k_store, v_store,
    rec_out, ques_out,
    pos_off, owner_map, pids, rec_count, rec_index, freq_ref, fresh_q, fresh_kv, ques_q, ques_kv,
    xfin0, xfin1, mb00, mb01, mb10, mb11, msend, zsend, zin0, zin1, tab, keep, repl, kvall, kvq,
    qall, qpos, kt, mst, ast,
    osend, orecv, lsend, lrecv,
    isem, lsem, xs, xr, zs, zr, qs, qr, ps, pr, ns, nr, cs, cr, os_, or_,
):
    xfin = (xfin0, xfin1)
    mbuf = ((mb00, mb01), (mb10, mb11))
    zin = (zin0, zin1)
    bank = lax.axis_index("bank")
    blk = lax.axis_index("blk")
    x = lax.div(bank, 4)
    z_hi = lax.rem(bank, 4)
    zh = lax.div(z_hi, 2)
    b1 = lax.rem(z_hi, 2)
    z_lo = lax.div(blk, 16)
    g = lax.rem(blk, 16)
    y = lax.div(g, 2)
    core = lax.rem(g, 2)
    zc = 2 * z_hi + z_lo
    z4 = 2 * b1 + z_lo
    head = 2 * x + zh
    w = 2 * z_lo + b1

    def dev(xx, zz, gg):
        return (xx * 4 + lax.div(zz, 2), lax.rem(zz, 2) * 16 + gg)

    x_up = dev(lax.rem(x + 1, 4), zc, g)
    x_dn = dev(lax.rem(x + 3, 4), zc, g)
    y_up = dev(x, zc, lax.rem(y + 1, 8) * 2 + core)
    y_dn = dev(x, zc, lax.rem(y + 7, 8) * 2 + core)
    y_up2 = dev(x, zc, lax.rem(y + 2, 8) * 2 + core)
    y_dn2 = dev(x, zc, lax.rem(y + 6, 8) * 2 + core)
    twin = dev(x, zc, y * 2 + 1 - core)

    def z_dev(i):
        return dev(x, lax.rem(zc + i, 8), g)

    def peer_of(j):
        b = b1 if j == 0 else 1 - b1
        lo = z_lo if j == 2 else 1 - z_lo
        return 2 * lo + b, dev(x, 4 * zh + 2 * b + lo, g)

    def rcopy(src, dst, ssem, rsem, where):
        return pltpu.make_async_remote_copy(
            src_ref=src, dst_ref=dst, send_sem=ssem, recv_sem=rsem,
            device_id=where, device_id_type=MESH,
        )

    def cols(xx):
        return pl.ds(pl.multiple_of(lax.rem(xx, 4) * 256, 256), 256)

    hcol = pl.ds(pl.multiple_of(head * 128, 128), 128)

    barrier = pltpu.get_barrier_semaphore()
    peers = [x_up, x_dn, y_up, y_dn, y_up2, y_dn2, twin] + [z_dev(i) for i in range(1, 8)]
    for peer in peers:
        pl.semaphore_signal(barrier, inc=1, device_id=peer, device_id_type=MESH)

    moves = [
        (fresh_q_h, fresh_q), (rec_index_h, rec_index), (freq_h, freq_ref), (ques_q_h, ques_q),
        (ques_k_h.at[:, hcol], ques_kv.at[0]), (ques_v_h.at[:, hcol], ques_kv.at[1]),
        (owner_map_h, owner_map), (pids_h, pids), (pos_off_h, pos_off), (rec_count_h, rec_count),
        (fresh_k_h.at[:, cols(x)], fresh_kv.at[0]), (fresh_v_h.at[:, cols(x)], fresh_kv.at[1]),
    ]
    moves = [pltpu.make_async_copy(a, b, isem.at[i]) for i, (a, b) in enumerate(moves)]
    for c in moves:
        c.start()

    stores = (k_store, v_store)
    top = pl.ds(0, 2)
    low = pl.ds(2, 2)

    def toks(part):
        return pl.ds(part * TOK, TOK)

    def x_local(part):
        copies = []
        for kv in range(2):
            st = stores[kv]
            for j, (src, dst) in enumerate((
                (st.at[top, toks(part), cols(x + 1)], mbuf[part][0].at[0, kv]),
                (st.at[low, toks(part), cols(x + 3)], mbuf[part][1].at[0, kv]),
                (st.at[top, toks(part), cols(x)], xfin[part].at[0, kv, 0]),
                (st.at[low, toks(part), cols(x)], xfin[part].at[0, kv, 1]),
            )):
                c = pltpu.make_async_copy(src, dst, lsem.at[part, kv, j])
                c.start()
                copies.append(c)
        return copies

    loc = [x_local(part) for part in range(NP)]
    pl.semaphore_wait(barrier, len(peers))

    def x_relay(part):
        copies = []
        for kv in range(2):
            st = stores[kv]
            copies += [
                rcopy(st.at[top, toks(part), cols(x + 2)], mbuf[part][0].at[1, kv],
                      xs.at[part, 0, kv], xr.at[part, 0, kv], x_up),
                rcopy(st.at[low, toks(part), cols(x + 2)], mbuf[part][1].at[1, kv],
                      xs.at[part, 1, kv], xr.at[part, 1, kv], x_dn),
            ]
        for c in copies:
            c.start()
        return copies

    def x_plain(part):
        copies = []
        for kv in range(2):
            st = stores[kv]
            copies += [
                rcopy(st.at[low, toks(part), cols(x + 1)], xfin[part].at[1, kv, 1],
                      xs.at[part, 2, kv], xr.at[part, 2, kv], x_up),
                rcopy(st.at[top, toks(part), cols(x + 3)], xfin[part].at[2, kv, 0],
                      xs.at[part, 3, kv], xr.at[part, 3, kv], x_dn),
            ]
        for c in copies:
            c.start()
        return copies

    def x_merge(part, relay, owner_x):
        copies = []
        for d in range(2):
            for kv in range(2):
                loc[part][kv * 4 + d].wait()
                relay[kv * 2 + d].wait_recv()
            near = lax.rem(x + (3 if d == 0 else 1), 4)
            pick = jnp.where(owner_x == near, 1, 0)
            msend[part, d] = mbuf[part][d][pick]
            c = rcopy(msend.at[part, d], xfin[part].at[1 + d, :, d],
                      xs.at[part, 4 + d, 0], xr.at[part, 4 + d, 0], x_up if d == 0 else x_dn)
            c.start()
            copies.append(c)
        return copies

    def x_finish(part, plain, merged, owner_x, between):
        for kv in range(2):
            loc[part][kv * 4 + 2].wait()
            loc[part][kv * 4 + 3].wait()
        for c in plain + merged:
            c.wait_recv()
        is_own = owner_x == x
        idx_a = jnp.where(is_own, 0, jnp.where(owner_x == lax.rem(x + 1, 4), 2, 1))
        idx_b = jnp.where(is_own, 0, jnp.where(owner_x == lax.rem(x + 3, 4), 1, 2))
        for kv in range(2):
            for quarter in range(4):
                half = quarter // 2
                idx = idx_a if half == 0 else idx_b
                data = xfin[part][idx, kv, half, quarter % 2].astype(F32)
                for hh in range(2):
                    lanes = slice(hh * 128, (hh + 1) * 128)
                    piece = data[:, lanes]
                    if kv == 0:
                        piece = turn(piece, tab[part, quarter, 0], tab[part, quarter, 1])
                    else:
                        piece = piece * keep[part, quarter]
                    piece = piece + repl[part, quarter, kv, :, lanes]
                    zsend[part, hh, quarter, kv] = piece.astype(BF16)
            if kv == 0 and between is not None:
                between()
        copies = []
        for i in (1, 7, 2, 6, 3, 5, 4):
            t = lax.rem(zc + i, 8)
            c = rcopy(
                zsend.at[part, lax.div(t, 4), lax.rem(t, 4)], zin[part].at[i],
                zs.at[part, i - 1], zr.at[part, i - 1], z_dev(i),
            )
            c.start()
            copies.append(c)
        zin[part][0] = zsend[part, zh, z4]
        return copies

    def z_finish(part, copies):
        for c in copies:
            c.wait_recv()
        rows = pl.ds(pl.multiple_of(g * TOK, TOK), TOK)
        for c in range(2):
            owner_z = lax.rem(lax.div(owner_map[pids[c * 16 + g]], 32), 4)
            idx = lax.rem(zc + 8 - (2 * owner_z + c), 8)
            kvall[part, 0, c, rows, :] = zin[part][idx, 0]
            kvall[part, 1, c, rows, :] = zin[part][idx, 1]

    def gather_slices(fam, gg):
        if fam < 2:
            return kvall.at[fam, :, :, pl.ds(pl.multiple_of(gg * TOK, TOK), TOK), :]
        return kvq.at[:, pl.ds(pl.multiple_of(gg * 16, 16), 16), :]

    def reach(fam):
        return (4, 3) if fam % 2 == 0 else (3, 4)

    def at_y(dy):
        return lax.rem(y + 8 + dy, 8) * 2 + core

    def g_copy(fam, dy, which, hop):
        piece = gather_slices(fam, at_y(dy))
        if which == "up":
            return rcopy(piece, piece, ps.at[fam, hop], pr.at[fam, hop], y_up2 if hop % 2 else y_up)
        if which == "dn":
            return rcopy(piece, piece, ns.at[fam, hop], nr.at[fam, hop], y_dn2 if hop % 2 else y_dn)
        return rcopy(piece, piece, cs.at[fam, hop], cr.at[fam, hop], twin)

    def g_send(fam, dy, which, hop):
        g_copy(fam, dy, which, hop).start()

    def g_arrived(fam, dy, which, hop):
        g_copy(fam, dy, which, hop).wait_recv()

    def g_start(fam):
        for hop in range(2):
            g_send(fam, 0, "up", hop)
            g_send(fam, 0, "dn", hop)
        g_send(fam, 0, "twin", 0)

    def g_first(fam):
        n_up, n_dn = reach(fam)
        g_arrived(fam, -2, "up", 1)
        for hop in range(2, n_up):
            g_send(fam, -2, "up", hop)
        g_arrived(fam, 2, "dn", 1)
        for hop in range(2, n_dn):
            g_send(fam, 2, "dn", hop)
        g_send(fam, -2, "twin", 2)
        g_send(fam, 2, "twin", 6)
        g_arrived(fam, -1, "up", 0)
        g_send(fam, -1, "twin", 1)
        g_arrived(fam, 1, "dn", 0)
        g_send(fam, 1, "twin", 5)

    def g_second(fam):
        n_up, n_dn = reach(fam)
        for d in range(3, n_up + 1):
            g_arrived(fam, -d, "up", d - 1)
            g_send(fam, -d, "twin", d)
        for d in range(3, n_dn + 1):
            g_arrived(fam, d, "dn", d - 1)
            g_send(fam, d, "twin", d if d == 4 else 4 + d)

    def twin_hops(fam):
        n_up, n_dn = reach(fam)
        return [(0, 0)] + [(-d, d) for d in range(1, n_up + 1)] + [
            (d, d if d == 4 else 4 + d) for d in range(1, n_dn + 1)
        ]

    def g_end(fam):
        for dy, hop in twin_hops(fam):
            piece = gather_slices(fam, lax.rem(y + 8 + dy, 8) * 2 + 1 - core)
            rcopy(piece, piece, cs.at[fam, hop], cr.at[fam, hop], twin).wait_recv()

    def g_sent(fam):
        n_up, n_dn = reach(fam)
        for hop in range(n_up):
            g_copy(fam, 0 if hop < 2 else -2, "up", hop).wait_send()
        for hop in range(n_dn):
            g_copy(fam, 0 if hop < 2 else 2, "dn", hop).wait_send()
        for dy, hop in twin_hops(fam):
            g_copy(fam, dy, "twin", hop).wait_send()

    relay0 = x_relay(0)
    for c in moves:
        c.wait()
    slot = owner_map[pids[blk]]
    owner_x = lax.div(slot, 128)
    off = pos_off[slot]
    count = rec_count[0]

    freq = freq_ref[...]
    rec_row = rec_index[...].astype(F32)
    rec_pos_row = rec_row + (blk * PT).astype(F32)
    rec_pos = to_col(rec_pos_row, 128)
    c_rec, s_rec = cos_sin(rec_pos, freq)

    @pl.loop(0, HEADS)
    def _(hh):
        at = pl.ds(pl.multiple_of(hh * 128, 128), 128)
        q = turn(fresh_q[:, at].astype(F32), c_rec, s_rec) * SCALE
        qall[w, at, :] = q.astype(BF16)

    qpos[w] = jnp.broadcast_to(rec_pos_row, (8, 128))
    for c in relay0:
        c.wait_send()
    plain0 = x_plain(0)
    ques_pos = (
        lax.broadcasted_iota(jnp.int32, (QDEV, 1), 0) + (QSTART + blk * QDEV)
    ).astype(F32)
    c_q, s_q = cos_sin(ques_pos, freq)
    for hh in range(HEADS):
        lanes = slice(hh * 128, (hh + 1) * 128)
        q = turn(ques_q[:, lanes].astype(F32), c_q, s_q) * SCALE
        qall[w, ROWS + hh * 16:ROWS + (hh + 1) * 16, :] = q.astype(BF16)
    q_copies = []
    for j in range(3):
        for n, ref in enumerate((qall, qpos)):
            c = rcopy(ref.at[w], ref.at[w], qs.at[j, n], qr.at[j, n], peer_of(j)[1])
            c.start()
            q_copies.append(c)

    my_rows = pl.ds(pl.multiple_of(g * 16, 16), 16)
    kvq[0, my_rows, :] = turn(ques_kv[0].astype(F32), c_q, s_q).astype(BF16)
    kvq[1, my_rows, :] = ques_kv[1]
    merged0 = x_merge(0, relay0, owner_x)
    g_start(2)

    off_f = off.astype(F32)
    base_f = (blk * PT).astype(F32)
    slot_lane = lax.broadcasted_iota(jnp.int32, (TOK, 128), 1)

    def tables(part):
        @pl.loop(0, 4)
        def _(quarter):
            first = quarter * 128 + part * TOK
            tok = lax.broadcasted_iota(jnp.int32, (TOK, 128), 0) + first
            match = (tok.astype(F32) == jnp.broadcast_to(rec_row, (TOK, 128))) & (slot_lane < count)
            onehot = jnp.where(match, 1.0, 0.0)
            found = jnp.sum(onehot, axis=1, keepdims=True) > 0.5
            onehot = onehot.astype(BF16)
            tpos = (lax.broadcasted_iota(jnp.int32, (TOK, 1), 0) + first).astype(F32) + base_f
            tpos = tpos - jnp.where(found, 0.0, off_f)
            c_t, s_t = cos_sin(tpos, freq)
            rk = jnp.dot(onehot, fresh_kv[0], preferred_element_type=F32)
            for hh in range(2):
                lanes = slice(hh * 128, (hh + 1) * 128)
                repl[part, quarter, 0, :, lanes] = turn(rk[:, lanes], c_t, s_t)
            repl[part, quarter, 1] = jnp.dot(onehot, fresh_kv[1], preferred_element_type=F32)
            stay = jnp.broadcast_to(jnp.where(found, 0.0, 1.0), (TOK, 128))
            keep[part, quarter] = stay
            tab[part, quarter, 0] = c_t * stay
            tab[part, quarter, 1] = s_t * stay

    tables(0)
    for c in merged0:
        c.wait_send()
    relay1 = x_relay(1)
    tables(1)
    plain1 = []

    def go_plain1():
        for c in relay1:
            c.wait_send()
        plain1.extend(x_plain(1))

    z0 = x_finish(0, plain0, merged0, owner_x, go_plain1)
    merged1 = x_merge(1, relay1, owner_x)
    g_first(2)
    g_second(2)
    z_finish(0, z0)
    g_start(0)
    z1 = x_finish(1, plain1, merged1, owner_x, None)
    g_first(0)
    g_second(0)
    z_finish(1, z1)
    g_start(1)
    g_end(2)
    g_end(0)
    for c in q_copies:
        c.wait_recv()

    key_lane = lax.broadcasted_iota(jnp.int32, (1, CHUNK), 1)
    key_off = lax.div(key_lane, TOK) * PT + lax.rem(key_lane, TOK) + z4 * 128
    key_off = key_off.astype(F32)

    def chunk_rows(ch):
        return pl.ds(pl.multiple_of(lax.rem(ch, 2) * CHUNK, CHUNK), CHUNK)

    ones = jnp.ones((CHUNK, 128), BF16)

    def transpose_keys(part):
        @pl.loop(0, 4)
        def _(ch):
            kt[ch] = jnp.transpose(kvall[part, 0, lax.div(ch, 2), chunk_rows(ch), :])

    def v_chunk(part, ch):
        return jnp.concatenate([kvall[part, 1, lax.div(ch, 2), chunk_rows(ch), :], ones], axis=1)

    def fold(s):
        m = s[:, 0:128]
        for j in range(1, s.shape[1] // 128):
            m = jnp.maximum(m, s[:, j * 128:(j + 1) * 128])
        return m

    def wide(m, n):
        return jnp.concatenate([m] * (n // 128), axis=1)

    def attend(n, rows_each, q_of, part, open_chunks, closing, m_ref, a_ref):
        blocks = [(b, slice(b * rows_each, (b + 1) * rows_each)) for b in range(n)]
        when, last_keys, last_values, mask = closing

        def step(b, rows, k, v, seen):
            s = jnp.dot(q_of(b), k, preferred_element_type=F32)
            if seen is not None:
                s = jnp.where(seen, s, FLOOR)
            old = m_ref[rows, :]
            new = jnp.maximum(old, jnp.max(fold(s), axis=1, keepdims=True))
            m_ref[rows, :] = new
            p = jnp.exp(s - wide(new, s.shape[1])).astype(BF16)
            scale = wide(jnp.exp(old - new), 256)
            a_ref[rows, :] = a_ref[rows, :] * scale + jnp.dot(p, v, preferred_element_type=F32)

        @pl.loop(0, open_chunks)
        def _(ch):
            k = kt[ch]
            v = v_chunk(part, ch)
            for b, rows in blocks:
                step(b, rows, k, v, None)

        def close():
            k = last_keys()
            v = last_values()
            seen = mask()
            for b, rows in blocks:
                step(b, rows, k, v, seen)

        if when is None:
            close()
        else:
            pl.when(when)(close)

    def log_sum(m, total, n):
        return to_row(m, n) + jnp.log(jnp.maximum(to_row(total, n), 1e-30))

    lsend[...] = jnp.zeros((4, 8, 128), F32)
    mst[...] = jnp.full((3, 2 * ROWS, 128), FLOOR, F32)
    ast[...] = jnp.zeros((3, 2 * ROWS, 256), F32)

    def out_copy(j, n):
        to, where = peer_of(j)
        a, b = ((osend, orecv), (lsend, lrecv))[n]
        return rcopy(a.at[to], b.at[w], os_.at[j, n], or_.at[j, n], where)

    def ques_mask():
        row = lax.broadcasted_iota(jnp.int32, (4 * QROWS, 1), 0)
        row_pos = lax.div(row, 2 * QROWS) * 256 + g * 16 + lax.rem(row, 16)
        col = lax.broadcasted_iota(jnp.int32, (1, 256), 1)
        col_mine = lax.div(lax.rem(col, 16), 8) == b1
        return jnp.where(col_mine, z_lo * 256 + col, 100000) <= row_pos

    def ques_pass(part):
        closing = (
            part == 0, lambda: jnp.transpose(kvq[0]),
            lambda: jnp.concatenate([kvq[1], ones[0:256]], axis=1), ques_mask,
        )
        attend(
            1, 4 * QROWS, lambda b: jnp.concatenate([qall[j, ROWS:, :] for j in range(4)], axis=0),
            part, 4, closing, mst.at[2], ast.at[2],
        )

        @pl.when(part == NP - 1)
        def _():
            for src in range(4):
                rows = slice(src * QROWS, (src + 1) * QROWS)
                total = ast[2, rows, 128:256]
                osend[src, ROWS:, :] = (ast[2, rows, 0:128] / total).astype(BF16)
                lsend[src, 6:7, :] = log_sum(mst[2, rows, :], total, QROWS)

    def rec_pass(part, c):
        n_open = 2 * c + lax.div(g, 8)
        pos_col = to_col(qpos[2 * c, 0:1, :], 128)
        pos_col = jnp.concatenate([pos_col] * HEADS, axis=0)
        key_pos = key_off + (n_open * (8 * PT) + part * TOK).astype(F32)
        closing = (
            None, lambda: kt[n_open], lambda: v_chunk(part, n_open),
            lambda: key_pos <= pos_col,
        )
        attend(
            2, ROWS, lambda b: qall[2 * c + b, 0:ROWS, :],
            part, n_open, closing, mst.at[c], ast.at[c],
        )

    def rec_end(c):
        for b in range(2):
            src = 2 * c + b
            for hh in range(HEADS):
                rows = slice(b * ROWS + hh * 128, b * ROWS + (hh + 1) * 128)
                total = ast[c, rows, 128:256]
                osend[src, hh * 128:(hh + 1) * 128, :] = (ast[c, rows, 0:128] / total).astype(BF16)
                lsend[src, hh:hh + 1, :] = log_sum(mst[c, rows, :], total, 128)

    @pl.loop(0, NP)
    def _(part):
        transpose_keys(part)
        ques_pass(part)

        @pl.loop(0, 2)
        def _(t):
            @pl.when((part == 0) & (t == 0))
            def _():
                g_first(1)

            @pl.when((part == 0) & (t == 1))
            def _():
                g_second(1)

            c = lax.rem(z_lo + 1 + t, 2)
            rec_pass(part, c)

            @pl.when(part == NP - 1)
            def _():
                rec_end(c)

            @pl.when((part == NP - 1) & (t == 0))
            def _():
                for j in range(2):
                    for n in range(2):
                        out_copy(j, n).start()

            @pl.when((part == NP - 1) & (t == 1))
            def _():
                for n in range(2):
                    out_copy(2, n).start()

        @pl.when(part == 0)
        def _():
            g_end(1)

    orecv[w] = osend[w]
    lrecv[w] = lsend[w]
    out_copies = [out_copy(j, n) for j in range(3) for n in range(2)]
    for c in out_copies:
        c.wait_recv()

    def join(parts, lses, n):
        cols_ = [to_col(l, n) for l in lses]
        top_ = functools.reduce(jnp.maximum, cols_)
        ws = [jnp.exp(c - top_) for c in cols_]
        total = ws[0] + ws[1] + ws[2] + ws[3]
        acc = ws[0] * parts[0].astype(F32)
        for w, part in zip(ws[1:], parts[1:]):
            acc = acc + w * part.astype(F32)
        return acc / total

    used = lax.broadcasted_iota(jnp.int32, (128, 1), 0) < count

    @pl.loop(0, HEADS)
    def _(hh):
        rows = pl.ds(pl.multiple_of(hh * 128, 128), 128)
        o = join([orecv[j, rows, :] for j in range(4)], [lrecv[j, pl.ds(hh, 1), :] for j in range(4)], 128)
        rec_out[:, rows] = jnp.where(used, o, 0.0).astype(BF16)

    o = join([orecv[j, ROWS:, :] for j in range(4)], [lrecv[j, 6:7, :] for j in range(4)], QROWS)
    for hh in range(HEADS):
        ques_out[:, hh * 128:(hh + 1) * 128] = o[hh * 16:(hh + 1) * 16].astype(BF16)

    for c in plain0 + plain1 + merged1 + z0 + z1 + q_copies + out_copies:
        c.wait_send()
    for fam in range(3):
        g_sent(fam)


def on_device(
    k_store, v_store, pos_offset, owner_map, passage_ids, rec_index, rec_count,
    fresh_q, fresh_k, fresh_v, ques_q, ques_k, ques_v,
):
    vmem = pl.BlockSpec(memory_space=pltpu.VMEM)
    anym = pl.BlockSpec(memory_space=pl.ANY)
    dma = pltpu.SemaphoreType.DMA
    v = pltpu.VMEM
    smem = pltpu.SMEM
    i32 = jnp.int32
    return pl.pallas_call(
        kernel,
        out_shape=(
            jax.ShapeDtypeStruct((RECP, HEADS * HD), BF16),
            jax.ShapeDtypeStruct((QDEV, HEADS * HD), BF16),
        ),
        in_specs=[anym] * 14,
        out_specs=(vmem, vmem),
        scratch_shapes=[
            smem((512,), i32), smem((512,), i32), smem((32,), i32), smem((1,), i32),
            v((1, 128), i32), v((1, 128), F32), v((RECP, HEADS * HD), BF16),
            v((2, RECP, 256), BF16), v((QDEV, HEADS * HD), BF16), v((2, QDEV, 128), BF16),
            v((3, 2, 2, 2, TOK, 256), BF16), v((3, 2, 2, 2, TOK, 256), BF16),
            v((2, 2, 2, TOK, 256), BF16), v((2, 2, 2, TOK, 256), BF16),
            v((2, 2, 2, TOK, 256), BF16), v((2, 2, 2, TOK, 256), BF16),
            v((NP, 2, 2, 2, TOK, 256), BF16),
            v((NP, 2, 4, 2, TOK, 128), BF16),
            v((8, 2, TOK, 128), BF16), v((8, 2, TOK, 128), BF16),
            v((NP, 4, 2, TOK, 128), F32),
            v((NP, 4, TOK, 128), F32),
            v((NP, 4, 2, TOK, 256), F32),
            v((NP, 2, 2, 16 * TOK, 128), BF16),
            v((2, 256, 128), BF16),
            v((4, ROWS + QROWS, 128), BF16),
            v((4, 8, 128), F32),
            v((4, 128, CHUNK), BF16),
            v((3, 2 * ROWS, 128), F32), v((3, 2 * ROWS, 256), F32),
            v((4, ROWS + QROWS, 128), BF16),
            v((4, ROWS + QROWS, 128), BF16),
            v((4, 8, 128), F32),
            v((4, 8, 128), F32),
            dma((12,)),
            dma((NP, 2, 4)),
            dma((NP, 6, 2)), dma((NP, 6, 2)),
            dma((NP, 7)), dma((NP, 7)),
            dma((3, 2)), dma((3, 2)),
            dma((3, 4)), dma((3, 4)),
            dma((3, 4)), dma((3, 4)),
            dma((3, 8)), dma((3, 8)),
            dma((3, 2)), dma((3, 2)),
        ],
        compiler_params=pltpu.CompilerParams(
            collective_id=0, has_side_effects=True, vmem_limit_bytes=VMEM_LIMIT
        ),
        cost_estimate=pl.CostEstimate(
            flops=8_000_000_000, bytes_accessed=4_000_000, transcendentals=15_000_000
        ),
        name="blend_attend",
    )(
        pos_offset, owner_map, passage_ids, rec_count, rec_index, jnp.asarray(freq_table()),
        fresh_q, fresh_k, fresh_v, ques_q, ques_k, ques_v,
        k_store.reshape(4, 128, 1024), v_store.reshape(4, 128, 1024),
    )


def solution(mesh):
    return jax.shard_map(
        on_device,
        mesh=mesh,
        in_specs=(
            P(("bank", "blk"), None, None),
            P(("bank", "blk"), None, None),
            P(),
            P(),
            P(),
            P("blk", None),
            P("blk"),
            P("blk", "bank"),
            P("blk", None),
            P("blk", None),
            P("blk", "bank"),
            P("blk", None),
            P("blk", None),
        ),
        out_specs=(P("blk", "bank"), P("blk", "bank")),
        check_vma=False,
    )
```

```python
import functools

import jax
import jax.numpy as jnp
import numpy as np
from jax import lax
from jax.experimental import pallas as pl
from jax.experimental.pallas import tpu as pltpu
from jax.sharding import PartitionSpec as P

HD = 128
PT = 512
RECP = 128
QDEV = 16
PASS = 32
HEADS = 6
ROWS = HEADS * RECP
QROWS = HEADS * QDEV
QSTART = PASS * PT
CHUNK = 512
NP = 2
TOK = 64
VMEM_LIMIT = 62 * 1024 * 1024
FLOOR = -1e30
SCALE = float(1.0 / np.sqrt(128.0))
MESH = pl.DeviceIdType.MESH
F32 = jnp.float32
BF16 = jnp.bfloat16

INV_2PI = float(1.0 / (2.0 * np.pi))
PI_A = 6.28125
PI_B = 0.0019350051879882812
PI_C = 3.0199159795074593e-07
SIN_C = [float((-1.0) ** k / np.prod(np.arange(1, 2 * k + 2, dtype=np.float64))) for k in range(9)]
COS_C = [float((-1.0) ** k / np.prod(np.arange(1, 2 * k + 1, dtype=np.float64))) for k in range(10)]


def freq_table():
    half = HD // 2
    freqs = 1000000.0 ** (-np.arange(half, dtype=np.float64) * 2.0 / HD)
    return np.concatenate([freqs, freqs])[None, :].astype(np.float32)


def cos_sin(pos, freq):
    angle = pos * freq
    turns = jnp.floor(angle * INV_2PI + 0.5)
    r = ((angle - turns * PI_A) - turns * PI_B) - turns * PI_C
    r2 = r * r
    s = jnp.full_like(r, SIN_C[8])
    for k in range(7, -1, -1):
        s = s * r2 + SIN_C[k]
    s = s * r
    c = jnp.full_like(r, COS_C[9])
    for k in range(8, -1, -1):
        c = c * r2 + COS_C[k]
    lane = lax.broadcasted_iota(jnp.int32, s.shape, 1)
    return c, jnp.where(lane < HD // 2, -s, s)


def turn(x, c, s):
    return x * c + pltpu.roll(x, HD // 2, 1) * s


def eye_mask(n, m):
    row = lax.broadcasted_iota(jnp.int32, (n, m), 0)
    col = lax.broadcasted_iota(jnp.int32, (n, m), 1)
    return row == col


def to_col(row, n):
    full = jnp.broadcast_to(row, (n, 128))
    return jnp.sum(jnp.where(eye_mask(n, 128), full, 0.0), axis=1, keepdims=True)


def to_row(col, n):
    return jnp.sum(jnp.where(eye_mask(n, 128), col, 0.0), axis=0, keepdims=True)


def nt_dot(a, b):
    return lax.dot_general(a, b, (((1,), (1,)), ((), ())), preferred_element_type=F32)


def kernel(
    pos_off_h, owner_map_h, pids_h, rec_count_h, rec_index_h, freq_h, fresh_q_h, fresh_k_h,
    fresh_v_h, ques_q_h, ques_k_h, ques_v_h, k_store, v_store,
    rec_out, ques_out,
    pos_off, owner_map, pids, rec_count, rec_index, freq_ref, fresh_q, fresh_kv, ques_q, ques_kv,
    xfin0, xfin1, mb00, mb01, mb10, mb11, msend, zsend, zin0, zin1, tab, keep, repl, kvall, kvq,
    qall, qpos, kt, mst, ast,
    osend, orecv, lsend, lrecv,
    isem, lsem, xs, xr, zs, zr, bs, br, qs, qr, ps, pr, ns, nr, cs, cr, os_, or_,
):
    xfin = (xfin0, xfin1)
    mbuf = ((mb00, mb01), (mb10, mb11))
    zin = (zin0, zin1)
    bank = lax.axis_index("bank")
    blk = lax.axis_index("blk")
    x = lax.div(bank, 4)
    z_hi = lax.rem(bank, 4)
    zh = lax.div(z_hi, 2)
    b1 = lax.rem(z_hi, 2)
    z_lo = lax.div(blk, 16)
    g = lax.rem(blk, 16)
    y = lax.div(g, 2)
    core = lax.rem(g, 2)
    zc = 2 * z_hi + z_lo
    z4 = 2 * b1 + z_lo
    head = 2 * x + zh

    def dev(xx, zz, gg):
        return (xx * 4 + lax.div(zz, 2), lax.rem(zz, 2) * 16 + gg)

    x_up = dev(lax.rem(x + 1, 4), zc, g)
    x_dn = dev(lax.rem(x + 3, 4), zc, g)
    y_up = dev(x, zc, lax.rem(y + 1, 8) * 2 + core)
    y_dn = dev(x, zc, lax.rem(y + 7, 8) * 2 + core)
    y_up2 = dev(x, zc, lax.rem(y + 2, 8) * 2 + core)
    y_dn2 = dev(x, zc, lax.rem(y + 6, 8) * 2 + core)
    twin = dev(x, zc, y * 2 + 1 - core)

    def z_dev(i):
        return dev(x, lax.rem(zc + i, 8), g)

    partner = dev(x, 4 * zh + 2 * b1 + 1 - z_lo, g)
    other_b = dev(x, 4 * zh + 2 * (1 - b1) + z_lo, g)

    def rcopy(src, dst, ssem, rsem, where):
        return pltpu.make_async_remote_copy(
            src_ref=src, dst_ref=dst, send_sem=ssem, recv_sem=rsem,
            device_id=where, device_id_type=MESH,
        )

    def cols(xx):
        return pl.ds(pl.multiple_of(lax.rem(xx, 4) * 256, 256), 256)

    hcol = pl.ds(pl.multiple_of(head * 128, 128), 128)

    barrier = pltpu.get_barrier_semaphore()
    peers = [x_up, x_dn, y_up, y_dn, y_up2, y_dn2, twin] + [z_dev(i) for i in range(1, 8)]
    for peer in peers:
        pl.semaphore_signal(barrier, inc=1, device_id=peer, device_id_type=MESH)

    moves = [
        (fresh_q_h, fresh_q), (rec_index_h, rec_index), (freq_h, freq_ref), (ques_q_h, ques_q),
        (ques_k_h.at[:, hcol], ques_kv.at[0]), (ques_v_h.at[:, hcol], ques_kv.at[1]),
        (owner_map_h, owner_map), (pids_h, pids), (pos_off_h, pos_off), (rec_count_h, rec_count),
        (fresh_k_h.at[:, cols(x)], fresh_kv.at[0]), (fresh_v_h.at[:, cols(x)], fresh_kv.at[1]),
    ]
    moves = [pltpu.make_async_copy(a, b, isem.at[i]) for i, (a, b) in enumerate(moves)]
    for c in moves:
        c.start()

    stores = (k_store, v_store)
    top = pl.ds(0, 2)
    low = pl.ds(2, 2)

    def toks(part):
        return pl.ds(part * TOK, TOK)

    def x_local(part):
        copies = []
        for kv in range(2):
            st = stores[kv]
            for j, (src, dst) in enumerate((
                (st.at[top, toks(part), cols(x + 1)], mbuf[part][0].at[0, kv]),
                (st.at[low, toks(part), cols(x + 3)], mbuf[part][1].at[0, kv]),
                (st.at[top, toks(part), cols(x)], xfin[part].at[0, kv, 0]),
                (st.at[low, toks(part), cols(x)], xfin[part].at[0, kv, 1]),
            )):
                c = pltpu.make_async_copy(src, dst, lsem.at[part, kv, j])
                c.start()
                copies.append(c)
        return copies

    loc = [x_local(part) for part in range(NP)]
    pl.semaphore_wait(barrier, len(peers))

    def x_relay(part):
        copies = []
        for kv in range(2):
            st = stores[kv]
            copies += [
                rcopy(st.at[top, toks(part), cols(x + 2)], mbuf[part][0].at[1, kv],
                      xs.at[part, 0, kv], xr.at[part, 0, kv], x_up),
                rcopy(st.at[low, toks(part), cols(x + 2)], mbuf[part][1].at[1, kv],
                      xs.at[part, 1, kv], xr.at[part, 1, kv], x_dn),
            ]
        for c in copies:
            c.start()
        return copies

    def x_plain(part):
        copies = []
        for kv in range(2):
            st = stores[kv]
            copies += [
                rcopy(st.at[low, toks(part), cols(x + 1)], xfin[part].at[1, kv, 1],
                      xs.at[part, 2, kv], xr.at[part, 2, kv], x_up),
                rcopy(st.at[top, toks(part), cols(x + 3)], xfin[part].at[2, kv, 0],
                      xs.at[part, 3, kv], xr.at[part, 3, kv], x_dn),
            ]
        for c in copies:
            c.start()
        return copies

    def x_merge(part, relay, owner_x):
        copies = []
        for d in range(2):
            for kv in range(2):
                loc[part][kv * 4 + d].wait()
                relay[kv * 2 + d].wait_recv()
            near = lax.rem(x + (3 if d == 0 else 1), 4)
            pick = jnp.where(owner_x == near, 1, 0)
            msend[part, d] = mbuf[part][d][pick]
            c = rcopy(msend.at[part, d], xfin[part].at[1 + d, :, d],
                      xs.at[part, 4 + d, 0], xr.at[part, 4 + d, 0], x_up if d == 0 else x_dn)
            c.start()
            copies.append(c)
        return copies

    def x_finish(part, plain, merged, owner_x, between):
        for kv in range(2):
            loc[part][kv * 4 + 2].wait()
            loc[part][kv * 4 + 3].wait()
        for c in plain + merged:
            c.wait_recv()
        is_own = owner_x == x
        idx_a = jnp.where(is_own, 0, jnp.where(owner_x == lax.rem(x + 1, 4), 2, 1))
        idx_b = jnp.where(is_own, 0, jnp.where(owner_x == lax.rem(x + 3, 4), 1, 2))
        for kv in range(2):
            for quarter in range(4):
                half = quarter // 2
                idx = idx_a if half == 0 else idx_b
                data = xfin[part][idx, kv, half, quarter % 2].astype(F32)
                for hh in range(2):
                    lanes = slice(hh * 128, (hh + 1) * 128)
                    piece = data[:, lanes]
                    if kv == 0:
                        piece = turn(piece, tab[part, quarter, 0], tab[part, quarter, 1])
                    else:
                        piece = piece * keep[part, quarter]
                    piece = piece + repl[part, quarter, kv, :, lanes]
                    zsend[part, hh, quarter, kv] = piece.astype(BF16)
            if kv == 0 and between is not None:
                between()
        copies = []
        for i in (1, 7, 2, 6, 3, 5, 4):
            t = lax.rem(zc + i, 8)
            c = rcopy(
                zsend.at[part, lax.div(t, 4), lax.rem(t, 4)], zin[part].at[i],
                zs.at[part, i - 1], zr.at[part, i - 1], z_dev(i),
            )
            c.start()
            copies.append(c)
        zin[part][0] = zsend[part, zh, z4]
        return copies

    def g_rows(gg):
        return pl.ds(pl.multiple_of(gg * TOK, TOK), TOK)

    def swap_copy(part):
        piece = kvall.at[part, b1, :, :, g_rows(g), :]
        return rcopy(piece, piece, bs.at[part], br.at[part], other_b)

    def z_finish(part, copies):
        for c in copies:
            c.wait_recv()
        for c in range(2):
            owner_z = lax.rem(lax.div(owner_map[pids[c * 16 + g]], 32), 4)
            idx = lax.rem(zc + 8 - (2 * owner_z + c), 8)
            kvall[part, b1, 0, c, g_rows(g), :] = zin[part][idx, 0]
            kvall[part, b1, 1, c, g_rows(g), :] = zin[part][idx, 1]
        swap_copy(part).start()
        g_start(2 * part)

    def swap_finish(part):
        piece = kvall.at[part, 1 - b1, :, :, g_rows(g), :]
        rcopy(piece, piece, bs.at[part], br.at[part], other_b).wait_recv()
        g_start(2 * part + 1)

    def gather_slices(fam, gg):
        if fam < 4:
            return kvall.at[fam // 2, b1 if fam % 2 == 0 else 1 - b1, :, :, g_rows(gg), :]
        return kvq.at[:, pl.ds(pl.multiple_of(gg * 16, 16), 16), :]

    def reach(fam):
        return (4, 3) if fam % 2 == 0 else (3, 4)

    def at_y(dy):
        return lax.rem(y + 8 + dy, 8) * 2 + core

    def g_copy(fam, dy, which, hop):
        piece = gather_slices(fam, at_y(dy))
        if which == "up":
            return rcopy(piece, piece, ps.at[fam, hop], pr.at[fam, hop], y_up2 if hop % 2 else y_up)
        if which == "dn":
            return rcopy(piece, piece, ns.at[fam, hop], nr.at[fam, hop], y_dn2 if hop % 2 else y_dn)
        return rcopy(piece, piece, cs.at[fam, hop], cr.at[fam, hop], twin)

    def g_send(fam, dy, which, hop):
        g_copy(fam, dy, which, hop).start()

    def g_arrived(fam, dy, which, hop):
        g_copy(fam, dy, which, hop).wait_recv()

    def g_start(fam):
        for hop in range(2):
            g_send(fam, 0, "up", hop)
            g_send(fam, 0, "dn", hop)
        g_send(fam, 0, "twin", 0)

    def g_first(fam):
        n_up, n_dn = reach(fam)
        g_arrived(fam, -2, "up", 1)
        for hop in range(2, n_up):
            g_send(fam, -2, "up", hop)
        g_arrived(fam, 2, "dn", 1)
        for hop in range(2, n_dn):
            g_send(fam, 2, "dn", hop)
        g_send(fam, -2, "twin", 2)
        g_send(fam, 2, "twin", 6)
        g_arrived(fam, -1, "up", 0)
        g_send(fam, -1, "twin", 1)
        g_arrived(fam, 1, "dn", 0)
        g_send(fam, 1, "twin", 5)

    def g_second(fam):
        n_up, n_dn = reach(fam)
        for d in range(3, n_up + 1):
            g_arrived(fam, -d, "up", d - 1)
            g_send(fam, -d, "twin", d)
        for d in range(3, n_dn + 1):
            g_arrived(fam, d, "dn", d - 1)
            g_send(fam, d, "twin", d if d == 4 else 4 + d)

    def twin_hops(fam):
        n_up, n_dn = reach(fam)
        return [(0, 0)] + [(-d, d) for d in range(1, n_up + 1)] + [
            (d, d if d == 4 else 4 + d) for d in range(1, n_dn + 1)
        ]

    def g_end(fam):
        for dy, hop in twin_hops(fam):
            piece = gather_slices(fam, lax.rem(y + 8 + dy, 8) * 2 + 1 - core)
            rcopy(piece, piece, cs.at[fam, hop], cr.at[fam, hop], twin).wait_recv()

    def g_sent(fam):
        n_up, n_dn = reach(fam)
        for hop in range(n_up):
            g_copy(fam, 0 if hop < 2 else -2, "up", hop).wait_send()
        for hop in range(n_dn):
            g_copy(fam, 0 if hop < 2 else 2, "dn", hop).wait_send()
        for dy, hop in twin_hops(fam):
            g_copy(fam, dy, "twin", hop).wait_send()

    relay0 = x_relay(0)
    for c in moves:
        c.wait()
    slot = owner_map[pids[blk]]
    owner_x = lax.div(slot, 128)
    off = pos_off[slot]
    count = rec_count[0]

    freq = freq_ref[...]
    rec_row = rec_index[...].astype(F32)
    rec_pos_row = rec_row + (blk * PT).astype(F32)
    rec_pos = to_col(rec_pos_row, 128)
    c_rec, s_rec = cos_sin(rec_pos, freq)

    @pl.loop(0, HEADS)
    def _(hh):
        at = pl.ds(pl.multiple_of(hh * 128, 128), 128)
        q = turn(fresh_q[:, at].astype(F32), c_rec, s_rec) * SCALE
        qall[z_lo, at, :] = q.astype(BF16)

    qpos[z_lo] = jnp.broadcast_to(rec_pos_row, (8, 128))
    for c in relay0:
        c.wait_send()
    plain0 = x_plain(0)
    ques_pos = (
        lax.broadcasted_iota(jnp.int32, (QDEV, 1), 0) + (QSTART + blk * QDEV)
    ).astype(F32)
    c_q, s_q = cos_sin(ques_pos, freq)
    for hh in range(HEADS):
        lanes = slice(hh * 128, (hh + 1) * 128)
        q = turn(ques_q[:, lanes].astype(F32), c_q, s_q) * SCALE
        qall[z_lo, ROWS + hh * 16:ROWS + (hh + 1) * 16, :] = q.astype(BF16)
    q_copies = []
    for n, ref in enumerate((qall, qpos)):
        c = rcopy(ref.at[z_lo], ref.at[z_lo], qs.at[n], qr.at[n], partner)
        c.start()
        q_copies.append(c)

    my_rows = pl.ds(pl.multiple_of(g * 16, 16), 16)
    kvq[0, my_rows, :] = turn(ques_kv[0].astype(F32), c_q, s_q).astype(BF16)
    kvq[1, my_rows, :] = ques_kv[1]
    merged0 = x_merge(0, relay0, owner_x)
    g_start(4)

    off_f = off.astype(F32)
    base_f = (blk * PT).astype(F32)
    slot_lane = lax.broadcasted_iota(jnp.int32, (TOK, 128), 1)

    def tables(part):
        @pl.loop(0, 4)
        def _(quarter):
            first = quarter * 128 + part * TOK
            tok = lax.broadcasted_iota(jnp.int32, (TOK, 128), 0) + first
            match = (tok.astype(F32) == jnp.broadcast_to(rec_row, (TOK, 128))) & (slot_lane < count)
            onehot = jnp.where(match, 1.0, 0.0)
            found = jnp.sum(onehot, axis=1, keepdims=True) > 0.5
            onehot = onehot.astype(BF16)
            tpos = (lax.broadcasted_iota(jnp.int32, (TOK, 1), 0) + first).astype(F32) + base_f
            tpos = tpos - jnp.where(found, 0.0, off_f)
            c_t, s_t = cos_sin(tpos, freq)
            rk = jnp.dot(onehot, fresh_kv[0], preferred_element_type=F32)
            for hh in range(2):
                lanes = slice(hh * 128, (hh + 1) * 128)
                repl[part, quarter, 0, :, lanes] = turn(rk[:, lanes], c_t, s_t)
            repl[part, quarter, 1] = jnp.dot(onehot, fresh_kv[1], preferred_element_type=F32)
            stay = jnp.broadcast_to(jnp.where(found, 0.0, 1.0), (TOK, 128))
            keep[part, quarter] = stay
            tab[part, quarter, 0] = c_t * stay
            tab[part, quarter, 1] = s_t * stay

    tables(0)
    for c in merged0:
        c.wait_send()
    relay1 = x_relay(1)
    tables(1)
    plain1 = []

    def go_plain1():
        for c in relay1:
            c.wait_send()
        plain1.extend(x_plain(1))

    z0 = x_finish(0, plain0, merged0, owner_x, go_plain1)
    merged1 = x_merge(1, relay1, owner_x)
    g_first(4)
    g_second(4)
    z_finish(0, z0)
    swap_finish(0)
    z1 = x_finish(1, plain1, merged1, owner_x, None)
    for step in (g_first, g_second):
        step(0)
        step(1)
    z_finish(1, z1)
    g_end(4)
    g_end(0)
    g_end(1)
    for c in q_copies:
        c.wait_recv()
    swap_finish(1)

    key_lane = lax.broadcasted_iota(jnp.int32, (1, 2 * CHUNK), 1)
    key_in = lax.rem(key_lane, CHUNK)
    key_off = lax.div(key_in, TOK) * PT + lax.rem(key_in, TOK)
    key_off = (key_off + (2 * lax.div(key_lane, CHUNK) + z_lo) * 128).astype(F32)
    ones = jnp.ones((2 * CHUNK, 128), BF16)

    def chunk_of(part, b, kv, ch):
        rows = pl.ds(pl.multiple_of(lax.rem(ch, 2) * CHUNK, CHUNK), CHUNK)
        return kvall[part, b, kv, lax.div(ch, 2), rows, :]

    def transpose_keys(part):
        @pl.loop(0, 4)
        def _(ch):
            for b in range(2):
                kt[ch, :, b * CHUNK:(b + 1) * CHUNK] = jnp.transpose(chunk_of(part, b, 0, ch))

    def v_chunk(part, ch):
        v = jnp.concatenate([chunk_of(part, b, 1, ch) for b in range(2)], axis=0)
        return jnp.concatenate([v, ones], axis=1)

    def fold(s):
        m = s[:, 0:128]
        for j in range(1, s.shape[1] // 128):
            m = jnp.maximum(m, s[:, j * 128:(j + 1) * 128])
        return m

    def wide(m, n):
        return jnp.concatenate([m] * (n // 128), axis=1)

    def attend(n, rows_each, q_of, part, open_chunks, closing, m_ref, a_ref):
        blocks = [(b, slice(b * rows_each, (b + 1) * rows_each)) for b in range(n)]
        when, last_keys, last_values, mask = closing

        def step(b, rows, k, v, seen):
            s = jnp.dot(q_of(b), k, preferred_element_type=F32)
            if seen is not None:
                s = jnp.where(seen, s, FLOOR)
            old = m_ref[rows, :]
            new = jnp.maximum(old, jnp.max(fold(s), axis=1, keepdims=True))
            m_ref[rows, :] = new
            p = jnp.exp(s - wide(new, s.shape[1])).astype(BF16)
            scale = wide(jnp.exp(old - new), 256)
            a_ref[rows, :] = a_ref[rows, :] * scale + jnp.dot(p, v, preferred_element_type=F32)

        @pl.loop(0, open_chunks)
        def _(ch):
            k = kt[ch]
            v = v_chunk(part, ch)
            for b, rows in blocks:
                step(b, rows, k, v, None)

        def close():
            k = last_keys()
            v = last_values()
            seen = mask()
            for b, rows in blocks:
                step(b, rows, k, v, seen)

        if when is None:
            close()
        else:
            pl.when(when)(close)

    def log_sum(m, total, n):
        return to_row(m, n) + jnp.log(jnp.maximum(to_row(total, n), 1e-30))

    lsend[...] = jnp.zeros((2, 8, 128), F32)
    mst[...] = jnp.full((3, ROWS, 128), FLOOR, F32)
    ast[...] = jnp.zeros((3, ROWS, 256), F32)

    def out_copy(n):
        a, b = ((osend, orecv), (lsend, lrecv))[n]
        return rcopy(a.at[1 - z_lo], b.at[z_lo], os_.at[n], or_.at[n], partner)

    def ques_mask():
        row = lax.broadcasted_iota(jnp.int32, (2 * QROWS, 1), 0)
        row_pos = lax.div(row, QROWS) * 256 + g * 16 + lax.rem(row, 16)
        col = lax.broadcasted_iota(jnp.int32, (1, 256), 1)
        return z_lo * 256 + col <= row_pos

    def ques_pass(part):
        closing = (
            part == 0, lambda: jnp.transpose(kvq[0]),
            lambda: jnp.concatenate([kvq[1], ones[0:256]], axis=1), ques_mask,
        )
        attend(
            1, 2 * QROWS, lambda b: jnp.concatenate([qall[j, ROWS:, :] for j in range(2)], axis=0),
            part, 4, closing, mst.at[2], ast.at[2],
        )

        @pl.when(part == NP - 1)
        def _():
            for src in range(2):
                rows = slice(src * QROWS, (src + 1) * QROWS)
                total = ast[2, rows, 128:256]
                osend[src, ROWS:, :] = (ast[2, rows, 0:128] / total).astype(BF16)
                lsend[src, 6:7, :] = log_sum(mst[2, rows, :], total, QROWS)

    def rec_pass(part, c):
        n_open = 2 * c + lax.div(g, 8)
        pos_col = to_col(qpos[c, 0:1, :], 128)
        pos_col = jnp.concatenate([pos_col] * 3, axis=0)
        key_pos = key_off + (n_open * (8 * PT) + part * TOK).astype(F32)
        closing = (
            None, lambda: kt[n_open], lambda: v_chunk(part, n_open),
            lambda: key_pos <= pos_col,
        )
        attend(
            2, 384, lambda b: qall[c, b * 384:(b + 1) * 384, :],
            part, n_open, closing, mst.at[c], ast.at[c],
        )

    def rec_end(c):
        for hh in range(HEADS):
            rows = slice(hh * 128, (hh + 1) * 128)
            total = ast[c, rows, 128:256]
            osend[c, rows, :] = (ast[c, rows, 0:128] / total).astype(BF16)
            lsend[c, hh:hh + 1, :] = log_sum(mst[c, rows, :], total, 128)

    @pl.loop(0, NP)
    def _(part):
        transpose_keys(part)
        ques_pass(part)

        @pl.loop(0, 2)
        def _(t):
            @pl.when((part == 0) & (t == 0))
            def _():
                g_first(2)
                g_first(3)

            @pl.when((part == 0) & (t == 1))
            def _():
                g_second(2)
                g_second(3)

            c = lax.rem(z_lo + 1 + t, 2)
            rec_pass(part, c)

            @pl.when(part == NP - 1)
            def _():
                rec_end(c)

            @pl.when((part == NP - 1) & (t == 0))
            def _():
                for n in range(2):
                    out_copy(n).start()

        @pl.when(part == 0)
        def _():
            g_end(2)
            g_end(3)

    orecv[z_lo] = osend[z_lo]
    lrecv[z_lo] = lsend[z_lo]
    out_copies = [out_copy(n) for n in range(2)]
    for c in out_copies:
        c.wait_recv()

    def join(parts, lses, n):
        cols_ = [to_col(l, n) for l in lses]
        top_ = functools.reduce(jnp.maximum, cols_)
        ws = [jnp.exp(c - top_) for c in cols_]
        total = ws[0] + ws[1]
        acc = ws[0] * parts[0].astype(F32)
        for w, part in zip(ws[1:], parts[1:]):
            acc = acc + w * part.astype(F32)
        return acc / total

    used = lax.broadcasted_iota(jnp.int32, (128, 1), 0) < count

    @pl.loop(0, HEADS)
    def _(hh):
        rows = pl.ds(pl.multiple_of(hh * 128, 128), 128)
        o = join([orecv[j, rows, :] for j in range(2)], [lrecv[j, pl.ds(hh, 1), :] for j in range(2)], 128)
        rec_out[:, rows] = jnp.where(used, o, 0.0).astype(BF16)

    o = join([orecv[j, ROWS:, :] for j in range(2)], [lrecv[j, 6:7, :] for j in range(2)], QROWS)
    for hh in range(HEADS):
        ques_out[:, hh * 128:(hh + 1) * 128] = o[hh * 16:(hh + 1) * 16].astype(BF16)

    for c in plain0 + plain1 + merged1 + z0 + z1 + q_copies + out_copies:
        c.wait_send()
    for fam in range(5):
        g_sent(fam)
    for part in range(NP):
        swap_copy(part).wait_send()


def on_device(
    k_store, v_store, pos_offset, owner_map, passage_ids, rec_index, rec_count,
    fresh_q, fresh_k, fresh_v, ques_q, ques_k, ques_v,
):
    vmem = pl.BlockSpec(memory_space=pltpu.VMEM)
    anym = pl.BlockSpec(memory_space=pl.ANY)
    dma = pltpu.SemaphoreType.DMA
    v = pltpu.VMEM
    smem = pltpu.SMEM
    i32 = jnp.int32
    return pl.pallas_call(
        kernel,
        out_shape=(
            jax.ShapeDtypeStruct((RECP, HEADS * HD), BF16),
            jax.ShapeDtypeStruct((QDEV, HEADS * HD), BF16),
        ),
        in_specs=[anym] * 14,
        out_specs=(vmem, vmem),
        scratch_shapes=[
            smem((512,), i32), smem((512,), i32), smem((32,), i32), smem((1,), i32),
            v((1, 128), i32), v((1, 128), F32), v((RECP, HEADS * HD), BF16),
            v((2, RECP, 256), BF16), v((QDEV, HEADS * HD), BF16), v((2, QDEV, 128), BF16),
            v((3, 2, 2, 2, TOK, 256), BF16), v((3, 2, 2, 2, TOK, 256), BF16),
            v((2, 2, 2, TOK, 256), BF16), v((2, 2, 2, TOK, 256), BF16),
            v((2, 2, 2, TOK, 256), BF16), v((2, 2, 2, TOK, 256), BF16),
            v((NP, 2, 2, 2, TOK, 256), BF16),
            v((NP, 2, 4, 2, TOK, 128), BF16),
            v((8, 2, TOK, 128), BF16), v((8, 2, TOK, 128), BF16),
            v((NP, 4, 2, TOK, 128), F32),
            v((NP, 4, TOK, 128), F32),
            v((NP, 4, 2, TOK, 256), F32),
            v((NP, 2, 2, 2, 16 * TOK, 128), BF16),
            v((2, 256, 128), BF16),
            v((2, ROWS + QROWS, 128), BF16),
            v((2, 8, 128), F32),
            v((4, 128, 2 * CHUNK), BF16),
            v((3, ROWS, 128), F32), v((3, ROWS, 256), F32),
            v((2, ROWS + QROWS, 128), BF16),
            v((2, ROWS + QROWS, 128), BF16),
            v((2, 8, 128), F32),
            v((2, 8, 128), F32),
            dma((12,)),
            dma((NP, 2, 4)),
            dma((NP, 6, 2)), dma((NP, 6, 2)),
            dma((NP, 7)), dma((NP, 7)),
            dma((NP,)), dma((NP,)),
            dma((2,)), dma((2,)),
            dma((5, 4)), dma((5, 4)),
            dma((5, 4)), dma((5, 4)),
            dma((5, 8)), dma((5, 8)),
            dma((2,)), dma((2,)),
        ],
        compiler_params=pltpu.CompilerParams(
            collective_id=0, has_side_effects=True, vmem_limit_bytes=VMEM_LIMIT
        ),
        cost_estimate=pl.CostEstimate(
            flops=8_000_000_000, bytes_accessed=4_000_000, transcendentals=15_000_000
        ),
        name="blend_attend",
    )(
        pos_offset, owner_map, passage_ids, rec_count, rec_index, jnp.asarray(freq_table()),
        fresh_q, fresh_k, fresh_v, ques_q, ques_k, ques_v,
        k_store.reshape(4, 128, 1024), v_store.reshape(4, 128, 1024),
    )


def solution(mesh):
    return jax.shard_map(
        on_device,
        mesh=mesh,
        in_specs=(
            P(("bank", "blk"), None, None),
            P(("bank", "blk"), None, None),
            P(),
            P(),
            P(),
            P("blk", None),
            P("blk"),
            P("blk", "bank"),
            P("blk", None),
            P("blk", None),
            P("blk", "bank"),
            P("blk", None),
            P("blk", None),
        ),
        out_specs=(P("blk", "bank"), P("blk", "bank")),
        check_vma=False,
    )
```

```python
import functools

import jax
import jax.numpy as jnp
import numpy as np
from jax import lax
from jax.experimental import pallas as pl
from jax.experimental.pallas import tpu as pltpu
from jax.sharding import PartitionSpec as P

HD = 128
PT = 512
RECP = 128
QDEV = 16
PASS = 32
HEADS = 6
ROWS = HEADS * RECP
QROWS = HEADS * QDEV
QSTART = PASS * PT
CHUNK = 512
NP = 4
TOK = 32
VMEM_LIMIT = 62 * 1024 * 1024
FLOOR = -1e30
SCALE = float(1.0 / np.sqrt(128.0))
MESH = pl.DeviceIdType.MESH
F32 = jnp.float32
BF16 = jnp.bfloat16

INV_2PI = float(1.0 / (2.0 * np.pi))
PI_A = 6.28125
PI_B = 0.0019350051879882812
PI_C = 3.0199159795074593e-07
SIN_C = [float((-1.0) ** k / np.prod(np.arange(1, 2 * k + 2, dtype=np.float64))) for k in range(9)]
COS_C = [float((-1.0) ** k / np.prod(np.arange(1, 2 * k + 1, dtype=np.float64))) for k in range(10)]


def freq_table():
    half = HD // 2
    freqs = 1000000.0 ** (-np.arange(half, dtype=np.float64) * 2.0 / HD)
    return np.concatenate([freqs, freqs])[None, :].astype(np.float32)


def cos_sin(pos, freq):
    angle = pos * freq
    turns = jnp.floor(angle * INV_2PI + 0.5)
    r = ((angle - turns * PI_A) - turns * PI_B) - turns * PI_C
    r2 = r * r
    s = jnp.full_like(r, SIN_C[8])
    for k in range(7, -1, -1):
        s = s * r2 + SIN_C[k]
    s = s * r
    c = jnp.full_like(r, COS_C[9])
    for k in range(8, -1, -1):
        c = c * r2 + COS_C[k]
    lane = lax.broadcasted_iota(jnp.int32, s.shape, 1)
    return c, jnp.where(lane < HD // 2, -s, s)


def turn(x, c, s):
    return x * c + pltpu.roll(x, HD // 2, 1) * s


def eye_mask(n, m):
    row = lax.broadcasted_iota(jnp.int32, (n, m), 0)
    col = lax.broadcasted_iota(jnp.int32, (n, m), 1)
    return row == col


def to_col(row, n):
    full = jnp.broadcast_to(row, (n, 128))
    return jnp.sum(jnp.where(eye_mask(n, 128), full, 0.0), axis=1, keepdims=True)


def to_row(col, n):
    return jnp.sum(jnp.where(eye_mask(n, 128), col, 0.0), axis=0, keepdims=True)


def nt_dot(a, b):
    return lax.dot_general(a, b, (((1,), (1,)), ((), ())), preferred_element_type=F32)


def kernel(
    pos_off_h, owner_map_h, pids_h, rec_count_h, rec_index_h, freq_h, fresh_q_h, fresh_k_h,
    fresh_v_h, ques_q_h, ques_k_h, ques_v_h, k_store, v_store,
    rec_out, ques_out,
    pos_off, owner_map, pids, rec_count, rec_index, freq_ref, fresh_q, fresh_kv, ques_q, ques_kv,
    xfin, mbuf, msend, zsend, zin, tab, keep, repl, kvall, kvq,
    qall, qpos, kt, mst, ast,
    osend, orecv, lsend, lrecv,
    isem, lsem, xs, xr, zs, zr, bs, br, qs, qr, ps, pr, ns, nr, cs, cr, os_, or_,
):
    bank = lax.axis_index("bank")
    blk = lax.axis_index("blk")
    x = lax.div(bank, 4)
    z_hi = lax.rem(bank, 4)
    zh = lax.div(z_hi, 2)
    b1 = lax.rem(z_hi, 2)
    z_lo = lax.div(blk, 16)
    g = lax.rem(blk, 16)
    y = lax.div(g, 2)
    core = lax.rem(g, 2)
    zc = 2 * z_hi + z_lo
    z4 = 2 * b1 + z_lo
    head = 2 * x + zh

    def dev(xx, zz, gg):
        return (xx * 4 + lax.div(zz, 2), lax.rem(zz, 2) * 16 + gg)

    x_up = dev(lax.rem(x + 1, 4), zc, g)
    x_dn = dev(lax.rem(x + 3, 4), zc, g)
    y_up = dev(x, zc, lax.rem(y + 1, 8) * 2 + core)
    y_dn = dev(x, zc, lax.rem(y + 7, 8) * 2 + core)
    y_up2 = dev(x, zc, lax.rem(y + 2, 8) * 2 + core)
    y_dn2 = dev(x, zc, lax.rem(y + 6, 8) * 2 + core)
    twin = dev(x, zc, y * 2 + 1 - core)

    def z_dev(i):
        return dev(x, lax.rem(zc + i, 8), g)

    partner = dev(x, 4 * zh + 2 * b1 + 1 - z_lo, g)
    other_b = dev(x, 4 * zh + 2 * (1 - b1) + z_lo, g)

    def rcopy(src, dst, ssem, rsem, where):
        return pltpu.make_async_remote_copy(
            src_ref=src, dst_ref=dst, send_sem=ssem, recv_sem=rsem,
            device_id=where, device_id_type=MESH,
        )

    def cols(xx):
        return pl.ds(pl.multiple_of(lax.rem(xx, 4) * 256, 256), 256)

    hcol = pl.ds(pl.multiple_of(head * 128, 128), 128)

    barrier = pltpu.get_barrier_semaphore()
    peers = [x_up, x_dn, y_up, y_dn, y_up2, y_dn2, twin] + [z_dev(i) for i in range(1, 8)]
    for peer in peers:
        pl.semaphore_signal(barrier, inc=1, device_id=peer, device_id_type=MESH)

    moves = [
        (fresh_q_h, fresh_q), (rec_index_h, rec_index), (freq_h, freq_ref), (ques_q_h, ques_q),
        (ques_k_h.at[:, hcol], ques_kv.at[0]), (ques_v_h.at[:, hcol], ques_kv.at[1]),
        (owner_map_h, owner_map), (pids_h, pids), (pos_off_h, pos_off), (rec_count_h, rec_count),
        (fresh_k_h.at[:, cols(x)], fresh_kv.at[0]), (fresh_v_h.at[:, cols(x)], fresh_kv.at[1]),
    ]
    moves = [pltpu.make_async_copy(a, b, isem.at[i]) for i, (a, b) in enumerate(moves)]
    for c in moves:
        c.start()

    stores = (k_store, v_store)
    top = pl.ds(0, 2)
    low = pl.ds(2, 2)

    def toks(part):
        return pl.ds(part * TOK, TOK)

    def x_local(part):
        copies = []
        for kv in range(2):
            st = stores[kv]
            for j, (src, dst) in enumerate((
                (st.at[top, toks(part), cols(x + 1)], mbuf[part][0].at[0, kv]),
                (st.at[low, toks(part), cols(x + 3)], mbuf[part][1].at[0, kv]),
                (st.at[top, toks(part), cols(x)], xfin[part].at[0, kv, 0]),
                (st.at[low, toks(part), cols(x)], xfin[part].at[0, kv, 1]),
            )):
                c = pltpu.make_async_copy(src, dst, lsem.at[part, kv, j])
                c.start()
                copies.append(c)
        return copies

    loc = [x_local(part) for part in range(NP)]
    pl.semaphore_wait(barrier, len(peers))

    def x_relay(part):
        copies = []
        for kv in range(2):
            st = stores[kv]
            copies += [
                rcopy(st.at[top, toks(part), cols(x + 2)], mbuf[part][0].at[1, kv],
                      xs.at[part, 0, kv], xr.at[part, 0, kv], x_up),
                rcopy(st.at[low, toks(part), cols(x + 2)], mbuf[part][1].at[1, kv],
                      xs.at[part, 1, kv], xr.at[part, 1, kv], x_dn),
            ]
        for c in copies:
            c.start()
        return copies

    def x_plain(part):
        copies = []
        for kv in range(2):
            st = stores[kv]
            copies += [
                rcopy(st.at[low, toks(part), cols(x + 1)], xfin[part].at[1, kv, 1],
                      xs.at[part, 2, kv], xr.at[part, 2, kv], x_up),
                rcopy(st.at[top, toks(part), cols(x + 3)], xfin[part].at[2, kv, 0],
                      xs.at[part, 3, kv], xr.at[part, 3, kv], x_dn),
            ]
        for c in copies:
            c.start()
        return copies

    def x_merge(part, relay, owner_x):
        copies = []
        for d in range(2):
            for kv in range(2):
                loc[part][kv * 4 + d].wait()
                relay[kv * 2 + d].wait_recv()
            near = lax.rem(x + (3 if d == 0 else 1), 4)
            pick = jnp.where(owner_x == near, 1, 0)
            msend[part, d] = mbuf[part][d][pick]
            c = rcopy(msend.at[part, d], xfin[part].at[1 + d, :, d],
                      xs.at[part, 4 + d, 0], xr.at[part, 4 + d, 0], x_up if d == 0 else x_dn)
            c.start()
            copies.append(c)
        return copies

    def x_finish(part, plain, merged, owner_x):
        at_tok = slice(part * TOK, (part + 1) * TOK)
        for kv in range(2):
            loc[part][kv * 4 + 2].wait()
            loc[part][kv * 4 + 3].wait()
        for c in plain + merged:
            c.wait_recv()
        is_own = owner_x == x
        idx_a = jnp.where(is_own, 0, jnp.where(owner_x == lax.rem(x + 1, 4), 2, 1))
        idx_b = jnp.where(is_own, 0, jnp.where(owner_x == lax.rem(x + 3, 4), 1, 2))
        for kv in range(2):
            for quarter in range(4):
                half = quarter // 2
                idx = idx_a if half == 0 else idx_b
                data = xfin[part][idx, kv, half, quarter % 2].astype(F32)
                for hh in range(2):
                    lanes = slice(hh * 128, (hh + 1) * 128)
                    piece = data[:, lanes]
                    if kv == 0:
                        piece = turn(piece, tab[quarter, 0, at_tok], tab[quarter, 1, at_tok])
                    else:
                        piece = piece * keep[quarter, at_tok]
                    piece = piece + repl[quarter, kv, at_tok, lanes]
                    zsend[part, hh, quarter, kv] = piece.astype(BF16)
        copies = []
        for i in (1, 7, 2, 6, 3, 5, 4):
            t = lax.rem(zc + i, 8)
            c = rcopy(
                zsend.at[part, lax.div(t, 4), lax.rem(t, 4)], zin[part].at[i],
                zs.at[part, i - 1], zr.at[part, i - 1], z_dev(i),
            )
            c.start()
            copies.append(c)
        zin[part][0] = zsend[part, zh, z4]
        return copies

    def g_rows(gg):
        return pl.ds(pl.multiple_of(gg * TOK, TOK), TOK)

    def swap_copy(part):
        piece = kvall.at[part, b1, :, :, g_rows(g), :]
        return rcopy(piece, piece, bs.at[part], br.at[part], other_b)

    def z_finish(part, copies):
        for c in copies:
            c.wait_recv()
        for c in range(2):
            owner_z = lax.rem(lax.div(owner_map[pids[c * 16 + g]], 32), 4)
            idx = lax.rem(zc + 8 - (2 * owner_z + c), 8)
            kvall[part, b1, 0, c, g_rows(g), :] = zin[part][idx, 0]
            kvall[part, b1, 1, c, g_rows(g), :] = zin[part][idx, 1]
        swap_copy(part).start()
        g_start(part, 0)

    def swap_finish(part):
        piece = kvall.at[part, 1 - b1, :, :, g_rows(g), :]
        rcopy(piece, piece, bs.at[part], br.at[part], other_b).wait_recv()
        g_start(part, 1)

    def gather_slices(part, o, gg):
        if o < 2:
            return kvall.at[part, b1 if o == 0 else 1 - b1, :, :, g_rows(gg), :]
        return kvq.at[:, pl.ds(pl.multiple_of(gg * 16, 16), 16), :]

    def reach(o):
        return (4, 3) if o % 2 == 0 else (3, 4)

    def at_y(dy):
        return lax.rem(y + 8 + dy, 8) * 2 + core

    def g_copy(part, o, dy, which, hop):
        piece = gather_slices(part, o, at_y(dy))
        fam = 2 * NP if o == 2 else 2 * part + o
        if which == "up":
            return rcopy(piece, piece, ps.at[fam, hop], pr.at[fam, hop], y_up2 if hop % 2 else y_up)
        if which == "dn":
            return rcopy(piece, piece, ns.at[fam, hop], nr.at[fam, hop], y_dn2 if hop % 2 else y_dn)
        return rcopy(piece, piece, cs.at[fam, hop], cr.at[fam, hop], twin)

    def g_send(part, o, dy, which, hop):
        g_copy(part, o, dy, which, hop).start()

    def g_arrived(part, o, dy, which, hop):
        g_copy(part, o, dy, which, hop).wait_recv()

    def g_start(part, o):
        for hop in (1, 0):
            g_send(part, o, 0, "up", hop)
            g_send(part, o, 0, "dn", hop)
        g_send(part, o, 0, "twin", 0)

    def g_first(part, o):
        n_up, n_dn = reach(o)
        g_arrived(part, o, -2, "up", 1)
        for hop in range(2, n_up):
            g_send(part, o, -2, "up", hop)
        g_arrived(part, o, 2, "dn", 1)
        for hop in range(2, n_dn):
            g_send(part, o, 2, "dn", hop)
        g_send(part, o, -2, "twin", 2)
        g_send(part, o, 2, "twin", 6)
        g_arrived(part, o, -1, "up", 0)
        g_send(part, o, -1, "twin", 1)
        g_arrived(part, o, 1, "dn", 0)
        g_send(part, o, 1, "twin", 5)

    def g_second(part, o):
        n_up, n_dn = reach(o)
        for d in range(3, n_up + 1):
            g_arrived(part, o, -d, "up", d - 1)
            g_send(part, o, -d, "twin", d)
        for d in range(3, n_dn + 1):
            g_arrived(part, o, d, "dn", d - 1)
            g_send(part, o, d, "twin", d if d == 4 else 4 + d)

    def twin_hops(o):
        n_up, n_dn = reach(o)
        return [(0, 0)] + [(-d, d) for d in range(1, n_up + 1)] + [
            (d, d if d == 4 else 4 + d) for d in range(1, n_dn + 1)
        ]

    def g_end(part, o):
        fam = 2 * NP if o == 2 else 2 * part + o
        for dy, hop in twin_hops(o):
            piece = gather_slices(part, o, lax.rem(y + 8 + dy, 8) * 2 + 1 - core)
            rcopy(piece, piece, cs.at[fam, hop], cr.at[fam, hop], twin).wait_recv()

    def g_sent(part, o):
        n_up, n_dn = reach(o)
        for hop in range(n_up):
            g_copy(part, o, 0 if hop < 2 else -2, "up", hop).wait_send()
        for hop in range(n_dn):
            g_copy(part, o, 0 if hop < 2 else 2, "dn", hop).wait_send()
        for dy, hop in twin_hops(o):
            g_copy(part, o, dy, "twin", hop).wait_send()

    relay0 = x_relay(0)
    for c in moves:
        c.wait()
    slot = owner_map[pids[blk]]
    owner_x = lax.div(slot, 128)
    off = pos_off[slot]
    count = rec_count[0]

    freq = freq_ref[...]
    rec_row = rec_index[...].astype(F32)
    off_f = off.astype(F32)
    base_f = (blk * PT).astype(F32)
    slot_lane = lax.broadcasted_iota(jnp.int32, (128, 128), 1)

    @pl.loop(0, 4)
    def _(quarter):
        first = quarter * 128
        tok = lax.broadcasted_iota(jnp.int32, (128, 128), 0) + first
        match = (tok.astype(F32) == jnp.broadcast_to(rec_row, (128, 128))) & (slot_lane < count)
        onehot = jnp.where(match, 1.0, 0.0)
        found = jnp.sum(onehot, axis=1, keepdims=True) > 0.5
        onehot = onehot.astype(BF16)
        tpos = (lax.broadcasted_iota(jnp.int32, (128, 1), 0) + first).astype(F32) + base_f
        tpos = tpos - jnp.where(found, 0.0, off_f)
        c_t, s_t = cos_sin(tpos, freq)
        rk = jnp.dot(onehot, fresh_kv[0], preferred_element_type=F32)
        for hh in range(2):
            lanes = slice(hh * 128, (hh + 1) * 128)
            repl[quarter, 0, :, lanes] = turn(rk[:, lanes], c_t, s_t)
        repl[quarter, 1] = jnp.dot(onehot, fresh_kv[1], preferred_element_type=F32)
        stay = jnp.broadcast_to(jnp.where(found, 0.0, 1.0), (128, 128))
        keep[quarter] = stay
        tab[quarter, 0] = c_t * stay
        tab[quarter, 1] = s_t * stay


    def after(copies):
        for c in copies:
            c.wait_send()

    after(relay0)
    plain0 = x_plain(0)
    merged0 = x_merge(0, relay0, owner_x)

    rec_pos_row = rec_row + (blk * PT).astype(F32)
    rec_pos = to_col(rec_pos_row, 128)
    c_rec, s_rec = cos_sin(rec_pos, freq)

    @pl.loop(0, HEADS)
    def _(hh):
        at = pl.ds(pl.multiple_of(hh * 128, 128), 128)
        q = turn(fresh_q[:, at].astype(F32), c_rec, s_rec) * SCALE
        qall[z_lo, at, :] = q.astype(BF16)

    qpos[z_lo] = jnp.broadcast_to(rec_pos_row, (8, 128))
    ques_pos = (
        lax.broadcasted_iota(jnp.int32, (QDEV, 1), 0) + (QSTART + blk * QDEV)
    ).astype(F32)
    c_q, s_q = cos_sin(ques_pos, freq)
    for hh in range(HEADS):
        lanes = slice(hh * 128, (hh + 1) * 128)
        q = turn(ques_q[:, lanes].astype(F32), c_q, s_q) * SCALE
        qall[z_lo, ROWS + hh * 16:ROWS + (hh + 1) * 16, :] = q.astype(BF16)
    q_copies = []
    for n, ref in enumerate((qall, qpos)):
        c = rcopy(ref.at[z_lo], ref.at[z_lo], qs.at[n], qr.at[n], partner)
        c.start()
        q_copies.append(c)

    my_rows = pl.ds(pl.multiple_of(g * 16, 16), 16)
    kvq[0, my_rows, :] = turn(ques_kv[0].astype(F32), c_q, s_q).astype(BF16)
    kvq[1, my_rows, :] = ques_kv[1]
    g_start(0, 2)
    after(merged0)
    relay1 = x_relay(1)
    z0 = x_finish(0, plain0, merged0, owner_x)
    after(relay1)
    plain1 = x_plain(1)
    merged1 = x_merge(1, relay1, owner_x)
    after(merged1)
    relay2 = x_relay(2)
    z1 = x_finish(1, plain1, merged1, owner_x)
    after(relay2)
    plain2 = x_plain(2)
    merged2 = x_merge(2, relay2, owner_x)
    g_first(0, 2)
    z_finish(0, z0)
    after(merged2)
    relay3 = x_relay(3)
    z2 = x_finish(2, plain2, merged2, owner_x)
    after(relay3)
    plain3 = x_plain(3)
    merged3 = x_merge(3, relay3, owner_x)
    swap_finish(0)
    z_finish(1, z1)
    g_first(0, 0)
    g_second(0, 2)
    z3 = x_finish(3, plain3, merged3, owner_x)
    g_first(0, 1)
    swap_finish(1)
    g_first(1, 0)
    z_finish(2, z2)
    g_second(0, 0)
    g_second(0, 1)
    g_first(1, 1)
    swap_finish(2)
    g_first(2, 0)
    z_finish(3, z3)
    g_second(1, 0)
    g_second(1, 1)
    g_first(2, 1)
    swap_finish(3)
    g_end(0, 2)
    g_end(0, 0)
    g_end(0, 1)
    for c in q_copies:
        c.wait_recv()

    key_lane = lax.broadcasted_iota(jnp.int32, (1, 2 * CHUNK), 1)
    key_in = lax.rem(key_lane, CHUNK)
    key_off = lax.div(key_in, TOK) * PT + lax.rem(key_in, TOK)
    key_off = (key_off + (2 * lax.div(key_lane, CHUNK) + z_lo) * 128).astype(F32)
    ones = jnp.ones((2 * CHUNK, 128), BF16)

    def chunk_of(part, b, kv, ch):
        return kvall[part, b, kv, ch]

    def transpose_keys(part):
        for ch in range(2):
            for b in range(2):
                kt[ch, :, b * CHUNK:(b + 1) * CHUNK] = jnp.transpose(chunk_of(part, b, 0, ch))

    def v_chunk(part, ch):
        v = jnp.concatenate([chunk_of(part, b, 1, ch) for b in range(2)], axis=0)
        return jnp.concatenate([v, ones], axis=1)

    def fold(s):
        m = s[:, 0:128]
        for j in range(1, s.shape[1] // 128):
            m = jnp.maximum(m, s[:, j * 128:(j + 1) * 128])
        return m

    def wide(m, n):
        return jnp.concatenate([m] * (n // 128), axis=1)

    def attend(n, rows_each, q_of, part, open_chunks, closing, m_ref, a_ref):
        blocks = [(b, slice(b * rows_each, (b + 1) * rows_each)) for b in range(n)]
        when, last_keys, last_values, mask = closing

        def step(b, rows, k, v, seen):
            s = jnp.dot(q_of(b), k, preferred_element_type=F32)
            if seen is not None:
                s = jnp.where(seen, s, FLOOR)
            old = m_ref[rows, :]
            new = jnp.maximum(old, jnp.max(fold(s), axis=1, keepdims=True))
            m_ref[rows, :] = new
            p = jnp.exp(s - wide(new, s.shape[1])).astype(BF16)
            scale = wide(jnp.exp(old - new), 256)
            a_ref[rows, :] = a_ref[rows, :] * scale + jnp.dot(p, v, preferred_element_type=F32)

        @pl.loop(0, open_chunks)
        def _(ch):
            k = kt[ch]
            v = v_chunk(part, ch)
            for b, rows in blocks:
                step(b, rows, k, v, None)

        def close():
            k = last_keys()
            v = last_values()
            seen = mask()
            for b, rows in blocks:
                step(b, rows, k, v, seen)

        if when is None:
            close()
        else:
            pl.when(when)(close)

    def log_sum(m, total, n):
        return to_row(m, n) + jnp.log(jnp.maximum(to_row(total, n), 1e-30))

    lsend[...] = jnp.zeros((2, 8, 128), F32)
    mst[...] = jnp.full((3, ROWS, 128), FLOOR, F32)
    ast[...] = jnp.zeros((3, ROWS, 256), F32)

    def out_copy(n):
        a, b = ((osend, orecv), (lsend, lrecv))[n]
        return rcopy(a.at[1 - z_lo], b.at[z_lo], os_.at[n], or_.at[n], partner)

    def ques_mask():
        row = lax.broadcasted_iota(jnp.int32, (2 * QROWS, 1), 0)
        row_pos = lax.div(row, QROWS) * 256 + g * 16 + lax.rem(row, 16)
        col = lax.broadcasted_iota(jnp.int32, (1, 256), 1)
        return z_lo * 256 + col <= row_pos

    def ques_pass(part):
        closing = (
            part == 0, lambda: jnp.transpose(kvq[0]),
            lambda: jnp.concatenate([kvq[1], ones[0:256]], axis=1), ques_mask,
        )
        attend(
            1, 2 * QROWS, lambda b: jnp.concatenate([qall[j, ROWS:, :] for j in range(2)], axis=0),
            part, 2, closing, mst.at[2], ast.at[2],
        )

        @pl.when(part == NP - 1)
        def _():
            for src in range(2):
                rows = slice(src * QROWS, (src + 1) * QROWS)
                total = ast[2, rows, 128:256]
                osend[src, ROWS:, :] = (ast[2, rows, 0:128] / total).astype(BF16)
                lsend[src, 6:7, :] = log_sum(mst[2, rows, :], total, QROWS)

    def rec_pass(part, c):
        n_open = c
        pos_col = to_col(qpos[c, 0:1, :], 128)
        pos_col = jnp.concatenate([pos_col] * 3, axis=0)
        key_pos = key_off + (n_open * (16 * PT) + part * TOK).astype(F32)
        closing = (
            None, lambda: kt[n_open], lambda: v_chunk(part, n_open),
            lambda: key_pos <= pos_col,
        )
        attend(
            2, 384, lambda b: qall[c, b * 384:(b + 1) * 384, :],
            part, n_open, closing, mst.at[c], ast.at[c],
        )

    def rec_end(c):
        for hh in range(HEADS):
            rows = slice(hh * 128, (hh + 1) * 128)
            total = ast[c, rows, 128:256]
            osend[c, rows, :] = (ast[c, rows, 0:128] / total).astype(BF16)
            lsend[c, hh:hh + 1, :] = log_sum(mst[c, rows, :], total, 128)

    @pl.loop(0, NP)
    def _(part):
        transpose_keys(part)
        ques_pass(part)

        @pl.loop(0, 2)
        def _(t):
            @pl.when((part == 0) & (t == 0))
            def _():
                g_first(3, 0)
                g_second(2, 0)
                g_second(2, 1)
                g_first(3, 1)

            @pl.when((part == 1) & (t == 0))
            def _():
                g_second(3, 0)
                g_second(3, 1)

            c = lax.rem(z_lo + 1 + t, 2)
            rec_pass(part, c)

            @pl.when(part == NP - 1)
            def _():
                rec_end(c)

            @pl.when((part == NP - 1) & (t == 0))
            def _():
                for n in range(2):
                    out_copy(n).start()

        @pl.when(part < NP - 1)
        def _():
            g_end(part + 1, 0)
            g_end(part + 1, 1)

    orecv[z_lo] = osend[z_lo]
    lrecv[z_lo] = lsend[z_lo]
    out_copies = [out_copy(n) for n in range(2)]
    for c in out_copies:
        c.wait_recv()

    def join(parts, lses, n):
        cols_ = [to_col(l, n) for l in lses]
        top_ = functools.reduce(jnp.maximum, cols_)
        ws = [jnp.exp(c - top_) for c in cols_]
        total = ws[0] + ws[1]
        acc = ws[0] * parts[0].astype(F32)
        for w, part in zip(ws[1:], parts[1:]):
            acc = acc + w * part.astype(F32)
        return acc / total

    used = lax.broadcasted_iota(jnp.int32, (128, 1), 0) < count

    @pl.loop(0, HEADS)
    def _(hh):
        rows = pl.ds(pl.multiple_of(hh * 128, 128), 128)
        o = join([orecv[j, rows, :] for j in range(2)], [lrecv[j, pl.ds(hh, 1), :] for j in range(2)], 128)
        rec_out[:, rows] = jnp.where(used, o, 0.0).astype(BF16)

    o = join([orecv[j, ROWS:, :] for j in range(2)], [lrecv[j, 6:7, :] for j in range(2)], QROWS)
    for hh in range(HEADS):
        ques_out[:, hh * 128:(hh + 1) * 128] = o[hh * 16:(hh + 1) * 16].astype(BF16)

    for c in plain0 + plain1 + plain2 + plain3 + merged3 + z0 + z1 + z2 + z3 + q_copies + out_copies:
        c.wait_send()
    g_sent(0, 2)

    @pl.loop(0, NP)
    def _(part):
        g_sent(part, 0)
        g_sent(part, 1)
        swap_copy(part).wait_send()


def on_device(
    k_store, v_store, pos_offset, owner_map, passage_ids, rec_index, rec_count,
    fresh_q, fresh_k, fresh_v, ques_q, ques_k, ques_v,
):
    vmem = pl.BlockSpec(memory_space=pltpu.VMEM)
    anym = pl.BlockSpec(memory_space=pl.ANY)
    dma = pltpu.SemaphoreType.DMA
    v = pltpu.VMEM
    smem = pltpu.SMEM
    i32 = jnp.int32
    return pl.pallas_call(
        kernel,
        out_shape=(
            jax.ShapeDtypeStruct((RECP, HEADS * HD), BF16),
            jax.ShapeDtypeStruct((QDEV, HEADS * HD), BF16),
        ),
        in_specs=[anym] * 14,
        out_specs=(vmem, vmem),
        scratch_shapes=[
            smem((512,), i32), smem((512,), i32), smem((32,), i32), smem((1,), i32),
            v((1, 128), i32), v((1, 128), F32), v((RECP, HEADS * HD), BF16),
            v((2, RECP, 256), BF16), v((QDEV, HEADS * HD), BF16), v((2, QDEV, 128), BF16),
            (v((3, 2, 2, 2, TOK, 256), BF16),) * NP,
            ((v((2, 2, 2, TOK, 256), BF16),) * 2,) * NP,
            v((NP, 2, 2, 2, TOK, 256), BF16),
            v((NP, 2, 4, 2, TOK, 128), BF16),
            (v((8, 2, TOK, 128), BF16),) * NP,
            v((4, 2, 128, 128), F32),
            v((4, 128, 128), F32),
            v((4, 2, 128, 256), F32),
            v((NP, 2, 2, 2, 16 * TOK, 128), BF16),
            v((2, 256, 128), BF16),
            v((2, ROWS + QROWS, 128), BF16),
            v((2, 8, 128), F32),
            v((2, 128, 2 * CHUNK), BF16),
            v((3, ROWS, 128), F32), v((3, ROWS, 256), F32),
            v((2, ROWS + QROWS, 128), BF16),
            v((2, ROWS + QROWS, 128), BF16),
            v((2, 8, 128), F32),
            v((2, 8, 128), F32),
            dma((12,)),
            dma((NP, 2, 4)),
            dma((NP, 6, 2)), dma((NP, 6, 2)),
            dma((NP, 7)), dma((NP, 7)),
            dma((NP,)), dma((NP,)),
            dma((2,)), dma((2,)),
            dma((9, 4)), dma((9, 4)),
            dma((9, 4)), dma((9, 4)),
            dma((9, 8)), dma((9, 8)),
            dma((2,)), dma((2,)),
        ],
        compiler_params=pltpu.CompilerParams(
            collective_id=0, has_side_effects=True, vmem_limit_bytes=VMEM_LIMIT
        ),
        cost_estimate=pl.CostEstimate(
            flops=8_000_000_000, bytes_accessed=4_000_000, transcendentals=15_000_000
        ),
        name="blend_attend",
    )(
        pos_offset, owner_map, passage_ids, rec_count, rec_index, jnp.asarray(freq_table()),
        fresh_q, fresh_k, fresh_v, ques_q, ques_k, ques_v,
        k_store.reshape(4, 128, 1024), v_store.reshape(4, 128, 1024),
    )


def solution(mesh):
    return jax.shard_map(
        on_device,
        mesh=mesh,
        in_specs=(
            P(("bank", "blk"), None, None),
            P(("bank", "blk"), None, None),
            P(),
            P(),
            P(),
            P("blk", None),
            P("blk"),
            P("blk", "bank"),
            P("blk", None),
            P("blk", None),
            P("blk", "bank"),
            P("blk", None),
            P("blk", None),
        ),
        out_specs=(P("blk", "bank"), P("blk", "bank")),
        check_vma=False,
    )
```

```python
import functools

import jax
import jax.numpy as jnp
import numpy as np
from jax import lax
from jax.experimental import pallas as pl
from jax.experimental.pallas import tpu as pltpu
from jax.sharding import PartitionSpec as P

HD = 128
PT = 512
RECP = 128
QDEV = 16
PASS = 32
HEADS = 6
ROWS = HEADS * RECP
QROWS = HEADS * QDEV
QSTART = PASS * PT
CHUNK = 512
NP = 2
TOK = 64
VMEM_LIMIT = 62 * 1024 * 1024
FLOOR = -1e30
SCALE = float(1.0 / np.sqrt(128.0))
MESH = pl.DeviceIdType.MESH
F32 = jnp.float32
BF16 = jnp.bfloat16

INV_2PI = float(1.0 / (2.0 * np.pi))
PI_A = 6.28125
PI_B = 0.0019350051879882812
PI_C = 3.0199159795074593e-07
SIN_C = [float((-1.0) ** k / np.prod(np.arange(1, 2 * k + 2, dtype=np.float64))) for k in range(9)]
COS_C = [float((-1.0) ** k / np.prod(np.arange(1, 2 * k + 1, dtype=np.float64))) for k in range(10)]


def freq_table():
    half = HD // 2
    freqs = 1000000.0 ** (-np.arange(half, dtype=np.float64) * 2.0 / HD)
    return np.concatenate([freqs, freqs])[None, :].astype(np.float32)


def cos_sin(pos, freq):
    angle = pos * freq
    turns = jnp.floor(angle * INV_2PI + 0.5)
    r = ((angle - turns * PI_A) - turns * PI_B) - turns * PI_C
    r2 = r * r
    s = jnp.full_like(r, SIN_C[8])
    for k in range(7, -1, -1):
        s = s * r2 + SIN_C[k]
    s = s * r
    c = jnp.full_like(r, COS_C[9])
    for k in range(8, -1, -1):
        c = c * r2 + COS_C[k]
    lane = lax.broadcasted_iota(jnp.int32, s.shape, 1)
    return c, jnp.where(lane < HD // 2, -s, s)


def turn(x, c, s):
    return x * c + pltpu.roll(x, HD // 2, 1) * s


def eye_mask(n, m):
    row = lax.broadcasted_iota(jnp.int32, (n, m), 0)
    col = lax.broadcasted_iota(jnp.int32, (n, m), 1)
    return row == col


def to_col(row, n):
    full = jnp.broadcast_to(row, (n, 128))
    return jnp.sum(jnp.where(eye_mask(n, 128), full, 0.0), axis=1, keepdims=True)


def to_row(col, n):
    return jnp.sum(jnp.where(eye_mask(n, 128), col, 0.0), axis=0, keepdims=True)


def nt_dot(a, b):
    return lax.dot_general(a, b, (((1,), (1,)), ((), ())), preferred_element_type=F32)


def kernel(
    pos_off_h, owner_map_h, pids_h, rec_count_h, rec_index_h, freq_h, fresh_q_h, fresh_k_h,
    fresh_v_h, ques_q_h, ques_k_h, ques_v_h, k_store, v_store,
    rec_out, ques_out,
    pos_off, owner_map, pids, rec_count, rec_index, freq_ref, fresh_q, fresh_kv, ques_q, ques_kv,
    stage, xfin, mbuf, msend, zsend, zin0, zin1, tab, keep, repl, kvall,
    qall, qpos, kt, mst, ast,
    osend, orecv, lsend, lrecv,
    isem, lsem, xs, xr, zs, zr, bs, br, qs, qr, ps, pr, ns, nr, cs, cr, os_, or_,
):
    zin = (zin0, zin1)
    bank = lax.axis_index("bank")
    blk = lax.axis_index("blk")
    x = lax.div(bank, 4)
    z_hi = lax.rem(bank, 4)
    zh = lax.div(z_hi, 2)
    b1 = lax.rem(z_hi, 2)
    z_lo = lax.div(blk, 16)
    g = lax.rem(blk, 16)
    y = lax.div(g, 2)
    core = lax.rem(g, 2)
    zc = 2 * z_hi + z_lo
    z4 = 2 * b1 + z_lo
    head = 2 * x + zh

    def dev(xx, zz, gg):
        return (xx * 4 + lax.div(zz, 2), lax.rem(zz, 2) * 16 + gg)

    x_up = dev(lax.rem(x + 1, 4), zc, g)
    x_dn = dev(lax.rem(x + 3, 4), zc, g)
    y_up = dev(x, zc, lax.rem(y + 1, 8) * 2 + core)
    y_dn = dev(x, zc, lax.rem(y + 7, 8) * 2 + core)
    y_up2 = dev(x, zc, lax.rem(y + 2, 8) * 2 + core)
    y_dn2 = dev(x, zc, lax.rem(y + 6, 8) * 2 + core)
    twin = dev(x, zc, y * 2 + 1 - core)

    def z_dev(i):
        return dev(x, lax.rem(zc + i, 8), g)

    partner = dev(x, 4 * zh + 2 * b1 + 1 - z_lo, g)
    other_b = dev(x, 4 * zh + 2 * (1 - b1) + z_lo, g)

    def rcopy(src, dst, ssem, rsem, where):
        return pltpu.make_async_remote_copy(
            src_ref=src, dst_ref=dst, send_sem=ssem, recv_sem=rsem,
            device_id=where, device_id_type=MESH,
        )

    def cols(xx):
        return pl.ds(pl.multiple_of(lax.rem(xx, 4) * 256, 256), 256)

    hcol = pl.ds(pl.multiple_of(head * 128, 128), 128)

    barrier = pltpu.get_barrier_semaphore()
    peers = [x_up, x_dn, y_up, y_dn, y_up2, y_dn2, twin] + [z_dev(i) for i in range(1, 8)]
    for peer in peers:
        pl.semaphore_signal(barrier, inc=1, device_id=peer, device_id_type=MESH)

    moves = [
        (fresh_q_h, fresh_q), (rec_index_h, rec_index), (freq_h, freq_ref), (ques_q_h, ques_q),
        (ques_k_h.at[:, hcol], ques_kv.at[0]), (ques_v_h.at[:, hcol], ques_kv.at[1]),
        (owner_map_h, owner_map), (pids_h, pids), (pos_off_h, pos_off), (rec_count_h, rec_count),
        (fresh_k_h.at[:, cols(x)], fresh_kv.at[0]), (fresh_v_h.at[:, cols(x)], fresh_kv.at[1]),
    ]
    moves = [pltpu.make_async_copy(a, b, isem.at[i]) for i, (a, b) in enumerate(moves)]
    for c in moves:
        c.start()

    staged = []
    for kv, st in enumerate((k_store, v_store)):
        for t in range(4):
            c = pltpu.make_async_copy(st.at[:, :, t * 256:(t + 1) * 256], stage.at[t, kv], lsem.at[kv, t])
            c.start()
            staged.append(c)
    top = pl.ds(0, 2)
    low = pl.ds(2, 2)

    def toks(part):
        return pl.ds(part * TOK, TOK)

    for c in staged:
        c.wait()
    pl.semaphore_wait(barrier, len(peers))

    def x_relay(part):
        far = lax.rem(x + 2, 4)
        copies = [
            rcopy(stage.at[far, :, top, toks(part)], mbuf.at[part, 0], xs.at[part, 0], xr.at[part, 0], x_up),
            rcopy(stage.at[far, :, low, toks(part)], mbuf.at[part, 1], xs.at[part, 1], xr.at[part, 1], x_dn),
        ]
        for c in copies:
            c.start()
        return copies

    def x_plain(part):
        up, dn = lax.rem(x + 1, 4), lax.rem(x + 3, 4)
        copies = [
            rcopy(stage.at[up, :, low, toks(part)], xfin.at[part, 0, :, low], xs.at[part, 2], xr.at[part, 2], x_up),
            rcopy(stage.at[dn, :, top, toks(part)], xfin.at[part, 1, :, top], xs.at[part, 3], xr.at[part, 3], x_dn),
        ]
        for c in copies:
            c.start()
        return copies

    def x_merge(part, relay, owner_x):
        copies = []
        for d in range(2):
            half = (top, low)[d]
            relay[d].wait_recv()
            target = lax.rem(x + (1 if d == 0 else 3), 4)
            source = lax.rem(x + (3 if d == 0 else 1), 4)
            mine = stage[target, :, half, toks(part), :]
            msend[part, d] = jnp.where(owner_x == source, mbuf[part, d], mine)
            c = rcopy(msend.at[part, d], xfin.at[part, d, :, half], xs.at[part, 4 + d], xr.at[part, 4 + d],
                      x_up if d == 0 else x_dn)
            c.start()
            copies.append(c)
        return copies

    def x_finish(part, plain, merged, owner_x, between):
        for c in plain + merged:
            c.wait_recv()
        is_own = owner_x == x
        from_up = owner_x == lax.rem(x + 1, 4)
        from_dn = owner_x == lax.rem(x + 3, 4)
        for kv in range(2):
            for quarter in range(4):
                sides = [xfin[part, side, kv, quarter] for side in range(2)]
                if quarter < 2:
                    data = jnp.where(from_up, sides[1], sides[0])
                else:
                    data = jnp.where(from_dn, sides[0], sides[1])
                data = jnp.where(is_own, stage[x, kv, quarter, toks(part), :], data).astype(F32)
                for hh in range(2):
                    lanes = slice(hh * 128, (hh + 1) * 128)
                    piece = data[:, lanes]
                    if kv == 0:
                        piece = turn(piece, tab[part, quarter, 0], tab[part, quarter, 1])
                    else:
                        piece = piece * keep[part, quarter]
                    piece = piece + repl[part, quarter, kv, :, lanes]
                    zsend[part, hh, quarter, kv] = piece.astype(BF16)
            if kv == 0 and between is not None:
                between()
        copies = []
        for i in (1, 7, 2, 6, 3, 5, 4):
            t = lax.rem(zc + i, 8)
            c = rcopy(
                zsend.at[part, lax.div(t, 4), lax.rem(t, 4)], zin[part].at[i],
                zs.at[part, i - 1], zr.at[part, i - 1], z_dev(i),
            )
            c.start()
            copies.append(c)
        zin[part][0] = zsend[part, zh, z4]
        return copies

    def rows_of(b, kv, c):
        return pl.ds(pl.multiple_of(((b * 2 + kv) * 2 + c) * TOK, TOK), TOK)

    def swap_copy(part):
        piece = kvall.at[part, g, pl.ds(pl.multiple_of(b1 * 4 * TOK, 4 * TOK), 4 * TOK), :]
        return rcopy(piece, piece, bs.at[part], br.at[part], other_b)

    def z_finish(part, copies):
        for c in copies:
            c.wait_recv()
        for c in range(2):
            owner_z = lax.rem(lax.div(owner_map[pids[c * 16 + g]], 32), 4)
            idx = lax.rem(zc + 8 - (2 * owner_z + c), 8)
            for kv in range(2):
                kvall[part, g, rows_of(b1, kv, c), :] = zin[part][idx, kv]
        swap_copy(part).start()

    def swap_finish(part):
        piece = kvall.at[part, g, pl.ds(pl.multiple_of((1 - b1) * 4 * TOK, 4 * TOK), 4 * TOK), :]
        rcopy(piece, piece, bs.at[part], br.at[part], other_b).wait_recv()
        g_start(part)

    def gather_slices(fam, gg):
        return kvall.at[fam, gg, pl.ds(0, 8 * TOK + (32 if fam == 0 else 0)), :]

    def reach(fam):
        return (4, 3) if fam % 2 == 0 else (3, 4)

    def at_y(dy):
        return lax.rem(y + 8 + dy, 8) * 2 + core

    def g_copy(fam, dy, which, hop):
        piece = gather_slices(fam, at_y(dy))
        if which == "up":
            return rcopy(piece, piece, ps.at[fam, hop], pr.at[fam, hop], y_up2 if hop % 2 else y_up)
        if which == "dn":
            return rcopy(piece, piece, ns.at[fam, hop], nr.at[fam, hop], y_dn2 if hop % 2 else y_dn)
        return rcopy(piece, piece, cs.at[fam, hop], cr.at[fam, hop], twin)

    def g_send(fam, dy, which, hop):
        g_copy(fam, dy, which, hop).start()

    def g_arrived(fam, dy, which, hop):
        g_copy(fam, dy, which, hop).wait_recv()

    def g_start(fam):
        for hop in range(2):
            g_send(fam, 0, "up", hop)
            g_send(fam, 0, "dn", hop)
        g_send(fam, 0, "twin", 0)

    def g_first(fam):
        n_up, n_dn = reach(fam)
        g_arrived(fam, -2, "up", 1)
        for hop in range(2, n_up):
            g_send(fam, -2, "up", hop)
        g_arrived(fam, 2, "dn", 1)
        for hop in range(2, n_dn):
            g_send(fam, 2, "dn", hop)
        g_send(fam, -2, "twin", 2)
        g_send(fam, 2, "twin", 6)
        g_arrived(fam, -1, "up", 0)
        g_send(fam, -1, "twin", 1)
        g_arrived(fam, 1, "dn", 0)
        g_send(fam, 1, "twin", 5)

    def g_second(fam):
        n_up, n_dn = reach(fam)
        for d in range(3, n_up + 1):
            g_arrived(fam, -d, "up", d - 1)
            g_send(fam, -d, "twin", d)
        for d in range(3, n_dn + 1):
            g_arrived(fam, d, "dn", d - 1)
            g_send(fam, d, "twin", d if d == 4 else 4 + d)

    def twin_hops(fam):
        n_up, n_dn = reach(fam)
        return [(0, 0)] + [(-d, d) for d in range(1, n_up + 1)] + [
            (d, d if d == 4 else 4 + d) for d in range(1, n_dn + 1)
        ]

    def g_end(fam):
        for dy, hop in twin_hops(fam):
            piece = gather_slices(fam, lax.rem(y + 8 + dy, 8) * 2 + 1 - core)
            rcopy(piece, piece, cs.at[fam, hop], cr.at[fam, hop], twin).wait_recv()

    def g_sent(fam):
        n_up, n_dn = reach(fam)
        for hop in range(n_up):
            g_copy(fam, 0 if hop < 2 else -2, "up", hop).wait_send()
        for hop in range(n_dn):
            g_copy(fam, 0 if hop < 2 else 2, "dn", hop).wait_send()
        for dy, hop in twin_hops(fam):
            g_copy(fam, dy, "twin", hop).wait_send()

    relay0 = x_relay(0)
    for c in moves:
        c.wait()
    slot = owner_map[pids[blk]]
    owner_x = lax.div(slot, 128)
    off = pos_off[slot]
    count = rec_count[0]

    freq = freq_ref[...]
    rec_row = rec_index[...].astype(F32)
    rec_pos_row = rec_row + (blk * PT).astype(F32)
    rec_pos = to_col(rec_pos_row, 128)
    c_rec, s_rec = cos_sin(rec_pos, freq)

    @pl.loop(0, HEADS)
    def _(hh):
        at = pl.ds(pl.multiple_of(hh * 128, 128), 128)
        q = turn(fresh_q[:, at].astype(F32), c_rec, s_rec) * SCALE
        qall[z_lo, at, :] = q.astype(BF16)

    qpos[z_lo] = jnp.broadcast_to(rec_pos_row, (8, 128))
    for c in relay0:
        c.wait_send()
    plain0 = x_plain(0)
    ques_pos = (
        lax.broadcasted_iota(jnp.int32, (QDEV, 1), 0) + (QSTART + blk * QDEV)
    ).astype(F32)
    c_q, s_q = cos_sin(ques_pos, freq)
    for hh in range(HEADS):
        lanes = slice(hh * 128, (hh + 1) * 128)
        q = turn(ques_q[:, lanes].astype(F32), c_q, s_q) * SCALE
        qall[z_lo, ROWS + hh * 16:ROWS + (hh + 1) * 16, :] = q.astype(BF16)
    q_copies = []
    for n, ref in enumerate((qall, qpos)):
        c = rcopy(ref.at[z_lo], ref.at[z_lo], qs.at[n], qr.at[n], partner)
        c.start()
        q_copies.append(c)

    kvall[0, g, 8 * TOK:8 * TOK + 16, :] = turn(ques_kv[0].astype(F32), c_q, s_q).astype(BF16)
    kvall[0, g, 8 * TOK + 16:8 * TOK + 32, :] = ques_kv[1]
    merged0 = x_merge(0, relay0, owner_x)

    off_f = off.astype(F32)
    base_f = (blk * PT).astype(F32)
    slot_lane = lax.broadcasted_iota(jnp.int32, (TOK, 128), 1)

    def tables(part):
        @pl.loop(0, 4)
        def _(quarter):
            first = quarter * 128 + part * TOK
            tok = lax.broadcasted_iota(jnp.int32, (TOK, 128), 0) + first
            match = (tok.astype(F32) == jnp.broadcast_to(rec_row, (TOK, 128))) & (slot_lane < count)
            onehot = jnp.where(match, 1.0, 0.0)
            found = jnp.sum(onehot, axis=1, keepdims=True) > 0.5
            onehot = onehot.astype(BF16)
            tpos = (lax.broadcasted_iota(jnp.int32, (TOK, 1), 0) + first).astype(F32) + base_f
            tpos = tpos - jnp.where(found, 0.0, off_f)
            c_t, s_t = cos_sin(tpos, freq)
            rk = jnp.dot(onehot, fresh_kv[0], preferred_element_type=F32)
            for hh in range(2):
                lanes = slice(hh * 128, (hh + 1) * 128)
                repl[part, quarter, 0, :, lanes] = turn(rk[:, lanes], c_t, s_t)
            repl[part, quarter, 1] = jnp.dot(onehot, fresh_kv[1], preferred_element_type=F32)
            stay = jnp.broadcast_to(jnp.where(found, 0.0, 1.0), (TOK, 128))
            keep[part, quarter] = stay
            tab[part, quarter, 0] = c_t * stay
            tab[part, quarter, 1] = s_t * stay

    tables(0)
    for c in merged0:
        c.wait_send()
    relay1 = x_relay(1)
    tables(1)
    plain1 = []

    def go_plain1():
        for c in relay1:
            c.wait_send()
        plain1.extend(x_plain(1))

    z0 = x_finish(0, plain0, merged0, owner_x, go_plain1)
    merged1 = x_merge(1, relay1, owner_x)
    z_finish(0, z0)
    z1 = x_finish(1, plain1, merged1, owner_x, None)
    swap_finish(0)
    z_finish(1, z1)
    g_first(0)
    swap_finish(1)
    g_second(0)
    g_end(0)
    for c in q_copies:
        c.wait_recv()

    key_lane = lax.broadcasted_iota(jnp.int32, (1, 2 * CHUNK), 1)
    key_in = lax.rem(key_lane, CHUNK)
    key_off = lax.div(key_in, TOK) * PT + lax.rem(key_in, TOK)
    key_off = (key_off + (2 * lax.div(key_lane, CHUNK) + z_lo) * 128).astype(F32)
    ones = jnp.ones((2 * CHUNK, 128), BF16)

    def chunk_of(part, b, kv, ch):
        groups = pl.ds(pl.multiple_of(lax.rem(ch, 2) * 8, 8), 8)
        return kvall[part, groups, rows_of(b, kv, lax.div(ch, 2)), :].reshape(CHUNK, 128)

    def ques_block(kv):
        first = 8 * TOK + kv * 16
        return kvall[0, :, first:first + 16, :].reshape(256, 128)

    def transpose_keys(part):
        @pl.loop(0, 4)
        def _(ch):
            for b in range(2):
                kt[ch, :, b * CHUNK:(b + 1) * CHUNK] = jnp.transpose(chunk_of(part, b, 0, ch))

    def v_chunk(part, ch):
        v = jnp.concatenate([chunk_of(part, b, 1, ch) for b in range(2)], axis=0)
        return jnp.concatenate([v, ones], axis=1)

    def fold(s):
        m = s[:, 0:128]
        for j in range(1, s.shape[1] // 128):
            m = jnp.maximum(m, s[:, j * 128:(j + 1) * 128])
        return m

    def wide(m, n):
        return jnp.concatenate([m] * (n // 128), axis=1)

    def attend(n, rows_each, q_of, part, open_chunks, closing, m_ref, a_ref):
        blocks = [(b, slice(b * rows_each, (b + 1) * rows_each)) for b in range(n)]
        when, last_keys, last_values, mask = closing

        def step(b, rows, k, v, seen):
            s = jnp.dot(q_of(b), k, preferred_element_type=F32)
            if seen is not None:
                s = jnp.where(seen, s, FLOOR)
            old = m_ref[rows, :]
            new = jnp.maximum(old, jnp.max(fold(s), axis=1, keepdims=True))
            m_ref[rows, :] = new
            p = jnp.exp(s - wide(new, s.shape[1])).astype(BF16)
            scale = wide(jnp.exp(old - new), 256)
            a_ref[rows, :] = a_ref[rows, :] * scale + jnp.dot(p, v, preferred_element_type=F32)

        @pl.loop(0, open_chunks)
        def _(ch):
            k = kt[ch]
            v = v_chunk(part, ch)
            for b, rows in blocks:
                step(b, rows, k, v, None)

        def close():
            k = last_keys()
            v = last_values()
            seen = mask()
            for b, rows in blocks:
                step(b, rows, k, v, seen)

        if when is None:
            close()
        else:
            pl.when(when)(close)

    def log_sum(m, total, n):
        return to_row(m, n) + jnp.log(jnp.maximum(to_row(total, n), 1e-30))

    lsend[...] = jnp.zeros((2, 8, 128), F32)
    mst[...] = jnp.full((3, ROWS, 128), FLOOR, F32)
    ast[...] = jnp.zeros((3, ROWS, 256), F32)

    def out_copy(n):
        a, b = ((osend, orecv), (lsend, lrecv))[n]
        return rcopy(a.at[1 - z_lo], b.at[z_lo], os_.at[n], or_.at[n], partner)

    def ques_mask():
        row = lax.broadcasted_iota(jnp.int32, (2 * QROWS, 1), 0)
        row_pos = lax.div(row, QROWS) * 256 + g * 16 + lax.rem(row, 16)
        col = lax.broadcasted_iota(jnp.int32, (1, 256), 1)
        return z_lo * 256 + col <= row_pos

    def ques_pass(part):
        closing = (
            part == 0, lambda: jnp.transpose(ques_block(0)),
            lambda: jnp.concatenate([ques_block(1), ones[0:256]], axis=1), ques_mask,
        )
        attend(
            1, 2 * QROWS, lambda b: jnp.concatenate([qall[j, ROWS:, :] for j in range(2)], axis=0),
            part, 4, closing, mst.at[2], ast.at[2],
        )

        @pl.when(part == NP - 1)
        def _():
            for src in range(2):
                rows = slice(src * QROWS, (src + 1) * QROWS)
                total = ast[2, rows, 128:256]
                osend[src, ROWS:, :] = (ast[2, rows, 0:128] / total).astype(BF16)
                lsend[src, 6:7, :] = log_sum(mst[2, rows, :], total, QROWS)

    def rec_pass(part, c):
        n_open = 2 * c + lax.div(g, 8)
        pos_col = to_col(qpos[c, 0:1, :], 128)
        pos_col = jnp.concatenate([pos_col] * 3, axis=0)
        key_pos = key_off + (n_open * (8 * PT) + part * TOK).astype(F32)
        closing = (
            None, lambda: kt[n_open], lambda: v_chunk(part, n_open),
            lambda: key_pos <= pos_col,
        )
        attend(
            2, 384, lambda b: qall[c, b * 384:(b + 1) * 384, :],
            part, n_open, closing, mst.at[c], ast.at[c],
        )

    def rec_end(c):
        for hh in range(HEADS):
            rows = slice(hh * 128, (hh + 1) * 128)
            total = ast[c, rows, 128:256]
            osend[c, rows, :] = (ast[c, rows, 0:128] / total).astype(BF16)
            lsend[c, hh:hh + 1, :] = log_sum(mst[c, rows, :], total, 128)

    @pl.loop(0, NP)
    def _(part):
        transpose_keys(part)
        ques_pass(part)

        @pl.loop(0, 2)
        def _(t):
            @pl.when((part == 0) & (t == 0))
            def _():
                g_first(1)

            @pl.when((part == 0) & (t == 1))
            def _():
                g_second(1)

            c = lax.rem(z_lo + 1 + t, 2)
            rec_pass(part, c)

            @pl.when(part == NP - 1)
            def _():
                rec_end(c)

            @pl.when((part == NP - 1) & (t == 0))
            def _():
                for n in range(2):
                    out_copy(n).start()

        @pl.when(part == 0)
        def _():
            g_end(1)

    orecv[z_lo] = osend[z_lo]
    lrecv[z_lo] = lsend[z_lo]
    out_copies = [out_copy(n) for n in range(2)]
    for c in out_copies:
        c.wait_recv()

    def join(parts, lses, n):
        cols_ = [to_col(l, n) for l in lses]
        top_ = functools.reduce(jnp.maximum, cols_)
        ws = [jnp.exp(c - top_) for c in cols_]
        total = ws[0] + ws[1]
        acc = ws[0] * parts[0].astype(F32)
        for w, part in zip(ws[1:], parts[1:]):
            acc = acc + w * part.astype(F32)
        return acc / total

    used = lax.broadcasted_iota(jnp.int32, (128, 1), 0) < count

    @pl.loop(0, HEADS)
    def _(hh):
        rows = pl.ds(pl.multiple_of(hh * 128, 128), 128)
        o = join([orecv[j, rows, :] for j in range(2)], [lrecv[j, pl.ds(hh, 1), :] for j in range(2)], 128)
        rec_out[:, rows] = jnp.where(used, o, 0.0).astype(BF16)

    o = join([orecv[j, ROWS:, :] for j in range(2)], [lrecv[j, 6:7, :] for j in range(2)], QROWS)
    for hh in range(HEADS):
        ques_out[:, hh * 128:(hh + 1) * 128] = o[hh * 16:(hh + 1) * 16].astype(BF16)

    for c in plain0 + plain1 + merged1 + z0 + z1 + q_copies + out_copies:
        c.wait_send()
    for fam in range(2):
        g_sent(fam)
    for part in range(NP):
        swap_copy(part).wait_send()


def on_device(
    k_store, v_store, pos_offset, owner_map, passage_ids, rec_index, rec_count,
    fresh_q, fresh_k, fresh_v, ques_q, ques_k, ques_v,
):
    vmem = pl.BlockSpec(memory_space=pltpu.VMEM)
    anym = pl.BlockSpec(memory_space=pl.ANY)
    dma = pltpu.SemaphoreType.DMA
    v = pltpu.VMEM
    smem = pltpu.SMEM
    i32 = jnp.int32
    return pl.pallas_call(
        kernel,
        out_shape=(
            jax.ShapeDtypeStruct((RECP, HEADS * HD), BF16),
            jax.ShapeDtypeStruct((QDEV, HEADS * HD), BF16),
        ),
        in_specs=[anym] * 14,
        out_specs=(vmem, vmem),
        scratch_shapes=[
            smem((512,), i32), smem((512,), i32), smem((32,), i32), smem((1,), i32),
            v((1, 128), i32), v((1, 128), F32), v((RECP, HEADS * HD), BF16),
            v((2, RECP, 256), BF16), v((QDEV, HEADS * HD), BF16), v((2, QDEV, 128), BF16),
            v((4, 2, 4, 128, 256), BF16),
            v((NP, 2, 2, 4, TOK, 256), BF16),
            v((NP, 2, 2, 2, TOK, 256), BF16),
            v((NP, 2, 2, 2, TOK, 256), BF16),
            v((NP, 2, 4, 2, TOK, 128), BF16),
            v((8, 2, TOK, 128), BF16), v((8, 2, TOK, 128), BF16),
            v((NP, 4, 2, TOK, 128), F32),
            v((NP, 4, TOK, 128), F32),
            v((NP, 4, 2, TOK, 256), F32),
            v((NP, 16, 8 * TOK + 32, 128), BF16),
            v((2, ROWS + QROWS, 128), BF16),
            v((2, 8, 128), F32),
            v((4, 128, 2 * CHUNK), BF16),
            v((3, ROWS, 128), F32), v((3, ROWS, 256), F32),
            v((2, ROWS + QROWS, 128), BF16),
            v((2, ROWS + QROWS, 128), BF16),
            v((2, 8, 128), F32),
            v((2, 8, 128), F32),
            dma((12,)),
            dma((2, 4)),
            dma((NP, 6)), dma((NP, 6)),
            dma((NP, 7)), dma((NP, 7)),
            dma((NP,)), dma((NP,)),
            dma((2,)), dma((2,)),
            dma((NP, 4)), dma((NP, 4)),
            dma((NP, 4)), dma((NP, 4)),
            dma((NP, 8)), dma((NP, 8)),
            dma((2,)), dma((2,)),
        ],
        compiler_params=pltpu.CompilerParams(
            collective_id=0, has_side_effects=True, vmem_limit_bytes=VMEM_LIMIT
        ),
        cost_estimate=pl.CostEstimate(
            flops=8_000_000_000, bytes_accessed=4_000_000, transcendentals=15_000_000
        ),
        name="blend_attend",
    )(
        pos_offset, owner_map, passage_ids, rec_count, rec_index, jnp.asarray(freq_table()),
        fresh_q, fresh_k, fresh_v, ques_q, ques_k, ques_v,
        k_store.reshape(4, 128, 1024), v_store.reshape(4, 128, 1024),
    )


def solution(mesh):
    return jax.shard_map(
        on_device,
        mesh=mesh,
        in_specs=(
            P(("bank", "blk"), None, None),
            P(("bank", "blk"), None, None),
            P(),
            P(),
            P(),
            P("blk", None),
            P("blk"),
            P("blk", "bank"),
            P("blk", None),
            P("blk", None),
            P("blk", "bank"),
            P("blk", None),
            P("blk", None),
        ),
        out_specs=(P("blk", "bank"), P("blk", "bank")),
        check_vma=False,
    )
```

```python
import functools

import jax
import jax.numpy as jnp
import numpy as np
from jax import lax
from jax.experimental import pallas as pl
from jax.experimental.pallas import tpu as pltpu
from jax.sharding import PartitionSpec as P

HD = 128
PT = 512
RECP = 128
QDEV = 16
PASS = 32
HEADS = 6
ROWS = HEADS * RECP
QROWS = HEADS * QDEV
QSTART = PASS * PT
CHUNK = 512
NP = 4
TOK = 32
VMEM_LIMIT = 62 * 1024 * 1024
FLOOR = -1e30
SCALE = float(1.0 / np.sqrt(128.0))
MESH = pl.DeviceIdType.MESH
F32 = jnp.float32
BF16 = jnp.bfloat16

INV_2PI = float(1.0 / (2.0 * np.pi))
PI_A = 6.28125
PI_B = 0.0019350051879882812
PI_C = 3.0199159795074593e-07
SIN_C = [float((-1.0) ** k / np.prod(np.arange(1, 2 * k + 2, dtype=np.float64))) for k in range(9)]
COS_C = [float((-1.0) ** k / np.prod(np.arange(1, 2 * k + 1, dtype=np.float64))) for k in range(10)]


def freq_table():
    half = HD // 2
    freqs = 1000000.0 ** (-np.arange(half, dtype=np.float64) * 2.0 / HD)
    return np.concatenate([freqs, freqs])[None, :].astype(np.float32)


def cos_sin(pos, freq):
    angle = pos * freq
    turns = jnp.floor(angle * INV_2PI + 0.5)
    r = ((angle - turns * PI_A) - turns * PI_B) - turns * PI_C
    r2 = r * r
    s = jnp.full_like(r, SIN_C[8])
    for k in range(7, -1, -1):
        s = s * r2 + SIN_C[k]
    s = s * r
    c = jnp.full_like(r, COS_C[9])
    for k in range(8, -1, -1):
        c = c * r2 + COS_C[k]
    lane = lax.broadcasted_iota(jnp.int32, s.shape, 1)
    return c, jnp.where(lane < HD // 2, -s, s)


def turn(x, c, s):
    return x * c + pltpu.roll(x, HD // 2, 1) * s


def eye_mask(n, m):
    row = lax.broadcasted_iota(jnp.int32, (n, m), 0)
    col = lax.broadcasted_iota(jnp.int32, (n, m), 1)
    return row == col


def to_col(row, n):
    full = jnp.broadcast_to(row, (n, 128))
    return jnp.sum(jnp.where(eye_mask(n, 128), full, 0.0), axis=1, keepdims=True)


def to_row(col, n):
    return jnp.sum(jnp.where(eye_mask(n, 128), col, 0.0), axis=0, keepdims=True)


def nt_dot(a, b):
    return lax.dot_general(a, b, (((1,), (1,)), ((), ())), preferred_element_type=F32)


def kernel(
    pos_off_h, owner_map_h, pids_h, rec_count_h, rec_index_h, freq_h, fresh_q_h, fresh_k_h,
    fresh_v_h, ques_q_h, ques_k_h, ques_v_h, k_store, v_store,
    rec_out, ques_out,
    pos_off, owner_map, pids, rec_count, rec_index, freq_ref, fresh_q, fresh_kv, ques_q, ques_kv,
    stage, xfin, mbuf, msend, zsend, zin, tab, keep, repl, kvall,
    qall, qpos, kt, mst, ast,
    osend, orecv, lsend, lrecv,
    isem, lsem, xs, xr, zs, zr, bs, br, qs, qr, ps, pr, ns, nr, cs, cr, os_, or_,
):
    bank = lax.axis_index("bank")
    blk = lax.axis_index("blk")
    x = lax.div(bank, 4)
    z_hi = lax.rem(bank, 4)
    zh = lax.div(z_hi, 2)
    b1 = lax.rem(z_hi, 2)
    z_lo = lax.div(blk, 16)
    g = lax.rem(blk, 16)
    y = lax.div(g, 2)
    core = lax.rem(g, 2)
    zc = 2 * z_hi + z_lo
    z4 = 2 * b1 + z_lo
    head = 2 * x + zh

    def dev(xx, zz, gg):
        return (xx * 4 + lax.div(zz, 2), lax.rem(zz, 2) * 16 + gg)

    x_up = dev(lax.rem(x + 1, 4), zc, g)
    x_dn = dev(lax.rem(x + 3, 4), zc, g)
    y_up = dev(x, zc, lax.rem(y + 1, 8) * 2 + core)
    y_dn = dev(x, zc, lax.rem(y + 7, 8) * 2 + core)
    y_up2 = dev(x, zc, lax.rem(y + 2, 8) * 2 + core)
    y_dn2 = dev(x, zc, lax.rem(y + 6, 8) * 2 + core)
    twin = dev(x, zc, y * 2 + 1 - core)

    def z_dev(i):
        return dev(x, lax.rem(zc + i, 8), g)

    partner = dev(x, 4 * zh + 2 * b1 + 1 - z_lo, g)
    other_b = dev(x, 4 * zh + 2 * (1 - b1) + z_lo, g)

    def rcopy(src, dst, ssem, rsem, where):
        return pltpu.make_async_remote_copy(
            src_ref=src, dst_ref=dst, send_sem=ssem, recv_sem=rsem,
            device_id=where, device_id_type=MESH,
        )

    def cols(xx):
        return pl.ds(pl.multiple_of(lax.rem(xx, 4) * 256, 256), 256)

    hcol = pl.ds(pl.multiple_of(head * 128, 128), 128)

    barrier = pltpu.get_barrier_semaphore()
    peers = [x_up, x_dn, y_up, y_dn, y_up2, y_dn2, twin] + [z_dev(i) for i in range(1, 8)]
    for peer in peers:
        pl.semaphore_signal(barrier, inc=1, device_id=peer, device_id_type=MESH)

    moves = [
        (fresh_q_h, fresh_q), (rec_index_h, rec_index), (freq_h, freq_ref), (ques_q_h, ques_q),
        (ques_k_h.at[:, hcol], ques_kv.at[0]), (ques_v_h.at[:, hcol], ques_kv.at[1]),
        (owner_map_h, owner_map), (pids_h, pids), (pos_off_h, pos_off), (rec_count_h, rec_count),
        (fresh_k_h.at[:, cols(x)], fresh_kv.at[0]), (fresh_v_h.at[:, cols(x)], fresh_kv.at[1]),
    ]
    moves = [pltpu.make_async_copy(a, b, isem.at[i]) for i, (a, b) in enumerate(moves)]
    for c in moves:
        c.start()

    staged = []
    for kv, st in enumerate((k_store, v_store)):
        for t in range(4):
            c = pltpu.make_async_copy(st.at[:, :, t * 256:(t + 1) * 256], stage.at[t, kv], lsem.at[kv, t])
            c.start()
            staged.append(c)
    top = pl.ds(0, 2)
    low = pl.ds(2, 2)

    def toks(part):
        return pl.ds(part * TOK, TOK)

    for c in staged:
        c.wait()
    pl.semaphore_wait(barrier, len(peers))

    def x_relay(part):
        far = lax.rem(x + 2, 4)
        copies = [
            rcopy(stage.at[far, :, top, toks(part)], mbuf.at[part, 0], xs.at[part, 0], xr.at[part, 0], x_up),
            rcopy(stage.at[far, :, low, toks(part)], mbuf.at[part, 1], xs.at[part, 1], xr.at[part, 1], x_dn),
        ]
        for c in copies:
            c.start()
        return copies

    def x_plain(part):
        up, dn = lax.rem(x + 1, 4), lax.rem(x + 3, 4)
        copies = [
            rcopy(stage.at[up, :, low, toks(part)], xfin.at[part, 0, :, low], xs.at[part, 2], xr.at[part, 2], x_up),
            rcopy(stage.at[dn, :, top, toks(part)], xfin.at[part, 1, :, top], xs.at[part, 3], xr.at[part, 3], x_dn),
        ]
        for c in copies:
            c.start()
        return copies

    def x_merge(part, relay, owner_x):
        copies = []
        for d in range(2):
            half = (top, low)[d]
            relay[d].wait_recv()
            target = lax.rem(x + (1 if d == 0 else 3), 4)
            source = lax.rem(x + (3 if d == 0 else 1), 4)
            mine = stage[target, :, half, toks(part), :]
            msend[part, d] = jnp.where(owner_x == source, mbuf[part, d], mine)
            c = rcopy(msend.at[part, d], xfin.at[part, d, :, half], xs.at[part, 4 + d], xr.at[part, 4 + d],
                      x_up if d == 0 else x_dn)
            c.start()
            copies.append(c)
        return copies

    def x_finish(part, plain, merged, owner_x):
        at_tok = slice(part * TOK, (part + 1) * TOK)
        for c in plain + merged:
            c.wait_recv()
        is_own = owner_x == x
        from_up = owner_x == lax.rem(x + 1, 4)
        from_dn = owner_x == lax.rem(x + 3, 4)
        for kv in range(2):
            for quarter in range(4):
                sides = [xfin[part, side, kv, quarter] for side in range(2)]
                if quarter < 2:
                    data = jnp.where(from_up, sides[1], sides[0])
                else:
                    data = jnp.where(from_dn, sides[0], sides[1])
                data = jnp.where(is_own, stage[x, kv, quarter, toks(part), :], data).astype(F32)
                for hh in range(2):
                    lanes = slice(hh * 128, (hh + 1) * 128)
                    piece = data[:, lanes]
                    if kv == 0:
                        piece = turn(piece, tab[quarter, 0, at_tok], tab[quarter, 1, at_tok])
                    else:
                        piece = piece * keep[quarter, at_tok]
                    piece = piece + repl[quarter, kv, at_tok, lanes]
                    zsend[part, hh, quarter, kv] = piece.astype(BF16)
        copies = []
        for i in (1, 7, 2, 6, 3, 5, 4):
            t = lax.rem(zc + i, 8)
            c = rcopy(
                zsend.at[part, lax.div(t, 4), lax.rem(t, 4)], zin[part].at[i],
                zs.at[part, i - 1], zr.at[part, i - 1], z_dev(i),
            )
            c.start()
            copies.append(c)
        zin[part][0] = zsend[part, zh, z4]
        return copies

    def rows_of(b, kv, c):
        return pl.ds(pl.multiple_of(((b * 2 + kv) * 2 + c) * TOK, TOK), TOK)

    def half_of(b):
        return pl.ds(pl.multiple_of(b * 4 * TOK, 4 * TOK), 4 * TOK)

    def swap_copy(part):
        piece = kvall.at[part, g, half_of(b1), :]
        return rcopy(piece, piece, bs.at[part], br.at[part], other_b)

    def z_finish(part, copies):
        for c in copies:
            c.wait_recv()
        for c in range(2):
            owner_z = lax.rem(lax.div(owner_map[pids[c * 16 + g]], 32), 4)
            idx = lax.rem(zc + 8 - (2 * owner_z + c), 8)
            for kv in range(2):
                kvall[part, g, rows_of(b1, kv, c), :] = zin[part][idx, kv]
        swap_copy(part).start()
        g_start(part, 0)

    def swap_finish(part):
        piece = kvall.at[part, g, half_of(1 - b1), :]
        rcopy(piece, piece, bs.at[part], br.at[part], other_b).wait_recv()
        g_start(part, 1)

    def gather_slices(part, o, gg):
        if o < 2:
            return kvall.at[part, gg, half_of(b1 if o == 0 else 1 - b1), :]
        return kvall.at[0, gg, pl.ds(8 * TOK, 32), :]

    def reach(o):
        return (4, 3) if o % 2 == 0 else (3, 4)

    def at_y(dy):
        return lax.rem(y + 8 + dy, 8) * 2 + core

    def g_copy(part, o, dy, which, hop):
        piece = gather_slices(part, o, at_y(dy))
        fam = 2 * NP if o == 2 else 2 * part + o
        if which == "up":
            return rcopy(piece, piece, ps.at[fam, hop], pr.at[fam, hop], y_up2 if hop % 2 else y_up)
        if which == "dn":
            return rcopy(piece, piece, ns.at[fam, hop], nr.at[fam, hop], y_dn2 if hop % 2 else y_dn)
        return rcopy(piece, piece, cs.at[fam, hop], cr.at[fam, hop], twin)

    def g_send(part, o, dy, which, hop):
        g_copy(part, o, dy, which, hop).start()

    def g_arrived(part, o, dy, which, hop):
        g_copy(part, o, dy, which, hop).wait_recv()

    def g_start(part, o):
        for hop in (1, 0):
            g_send(part, o, 0, "up", hop)
            g_send(part, o, 0, "dn", hop)
        g_send(part, o, 0, "twin", 0)

    def g_first(part, o):
        n_up, n_dn = reach(o)
        g_arrived(part, o, -2, "up", 1)
        for hop in range(2, n_up):
            g_send(part, o, -2, "up", hop)
        g_arrived(part, o, 2, "dn", 1)
        for hop in range(2, n_dn):
            g_send(part, o, 2, "dn", hop)
        g_send(part, o, -2, "twin", 2)
        g_send(part, o, 2, "twin", 6)
        g_arrived(part, o, -1, "up", 0)
        g_send(part, o, -1, "twin", 1)
        g_arrived(part, o, 1, "dn", 0)
        g_send(part, o, 1, "twin", 5)

    def g_second(part, o):
        n_up, n_dn = reach(o)
        for d in range(3, n_up + 1):
            g_arrived(part, o, -d, "up", d - 1)
            g_send(part, o, -d, "twin", d)
        for d in range(3, n_dn + 1):
            g_arrived(part, o, d, "dn", d - 1)
            g_send(part, o, d, "twin", d if d == 4 else 4 + d)

    def twin_hops(o):
        n_up, n_dn = reach(o)
        return [(0, 0)] + [(-d, d) for d in range(1, n_up + 1)] + [
            (d, d if d == 4 else 4 + d) for d in range(1, n_dn + 1)
        ]

    def g_end(part, o):
        fam = 2 * NP if o == 2 else 2 * part + o
        for dy, hop in twin_hops(o):
            piece = gather_slices(part, o, lax.rem(y + 8 + dy, 8) * 2 + 1 - core)
            rcopy(piece, piece, cs.at[fam, hop], cr.at[fam, hop], twin).wait_recv()

    def g_sent(part, o):
        n_up, n_dn = reach(o)
        for hop in range(n_up):
            g_copy(part, o, 0 if hop < 2 else -2, "up", hop).wait_send()
        for hop in range(n_dn):
            g_copy(part, o, 0 if hop < 2 else 2, "dn", hop).wait_send()
        for dy, hop in twin_hops(o):
            g_copy(part, o, dy, "twin", hop).wait_send()

    relay0 = x_relay(0)
    for c in moves:
        c.wait()
    slot = owner_map[pids[blk]]
    owner_x = lax.div(slot, 128)
    off = pos_off[slot]
    count = rec_count[0]

    freq = freq_ref[...]
    rec_row = rec_index[...].astype(F32)
    off_f = off.astype(F32)
    base_f = (blk * PT).astype(F32)
    slot_lane = lax.broadcasted_iota(jnp.int32, (128, 128), 1)

    @pl.loop(0, 4)
    def _(quarter):
        first = quarter * 128
        tok = lax.broadcasted_iota(jnp.int32, (128, 128), 0) + first
        match = (tok.astype(F32) == jnp.broadcast_to(rec_row, (128, 128))) & (slot_lane < count)
        onehot = jnp.where(match, 1.0, 0.0)
        found = jnp.sum(onehot, axis=1, keepdims=True) > 0.5
        onehot = onehot.astype(BF16)
        tpos = (lax.broadcasted_iota(jnp.int32, (128, 1), 0) + first).astype(F32) + base_f
        tpos = tpos - jnp.where(found, 0.0, off_f)
        c_t, s_t = cos_sin(tpos, freq)
        rk = jnp.dot(onehot, fresh_kv[0], preferred_element_type=F32)
        for hh in range(2):
            lanes = slice(hh * 128, (hh + 1) * 128)
            repl[quarter, 0, :, lanes] = turn(rk[:, lanes], c_t, s_t)
        repl[quarter, 1] = jnp.dot(onehot, fresh_kv[1], preferred_element_type=F32)
        stay = jnp.broadcast_to(jnp.where(found, 0.0, 1.0), (128, 128))
        keep[quarter] = stay
        tab[quarter, 0] = c_t * stay
        tab[quarter, 1] = s_t * stay


    def after(copies):
        for c in copies:
            c.wait_send()

    after(relay0)
    plain0 = x_plain(0)
    merged0 = x_merge(0, relay0, owner_x)

    rec_pos_row = rec_row + (blk * PT).astype(F32)
    rec_pos = to_col(rec_pos_row, 128)
    c_rec, s_rec = cos_sin(rec_pos, freq)

    @pl.loop(0, HEADS)
    def _(hh):
        at = pl.ds(pl.multiple_of(hh * 128, 128), 128)
        q = turn(fresh_q[:, at].astype(F32), c_rec, s_rec) * SCALE
        qall[z_lo, at, :] = q.astype(BF16)

    qpos[z_lo] = jnp.broadcast_to(rec_pos_row, (8, 128))
    ques_pos = (
        lax.broadcasted_iota(jnp.int32, (QDEV, 1), 0) + (QSTART + blk * QDEV)
    ).astype(F32)
    c_q, s_q = cos_sin(ques_pos, freq)
    for hh in range(HEADS):
        lanes = slice(hh * 128, (hh + 1) * 128)
        q = turn(ques_q[:, lanes].astype(F32), c_q, s_q) * SCALE
        qall[z_lo, ROWS + hh * 16:ROWS + (hh + 1) * 16, :] = q.astype(BF16)
    q_copies = []
    for n, ref in enumerate((qall, qpos)):
        c = rcopy(ref.at[z_lo], ref.at[z_lo], qs.at[n], qr.at[n], partner)
        c.start()
        q_copies.append(c)

    kvall[0, g, 8 * TOK:8 * TOK + 16, :] = turn(ques_kv[0].astype(F32), c_q, s_q).astype(BF16)
    kvall[0, g, 8 * TOK + 16:8 * TOK + 32, :] = ques_kv[1]
    g_start(0, 2)
    after(merged0)
    relay1 = x_relay(1)
    z0 = x_finish(0, plain0, merged0, owner_x)
    after(relay1)
    plain1 = x_plain(1)
    merged1 = x_merge(1, relay1, owner_x)
    after(merged1)
    relay2 = x_relay(2)
    z1 = x_finish(1, plain1, merged1, owner_x)
    after(relay2)
    plain2 = x_plain(2)
    merged2 = x_merge(2, relay2, owner_x)
    g_first(0, 2)
    z_finish(0, z0)
    after(merged2)
    relay3 = x_relay(3)
    z2 = x_finish(2, plain2, merged2, owner_x)
    after(relay3)
    plain3 = x_plain(3)
    merged3 = x_merge(3, relay3, owner_x)
    swap_finish(0)
    z_finish(1, z1)
    g_first(0, 0)
    g_second(0, 2)
    z3 = x_finish(3, plain3, merged3, owner_x)
    g_first(0, 1)
    swap_finish(1)
    g_first(1, 0)
    z_finish(2, z2)
    g_second(0, 0)
    g_second(0, 1)
    g_first(1, 1)
    swap_finish(2)
    g_first(2, 0)
    z_finish(3, z3)
    g_second(1, 0)
    g_second(1, 1)
    g_first(2, 1)
    swap_finish(3)
    g_end(0, 2)
    g_end(0, 0)
    g_end(0, 1)
    for c in q_copies:
        c.wait_recv()

    key_lane = lax.broadcasted_iota(jnp.int32, (1, 2 * CHUNK), 1)
    key_in = lax.rem(key_lane, CHUNK)
    key_off = lax.div(key_in, TOK) * PT + lax.rem(key_in, TOK)
    key_off = (key_off + (2 * lax.div(key_lane, CHUNK) + z_lo) * 128).astype(F32)
    ones = jnp.ones((2 * CHUNK, 128), BF16)

    def chunk_of(part, b, kv, ch):
        return kvall[part, :, rows_of(b, kv, ch), :].reshape(CHUNK, 128)

    def ques_block(kv):
        first = 8 * TOK + kv * 16
        return kvall[0, :, first:first + 16, :].reshape(256, 128)

    def transpose_keys(part):
        for ch in range(2):
            for b in range(2):
                kt[ch, :, b * CHUNK:(b + 1) * CHUNK] = jnp.transpose(chunk_of(part, b, 0, ch))

    def v_chunk(part, ch):
        v = jnp.concatenate([chunk_of(part, b, 1, ch) for b in range(2)], axis=0)
        return jnp.concatenate([v, ones], axis=1)

    def fold(s):
        m = s[:, 0:128]
        for j in range(1, s.shape[1] // 128):
            m = jnp.maximum(m, s[:, j * 128:(j + 1) * 128])
        return m

    def wide(m, n):
        return jnp.concatenate([m] * (n // 128), axis=1)

    def attend(n, rows_each, q_of, part, open_chunks, closing, m_ref, a_ref):
        blocks = [(b, slice(b * rows_each, (b + 1) * rows_each)) for b in range(n)]
        when, last_keys, last_values, mask = closing

        def step(b, rows, k, v, seen):
            s = jnp.dot(q_of(b), k, preferred_element_type=F32)
            if seen is not None:
                s = jnp.where(seen, s, FLOOR)
            old = m_ref[rows, :]
            new = jnp.maximum(old, jnp.max(fold(s), axis=1, keepdims=True))
            m_ref[rows, :] = new
            p = jnp.exp(s - wide(new, s.shape[1])).astype(BF16)
            scale = wide(jnp.exp(old - new), 256)
            a_ref[rows, :] = a_ref[rows, :] * scale + jnp.dot(p, v, preferred_element_type=F32)

        @pl.loop(0, open_chunks)
        def _(ch):
            k = kt[ch]
            v = v_chunk(part, ch)
            for b, rows in blocks:
                step(b, rows, k, v, None)

        def close():
            k = last_keys()
            v = last_values()
            seen = mask()
            for b, rows in blocks:
                step(b, rows, k, v, seen)

        if when is None:
            close()
        else:
            pl.when(when)(close)

    def log_sum(m, total, n):
        return to_row(m, n) + jnp.log(jnp.maximum(to_row(total, n), 1e-30))

    lsend[...] = jnp.zeros((2, 8, 128), F32)
    mst[...] = jnp.full((3, ROWS, 128), FLOOR, F32)
    ast[...] = jnp.zeros((3, ROWS, 256), F32)

    def out_copy(n):
        a, b = ((osend, orecv), (lsend, lrecv))[n]
        return rcopy(a.at[1 - z_lo], b.at[z_lo], os_.at[n], or_.at[n], partner)

    def ques_mask():
        row = lax.broadcasted_iota(jnp.int32, (2 * QROWS, 1), 0)
        row_pos = lax.div(row, QROWS) * 256 + g * 16 + lax.rem(row, 16)
        col = lax.broadcasted_iota(jnp.int32, (1, 256), 1)
        return z_lo * 256 + col <= row_pos

    def ques_pass(part):
        closing = (
            part == 0, lambda: jnp.transpose(ques_block(0)),
            lambda: jnp.concatenate([ques_block(1), ones[0:256]], axis=1), ques_mask,
        )
        attend(
            1, 2 * QROWS, lambda b: jnp.concatenate([qall[j, ROWS:, :] for j in range(2)], axis=0),
            part, 2, closing, mst.at[2], ast.at[2],
        )

        @pl.when(part == NP - 1)
        def _():
            for src in range(2):
                rows = slice(src * QROWS, (src + 1) * QROWS)
                total = ast[2, rows, 128:256]
                osend[src, ROWS:, :] = (ast[2, rows, 0:128] / total).astype(BF16)
                lsend[src, 6:7, :] = log_sum(mst[2, rows, :], total, QROWS)

    def rec_pass(part, c):
        n_open = c
        pos_col = to_col(qpos[c, 0:1, :], 128)
        pos_col = jnp.concatenate([pos_col] * 3, axis=0)
        key_pos = key_off + (n_open * (16 * PT) + part * TOK).astype(F32)
        closing = (
            None, lambda: kt[n_open], lambda: v_chunk(part, n_open),
            lambda: key_pos <= pos_col,
        )
        attend(
            2, 384, lambda b: qall[c, b * 384:(b + 1) * 384, :],
            part, n_open, closing, mst.at[c], ast.at[c],
        )

    def rec_end(c):
        for hh in range(HEADS):
            rows = slice(hh * 128, (hh + 1) * 128)
            total = ast[c, rows, 128:256]
            osend[c, rows, :] = (ast[c, rows, 0:128] / total).astype(BF16)
            lsend[c, hh:hh + 1, :] = log_sum(mst[c, rows, :], total, 128)

    @pl.loop(0, NP)
    def _(part):
        transpose_keys(part)
        ques_pass(part)

        @pl.loop(0, 2)
        def _(t):
            @pl.when((part == 0) & (t == 0))
            def _():
                g_first(3, 0)
                g_second(2, 0)
                g_second(2, 1)
                g_first(3, 1)

            @pl.when((part == 1) & (t == 0))
            def _():
                g_second(3, 0)
                g_second(3, 1)

            c = lax.rem(z_lo + 1 + t, 2)
            rec_pass(part, c)

            @pl.when(part == NP - 1)
            def _():
                rec_end(c)

            @pl.when((part == NP - 1) & (t == 0))
            def _():
                for n in range(2):
                    out_copy(n).start()

        @pl.when(part < NP - 1)
        def _():
            g_end(part + 1, 0)
            g_end(part + 1, 1)

    orecv[z_lo] = osend[z_lo]
    lrecv[z_lo] = lsend[z_lo]
    out_copies = [out_copy(n) for n in range(2)]
    for c in out_copies:
        c.wait_recv()

    def join(parts, lses, n):
        cols_ = [to_col(l, n) for l in lses]
        top_ = functools.reduce(jnp.maximum, cols_)
        ws = [jnp.exp(c - top_) for c in cols_]
        total = ws[0] + ws[1]
        acc = ws[0] * parts[0].astype(F32)
        for w, part in zip(ws[1:], parts[1:]):
            acc = acc + w * part.astype(F32)
        return acc / total

    used = lax.broadcasted_iota(jnp.int32, (128, 1), 0) < count

    @pl.loop(0, HEADS)
    def _(hh):
        rows = pl.ds(pl.multiple_of(hh * 128, 128), 128)
        o = join([orecv[j, rows, :] for j in range(2)], [lrecv[j, pl.ds(hh, 1), :] for j in range(2)], 128)
        rec_out[:, rows] = jnp.where(used, o, 0.0).astype(BF16)

    o = join([orecv[j, ROWS:, :] for j in range(2)], [lrecv[j, 6:7, :] for j in range(2)], QROWS)
    for hh in range(HEADS):
        ques_out[:, hh * 128:(hh + 1) * 128] = o[hh * 16:(hh + 1) * 16].astype(BF16)

    for c in plain0 + plain1 + plain2 + plain3 + merged3 + z0 + z1 + z2 + z3 + q_copies + out_copies:
        c.wait_send()
    g_sent(0, 2)

    @pl.loop(0, NP)
    def _(part):
        g_sent(part, 0)
        g_sent(part, 1)
        swap_copy(part).wait_send()


def on_device(
    k_store, v_store, pos_offset, owner_map, passage_ids, rec_index, rec_count,
    fresh_q, fresh_k, fresh_v, ques_q, ques_k, ques_v,
):
    vmem = pl.BlockSpec(memory_space=pltpu.VMEM)
    anym = pl.BlockSpec(memory_space=pl.ANY)
    dma = pltpu.SemaphoreType.DMA
    v = pltpu.VMEM
    smem = pltpu.SMEM
    i32 = jnp.int32
    return pl.pallas_call(
        kernel,
        out_shape=(
            jax.ShapeDtypeStruct((RECP, HEADS * HD), BF16),
            jax.ShapeDtypeStruct((QDEV, HEADS * HD), BF16),
        ),
        in_specs=[anym] * 14,
        out_specs=(vmem, vmem),
        scratch_shapes=[
            smem((512,), i32), smem((512,), i32), smem((32,), i32), smem((1,), i32),
            v((1, 128), i32), v((1, 128), F32), v((RECP, HEADS * HD), BF16),
            v((2, RECP, 256), BF16), v((QDEV, HEADS * HD), BF16), v((2, QDEV, 128), BF16),
            v((4, 2, 4, 128, 256), BF16),
            v((NP, 2, 2, 4, TOK, 256), BF16),
            v((NP, 2, 2, 2, TOK, 256), BF16),
            v((NP, 2, 2, 2, TOK, 256), BF16),
            v((NP, 2, 4, 2, TOK, 128), BF16),
            (v((8, 2, TOK, 128), BF16),) * NP,
            v((4, 2, 128, 128), F32),
            v((4, 128, 128), F32),
            v((4, 2, 128, 256), F32),
            v((NP, 16, 8 * TOK + 32, 128), BF16),
            v((2, ROWS + QROWS, 128), BF16),
            v((2, 8, 128), F32),
            v((2, 128, 2 * CHUNK), BF16),
            v((3, ROWS, 128), F32), v((3, ROWS, 256), F32),
            v((2, ROWS + QROWS, 128), BF16),
            v((2, ROWS + QROWS, 128), BF16),
            v((2, 8, 128), F32),
            v((2, 8, 128), F32),
            dma((12,)),
            dma((2, 4)),
            dma((NP, 6)), dma((NP, 6)),
            dma((NP, 7)), dma((NP, 7)),
            dma((NP,)), dma((NP,)),
            dma((2,)), dma((2,)),
            dma((9, 4)), dma((9, 4)),
            dma((9, 4)), dma((9, 4)),
            dma((9, 8)), dma((9, 8)),
            dma((2,)), dma((2,)),
        ],
        compiler_params=pltpu.CompilerParams(
            collective_id=0, has_side_effects=True, vmem_limit_bytes=VMEM_LIMIT
        ),
        cost_estimate=pl.CostEstimate(
            flops=8_000_000_000, bytes_accessed=4_000_000, transcendentals=15_000_000
        ),
        name="blend_attend",
    )(
        pos_offset, owner_map, passage_ids, rec_count, rec_index, jnp.asarray(freq_table()),
        fresh_q, fresh_k, fresh_v, ques_q, ques_k, ques_v,
        k_store.reshape(4, 128, 1024), v_store.reshape(4, 128, 1024),
    )


def solution(mesh):
    return jax.shard_map(
        on_device,
        mesh=mesh,
        in_specs=(
            P(("bank", "blk"), None, None),
            P(("bank", "blk"), None, None),
            P(),
            P(),
            P(),
            P("blk", None),
            P("blk"),
            P("blk", "bank"),
            P("blk", None),
            P("blk", None),
            P("blk", "bank"),
            P("blk", None),
            P("blk", None),
        ),
        out_specs=(P("blk", "bank"), P("blk", "bank")),
        check_vma=False,
    )
```

```python
import functools

import jax
import jax.numpy as jnp
import numpy as np
from jax import lax
from jax.experimental import pallas as pl
from jax.experimental.pallas import tpu as pltpu
from jax.sharding import PartitionSpec as P

HD = 128
PT = 512
RECP = 128
QDEV = 16
PASS = 32
HEADS = 6
ROWS = HEADS * RECP
QROWS = HEADS * QDEV
QSTART = PASS * PT
CHUNK = 512
NP = 4
TOK = 32
VMEM_LIMIT = 62 * 1024 * 1024
FLOOR = -1e30
SCALE = float(1.0 / np.sqrt(128.0))
MESH = pl.DeviceIdType.MESH
F32 = jnp.float32
BF16 = jnp.bfloat16

INV_2PI = float(1.0 / (2.0 * np.pi))
PI_A = 6.28125
PI_B = 0.0019350051879882812
PI_C = 3.0199159795074593e-07
SIN_C = [float((-1.0) ** k / np.prod(np.arange(1, 2 * k + 2, dtype=np.float64))) for k in range(9)]
COS_C = [float((-1.0) ** k / np.prod(np.arange(1, 2 * k + 1, dtype=np.float64))) for k in range(10)]


def freq_table():
    half = HD // 2
    freqs = 1000000.0 ** (-np.arange(half, dtype=np.float64) * 2.0 / HD)
    return np.concatenate([freqs, freqs])[None, :].astype(np.float32)


def cos_sin(pos, freq):
    angle = pos * freq
    turns = jnp.floor(angle * INV_2PI + 0.5)
    r = ((angle - turns * PI_A) - turns * PI_B) - turns * PI_C
    r2 = r * r
    s = jnp.full_like(r, SIN_C[8])
    for k in range(7, -1, -1):
        s = s * r2 + SIN_C[k]
    s = s * r
    c = jnp.full_like(r, COS_C[9])
    for k in range(8, -1, -1):
        c = c * r2 + COS_C[k]
    lane = lax.broadcasted_iota(jnp.int32, s.shape, 1)
    return c, jnp.where(lane < HD // 2, -s, s)


def turn(x, c, s):
    return x * c + pltpu.roll(x, HD // 2, 1) * s


def eye_mask(n, m):
    row = lax.broadcasted_iota(jnp.int32, (n, m), 0)
    col = lax.broadcasted_iota(jnp.int32, (n, m), 1)
    return row == col


def to_col(row, n):
    full = jnp.broadcast_to(row, (n, 128))
    return jnp.sum(jnp.where(eye_mask(n, 128), full, 0.0), axis=1, keepdims=True)


def to_row(col, n):
    return jnp.sum(jnp.where(eye_mask(n, 128), col, 0.0), axis=0, keepdims=True)


def nt_dot(a, b):
    return lax.dot_general(a, b, (((1,), (1,)), ((), ())), preferred_element_type=F32)


def kernel(
    pos_off_h, owner_map_h, pids_h, rec_count_h, rec_index_h, freq_h, fresh_q_h, fresh_k_h,
    fresh_v_h, ques_q_h, ques_k_h, ques_v_h, k_store, v_store,
    rec_out, ques_out,
    pos_off, owner_map, pids, rec_count, rec_index, freq_ref, fresh_q, fresh_kv, ques_q, ques_kv,
    stage, xfin, mbuf, msend, zsend, zin, tab, keep, repl, kvall,
    qall, qpos, kt, mst, ast,
    osend, orecv, lsend, lrecv,
    isem, lsem, xs, xr, zs, zr, bs, br, qs, qr, ps, pr, ns, nr, cs, cr, os_, or_,
):
    bank = lax.axis_index("bank")
    blk = lax.axis_index("blk")
    x = lax.div(bank, 4)
    z_hi = lax.rem(bank, 4)
    zh = lax.div(z_hi, 2)
    b1 = lax.rem(z_hi, 2)
    z_lo = lax.div(blk, 16)
    g = lax.rem(blk, 16)
    y = lax.div(g, 2)
    core = lax.rem(g, 2)
    zc = 2 * z_hi + z_lo
    z4 = 2 * b1 + z_lo
    head = 2 * x + zh

    def dev(xx, zz, gg):
        return (xx * 4 + lax.div(zz, 2), lax.rem(zz, 2) * 16 + gg)

    x_up = dev(lax.rem(x + 1, 4), zc, g)
    x_dn = dev(lax.rem(x + 3, 4), zc, g)
    y_up = dev(x, zc, lax.rem(y + 1, 8) * 2 + core)
    y_dn = dev(x, zc, lax.rem(y + 7, 8) * 2 + core)
    y_up2 = dev(x, zc, lax.rem(y + 2, 8) * 2 + core)
    y_dn2 = dev(x, zc, lax.rem(y + 6, 8) * 2 + core)
    twin = dev(x, zc, y * 2 + 1 - core)

    def z_dev(i):
        return dev(x, lax.rem(zc + i, 8), g)

    partner = dev(x, 4 * zh + 2 * b1 + 1 - z_lo, g)
    other_b = dev(x, 4 * zh + 2 * (1 - b1) + z_lo, g)

    def rcopy(src, dst, ssem, rsem, where):
        return pltpu.make_async_remote_copy(
            src_ref=src, dst_ref=dst, send_sem=ssem, recv_sem=rsem,
            device_id=where, device_id_type=MESH,
        )

    def cols(xx):
        return pl.ds(pl.multiple_of(lax.rem(xx, 4) * 256, 256), 256)

    hcol = pl.ds(pl.multiple_of(head * 128, 128), 128)

    barrier = pltpu.get_barrier_semaphore()
    peers = [x_up, x_dn, y_up, y_dn, y_up2, y_dn2, twin] + [z_dev(i) for i in range(1, 8)]
    for peer in peers:
        pl.semaphore_signal(barrier, inc=1, device_id=peer, device_id_type=MESH)

    moves = [
        (fresh_q_h, fresh_q), (rec_index_h, rec_index), (freq_h, freq_ref), (ques_q_h, ques_q),
        (ques_k_h.at[:, hcol], ques_kv.at[0]), (ques_v_h.at[:, hcol], ques_kv.at[1]),
        (owner_map_h, owner_map), (pids_h, pids), (pos_off_h, pos_off), (rec_count_h, rec_count),
        (fresh_k_h.at[:, cols(x)], fresh_kv.at[0]), (fresh_v_h.at[:, cols(x)], fresh_kv.at[1]),
    ]
    moves = [pltpu.make_async_copy(a, b, isem.at[i]) for i, (a, b) in enumerate(moves)]
    for c in moves:
        c.start()

    staged = []
    for kv, st in enumerate((k_store, v_store)):
        for t in range(4):
            c = pltpu.make_async_copy(st.at[:, :, t * 256:(t + 1) * 256], stage.at[t, kv], lsem.at[kv, t])
            c.start()
            staged.append(c)
    top = pl.ds(0, 2)
    low = pl.ds(2, 2)

    def toks(part):
        return pl.ds(part * TOK, TOK)

    for c in staged:
        c.wait()
    pl.semaphore_wait(barrier, len(peers))

    def x_relay(part):
        far = lax.rem(x + 2, 4)
        copies = [
            rcopy(stage.at[far, :, top, toks(part)], mbuf.at[part, 0], xs.at[part, 0], xr.at[part, 0], x_up),
            rcopy(stage.at[far, :, low, toks(part)], mbuf.at[part, 1], xs.at[part, 1], xr.at[part, 1], x_dn),
        ]
        for c in copies:
            c.start()
        return copies

    def x_plain(part):
        up, dn = lax.rem(x + 1, 4), lax.rem(x + 3, 4)
        copies = [
            rcopy(stage.at[up, :, low, toks(part)], xfin.at[part, 0, :, low], xs.at[part, 2], xr.at[part, 2], x_up),
            rcopy(stage.at[dn, :, top, toks(part)], xfin.at[part, 1, :, top], xs.at[part, 3], xr.at[part, 3], x_dn),
        ]
        for c in copies:
            c.start()
        return copies

    def x_merge(part, relay, owner_x):
        copies = []
        for d in range(2):
            half = (top, low)[d]
            relay[d].wait_recv()
            target = lax.rem(x + (1 if d == 0 else 3), 4)
            source = lax.rem(x + (3 if d == 0 else 1), 4)
            mine = stage[target, :, half, toks(part), :]
            msend[part, d] = jnp.where(owner_x == source, mbuf[part, d], mine)
            c = rcopy(msend.at[part, d], xfin.at[part, d, :, half], xs.at[part, 4 + d], xr.at[part, 4 + d],
                      x_up if d == 0 else x_dn)
            c.start()
            copies.append(c)
        return copies

    def x_finish(part, plain, merged, owner_x):
        at_tok = slice(part * TOK, (part + 1) * TOK)
        for c in plain + merged:
            c.wait_recv()
        is_own = owner_x == x
        from_up = owner_x == lax.rem(x + 1, 4)
        from_dn = owner_x == lax.rem(x + 3, 4)
        for kv in range(2):
            for quarter in range(4):
                sides = [xfin[part, side, kv, quarter] for side in range(2)]
                if quarter < 2:
                    data = jnp.where(from_up, sides[1], sides[0])
                else:
                    data = jnp.where(from_dn, sides[0], sides[1])
                data = jnp.where(is_own, stage[x, kv, quarter, toks(part), :], data).astype(F32)
                for hh in range(2):
                    lanes = slice(hh * 128, (hh + 1) * 128)
                    piece = data[:, lanes]
                    if kv == 0:
                        piece = turn(piece, tab[quarter, 0, at_tok], tab[quarter, 1, at_tok])
                    else:
                        piece = piece * keep[quarter, at_tok]
                    piece = piece + repl[quarter, kv, at_tok, lanes]
                    zsend[part, hh, quarter, kv] = piece.astype(BF16)
        copies = []
        for i in (1, 7, 2, 6, 3, 5, 4):
            t = lax.rem(zc + i, 8)
            c = rcopy(
                zsend.at[part, lax.div(t, 4), lax.rem(t, 4)], zin[part].at[i],
                zs.at[part, i - 1], zr.at[part, i - 1], z_dev(i),
            )
            c.start()
            copies.append(c)
        zin[part][0] = zsend[part, zh, z4]
        return copies

    def rows_of(b, kv, c):
        return pl.ds(pl.multiple_of(((b * 2 + kv) * 2 + c) * TOK, TOK), TOK)

    def half_of(b):
        return pl.ds(pl.multiple_of(b * 4 * TOK, 4 * TOK), 4 * TOK)

    def swap_copy(part):
        piece = kvall.at[part, g, half_of(b1), :]
        return rcopy(piece, piece, bs.at[part], br.at[part], other_b)

    def z_finish(part, copies):
        for c in copies:
            c.wait_recv()
        for c in range(2):
            owner_z = lax.rem(lax.div(owner_map[pids[c * 16 + g]], 32), 4)
            idx = lax.rem(zc + 8 - (2 * owner_z + c), 8)
            for kv in range(2):
                kvall[part, g, rows_of(b1, kv, c), :] = zin[part][idx, kv]
        swap_copy(part).start()
        g_start(part, 0)

    def swap_finish(part):
        piece = kvall.at[part, g, half_of(1 - b1), :]
        rcopy(piece, piece, bs.at[part], br.at[part], other_b).wait_recv()
        g_start(part, 1)

    def gather_slices(part, o, gg):
        if o < 2:
            return kvall.at[part, gg, half_of(b1 if o == 0 else 1 - b1), :]
        return kvall.at[0, gg, pl.ds(8 * TOK, 32), :]

    def reach(o):
        return (4, 3) if o % 2 == 0 else (3, 4)

    def at_y(dy):
        return lax.rem(y + 8 + dy, 8) * 2 + core

    def g_copy(part, o, dy, which, hop):
        piece = gather_slices(part, o, at_y(dy))
        fam = 2 * NP if o == 2 else 2 * part + o
        if which == "up":
            return rcopy(piece, piece, ps.at[fam, hop], pr.at[fam, hop], y_up2 if hop % 2 else y_up)
        if which == "dn":
            return rcopy(piece, piece, ns.at[fam, hop], nr.at[fam, hop], y_dn2 if hop % 2 else y_dn)
        return rcopy(piece, piece, cs.at[fam, hop], cr.at[fam, hop], twin)

    def g_send(part, o, dy, which, hop):
        g_copy(part, o, dy, which, hop).start()

    def g_arrived(part, o, dy, which, hop):
        g_copy(part, o, dy, which, hop).wait_recv()

    def g_start(part, o):
        for hop in (1, 0):
            g_send(part, o, 0, "up", hop)
            g_send(part, o, 0, "dn", hop)
        g_send(part, o, 0, "twin", 0)

    def g_first(part, o):
        n_up, n_dn = reach(o)
        g_arrived(part, o, -2, "up", 1)
        for hop in range(2, n_up):
            g_send(part, o, -2, "up", hop)
        g_arrived(part, o, 2, "dn", 1)
        for hop in range(2, n_dn):
            g_send(part, o, 2, "dn", hop)
        g_send(part, o, -2, "twin", 2)
        g_send(part, o, 2, "twin", 6)
        g_arrived(part, o, -1, "up", 0)
        g_send(part, o, -1, "twin", 1)
        g_arrived(part, o, 1, "dn", 0)
        g_send(part, o, 1, "twin", 5)

    def g_second(part, o):
        n_up, n_dn = reach(o)
        for d in range(3, n_up + 1):
            g_arrived(part, o, -d, "up", d - 1)
            g_send(part, o, -d, "twin", d)
        for d in range(3, n_dn + 1):
            g_arrived(part, o, d, "dn", d - 1)
            g_send(part, o, d, "twin", d if d == 4 else 4 + d)

    def twin_hops(o):
        n_up, n_dn = reach(o)
        return [(0, 0)] + [(-d, d) for d in range(1, n_up + 1)] + [
            (d, d if d == 4 else 4 + d) for d in range(1, n_dn + 1)
        ]

    def g_end(part, o):
        fam = 2 * NP if o == 2 else 2 * part + o
        for dy, hop in twin_hops(o):
            piece = gather_slices(part, o, lax.rem(y + 8 + dy, 8) * 2 + 1 - core)
            rcopy(piece, piece, cs.at[fam, hop], cr.at[fam, hop], twin).wait_recv()

    def g_sent(part, o):
        n_up, n_dn = reach(o)
        for hop in range(n_up):
            g_copy(part, o, 0 if hop < 2 else -2, "up", hop).wait_send()
        for hop in range(n_dn):
            g_copy(part, o, 0 if hop < 2 else 2, "dn", hop).wait_send()
        for dy, hop in twin_hops(o):
            g_copy(part, o, dy, "twin", hop).wait_send()

    relays = [x_relay(part) for part in range(NP)]
    plain0 = x_plain(0)
    for c in moves:
        c.wait()
    slot = owner_map[pids[blk]]
    owner_x = lax.div(slot, 128)
    off = pos_off[slot]
    count = rec_count[0]

    freq = freq_ref[...]
    rec_row = rec_index[...].astype(F32)
    off_f = off.astype(F32)
    base_f = (blk * PT).astype(F32)
    slot_lane = lax.broadcasted_iota(jnp.int32, (128, 128), 1)

    @pl.loop(0, 4)
    def _(quarter):
        first = quarter * 128
        tok = lax.broadcasted_iota(jnp.int32, (128, 128), 0) + first
        match = (tok.astype(F32) == jnp.broadcast_to(rec_row, (128, 128))) & (slot_lane < count)
        onehot = jnp.where(match, 1.0, 0.0)
        found = jnp.sum(onehot, axis=1, keepdims=True) > 0.5
        onehot = onehot.astype(BF16)
        tpos = (lax.broadcasted_iota(jnp.int32, (128, 1), 0) + first).astype(F32) + base_f
        tpos = tpos - jnp.where(found, 0.0, off_f)
        c_t, s_t = cos_sin(tpos, freq)
        rk = jnp.dot(onehot, fresh_kv[0], preferred_element_type=F32)
        for hh in range(2):
            lanes = slice(hh * 128, (hh + 1) * 128)
            repl[quarter, 0, :, lanes] = turn(rk[:, lanes], c_t, s_t)
        repl[quarter, 1] = jnp.dot(onehot, fresh_kv[1], preferred_element_type=F32)
        stay = jnp.broadcast_to(jnp.where(found, 0.0, 1.0), (128, 128))
        keep[quarter] = stay
        tab[quarter, 0] = c_t * stay
        tab[quarter, 1] = s_t * stay


    merged0 = x_merge(0, relays[0], owner_x)
    plain1 = x_plain(1)
    merged1 = x_merge(1, relays[1], owner_x)

    rec_pos_row = rec_row + (blk * PT).astype(F32)
    rec_pos = to_col(rec_pos_row, 128)
    c_rec, s_rec = cos_sin(rec_pos, freq)

    @pl.loop(0, HEADS)
    def _(hh):
        at = pl.ds(pl.multiple_of(hh * 128, 128), 128)
        q = turn(fresh_q[:, at].astype(F32), c_rec, s_rec) * SCALE
        qall[z_lo, at, :] = q.astype(BF16)

    qpos[z_lo] = jnp.broadcast_to(rec_pos_row, (8, 128))
    ques_pos = (
        lax.broadcasted_iota(jnp.int32, (QDEV, 1), 0) + (QSTART + blk * QDEV)
    ).astype(F32)
    c_q, s_q = cos_sin(ques_pos, freq)
    for hh in range(HEADS):
        lanes = slice(hh * 128, (hh + 1) * 128)
        q = turn(ques_q[:, lanes].astype(F32), c_q, s_q) * SCALE
        qall[z_lo, ROWS + hh * 16:ROWS + (hh + 1) * 16, :] = q.astype(BF16)
    q_copies = []
    for n, ref in enumerate((qall, qpos)):
        c = rcopy(ref.at[z_lo], ref.at[z_lo], qs.at[n], qr.at[n], partner)
        c.start()
        q_copies.append(c)

    kvall[0, g, 8 * TOK:8 * TOK + 16, :] = turn(ques_kv[0].astype(F32), c_q, s_q).astype(BF16)
    kvall[0, g, 8 * TOK + 16:8 * TOK + 32, :] = ques_kv[1]
    g_start(0, 2)
    z0 = x_finish(0, plain0, merged0, owner_x)
    plain2 = x_plain(2)
    merged2 = x_merge(2, relays[2], owner_x)
    z1 = x_finish(1, plain1, merged1, owner_x)
    plain3 = x_plain(3)
    merged3 = x_merge(3, relays[3], owner_x)
    z2 = x_finish(2, plain2, merged2, owner_x)
    g_first(0, 2)
    z_finish(0, z0)
    z3 = x_finish(3, plain3, merged3, owner_x)
    swap_finish(0)
    z_finish(1, z1)
    g_first(0, 0)
    g_second(0, 2)
    g_first(0, 1)
    swap_finish(1)
    g_first(1, 0)
    z_finish(2, z2)
    g_second(0, 0)
    g_second(0, 1)
    g_first(1, 1)
    swap_finish(2)
    g_first(2, 0)
    z_finish(3, z3)
    g_second(1, 0)
    g_second(1, 1)
    g_first(2, 1)
    swap_finish(3)
    g_end(0, 2)
    g_end(0, 0)
    g_end(0, 1)
    for c in q_copies:
        c.wait_recv()

    key_lane = lax.broadcasted_iota(jnp.int32, (1, 2 * CHUNK), 1)
    key_in = lax.rem(key_lane, CHUNK)
    key_off = lax.div(key_in, TOK) * PT + lax.rem(key_in, TOK)
    key_off = (key_off + (2 * lax.div(key_lane, CHUNK) + z_lo) * 128).astype(F32)
    ones = jnp.ones((2 * CHUNK, 128), BF16)

    def chunk_of(part, b, kv, ch):
        return kvall[part, :, rows_of(b, kv, ch), :].reshape(CHUNK, 128)

    def ques_block(kv):
        first = 8 * TOK + kv * 16
        return kvall[0, :, first:first + 16, :].reshape(256, 128)

    def transpose_keys(part):
        for ch in range(2):
            for b in range(2):
                kt[ch, :, b * CHUNK:(b + 1) * CHUNK] = jnp.transpose(chunk_of(part, b, 0, ch))

    def v_chunk(part, ch):
        v = jnp.concatenate([chunk_of(part, b, 1, ch) for b in range(2)], axis=0)
        return jnp.concatenate([v, ones], axis=1)

    def fold(s):
        m = s[:, 0:128]
        for j in range(1, s.shape[1] // 128):
            m = jnp.maximum(m, s[:, j * 128:(j + 1) * 128])
        return m

    def wide(m, n):
        return jnp.concatenate([m] * (n // 128), axis=1)

    def attend(n, rows_each, q_of, part, open_chunks, closing, m_ref, a_ref):
        blocks = [(b, slice(b * rows_each, (b + 1) * rows_each)) for b in range(n)]
        when, last_keys, last_values, mask = closing

        def step(b, rows, k, v, seen):
            s = jnp.dot(q_of(b), k, preferred_element_type=F32)
            if seen is not None:
                s = jnp.where(seen, s, FLOOR)
            old = m_ref[rows, :]
            new = jnp.maximum(old, jnp.max(fold(s), axis=1, keepdims=True))
            m_ref[rows, :] = new
            p = jnp.exp(s - wide(new, s.shape[1])).astype(BF16)
            scale = wide(jnp.exp(old - new), 256)
            a_ref[rows, :] = a_ref[rows, :] * scale + jnp.dot(p, v, preferred_element_type=F32)

        @pl.loop(0, open_chunks)
        def _(ch):
            k = kt[ch]
            v = v_chunk(part, ch)
            for b, rows in blocks:
                step(b, rows, k, v, None)

        def close():
            k = last_keys()
            v = last_values()
            seen = mask()
            for b, rows in blocks:
                step(b, rows, k, v, seen)

        if when is None:
            close()
        else:
            pl.when(when)(close)

    def log_sum(m, total, n):
        return to_row(m, n) + jnp.log(jnp.maximum(to_row(total, n), 1e-30))

    lsend[...] = jnp.zeros((2, 8, 128), F32)
    mst[...] = jnp.full((3, ROWS, 128), FLOOR, F32)
    ast[...] = jnp.zeros((3, ROWS, 256), F32)

    def out_copy(n):
        a, b = ((osend, orecv), (lsend, lrecv))[n]
        return rcopy(a.at[1 - z_lo], b.at[z_lo], os_.at[n], or_.at[n], partner)

    def ques_mask():
        row = lax.broadcasted_iota(jnp.int32, (2 * QROWS, 1), 0)
        row_pos = lax.div(row, QROWS) * 256 + g * 16 + lax.rem(row, 16)
        col = lax.broadcasted_iota(jnp.int32, (1, 256), 1)
        return z_lo * 256 + col <= row_pos

    def ques_pass(part):
        closing = (
            part == 0, lambda: jnp.transpose(ques_block(0)),
            lambda: jnp.concatenate([ques_block(1), ones[0:256]], axis=1), ques_mask,
        )
        attend(
            1, 2 * QROWS, lambda b: jnp.concatenate([qall[j, ROWS:, :] for j in range(2)], axis=0),
            part, 2, closing, mst.at[2], ast.at[2],
        )

        @pl.when(part == NP - 1)
        def _():
            for src in range(2):
                rows = slice(src * QROWS, (src + 1) * QROWS)
                total = ast[2, rows, 128:256]
                osend[src, ROWS:, :] = (ast[2, rows, 0:128] / total).astype(BF16)
                lsend[src, 6:7, :] = log_sum(mst[2, rows, :], total, QROWS)

    def rec_pass(part, c):
        n_open = c
        pos_col = to_col(qpos[c, 0:1, :], 128)
        pos_col = jnp.concatenate([pos_col] * 3, axis=0)
        key_pos = key_off + (n_open * (16 * PT) + part * TOK).astype(F32)
        closing = (
            None, lambda: kt[n_open], lambda: v_chunk(part, n_open),
            lambda: key_pos <= pos_col,
        )
        attend(
            2, 384, lambda b: qall[c, b * 384:(b + 1) * 384, :],
            part, n_open, closing, mst.at[c], ast.at[c],
        )

    def rec_end(c):
        for hh in range(HEADS):
            rows = slice(hh * 128, (hh + 1) * 128)
            total = ast[c, rows, 128:256]
            osend[c, rows, :] = (ast[c, rows, 0:128] / total).astype(BF16)
            lsend[c, hh:hh + 1, :] = log_sum(mst[c, rows, :], total, 128)

    @pl.loop(0, NP)
    def _(part):
        transpose_keys(part)
        ques_pass(part)

        @pl.loop(0, 2)
        def _(t):
            @pl.when((part == 0) & (t == 0))
            def _():
                g_first(3, 0)
                g_second(2, 0)
                g_second(2, 1)
                g_first(3, 1)

            @pl.when((part == 1) & (t == 0))
            def _():
                g_second(3, 0)
                g_second(3, 1)

            c = lax.rem(z_lo + 1 + t, 2)
            rec_pass(part, c)

            @pl.when(part == NP - 1)
            def _():
                rec_end(c)

            @pl.when((part == NP - 1) & (t == 0))
            def _():
                for n in range(2):
                    out_copy(n).start()

        @pl.when(part < NP - 1)
        def _():
            g_end(part + 1, 0)
            g_end(part + 1, 1)

    orecv[z_lo] = osend[z_lo]
    lrecv[z_lo] = lsend[z_lo]
    out_copies = [out_copy(n) for n in range(2)]
    for c in out_copies:
        c.wait_recv()

    def join(parts, lses, n):
        cols_ = [to_col(l, n) for l in lses]
        top_ = functools.reduce(jnp.maximum, cols_)
        ws = [jnp.exp(c - top_) for c in cols_]
        total = ws[0] + ws[1]
        acc = ws[0] * parts[0].astype(F32)
        for w, part in zip(ws[1:], parts[1:]):
            acc = acc + w * part.astype(F32)
        return acc / total

    used = lax.broadcasted_iota(jnp.int32, (128, 1), 0) < count

    @pl.loop(0, HEADS)
    def _(hh):
        rows = pl.ds(pl.multiple_of(hh * 128, 128), 128)
        o = join([orecv[j, rows, :] for j in range(2)], [lrecv[j, pl.ds(hh, 1), :] for j in range(2)], 128)
        rec_out[:, rows] = jnp.where(used, o, 0.0).astype(BF16)

    o = join([orecv[j, ROWS:, :] for j in range(2)], [lrecv[j, 6:7, :] for j in range(2)], QROWS)
    for hh in range(HEADS):
        ques_out[:, hh * 128:(hh + 1) * 128] = o[hh * 16:(hh + 1) * 16].astype(BF16)

    for c in sum(relays, []) + merged0 + merged1 + merged2:
        c.wait_send()
    for c in plain0 + plain1 + plain2 + plain3 + merged3 + z0 + z1 + z2 + z3 + q_copies + out_copies:
        c.wait_send()
    g_sent(0, 2)

    @pl.loop(0, NP)
    def _(part):
        g_sent(part, 0)
        g_sent(part, 1)
        swap_copy(part).wait_send()


def on_device(
    k_store, v_store, pos_offset, owner_map, passage_ids, rec_index, rec_count,
    fresh_q, fresh_k, fresh_v, ques_q, ques_k, ques_v,
):
    vmem = pl.BlockSpec(memory_space=pltpu.VMEM)
    anym = pl.BlockSpec(memory_space=pl.ANY)
    dma = pltpu.SemaphoreType.DMA
    v = pltpu.VMEM
    smem = pltpu.SMEM
    i32 = jnp.int32
    return pl.pallas_call(
        kernel,
        out_shape=(
            jax.ShapeDtypeStruct((RECP, HEADS * HD), BF16),
            jax.ShapeDtypeStruct((QDEV, HEADS * HD), BF16),
        ),
        in_specs=[anym] * 14,
        out_specs=(vmem, vmem),
        scratch_shapes=[
            smem((512,), i32), smem((512,), i32), smem((32,), i32), smem((1,), i32),
            v((1, 128), i32), v((1, 128), F32), v((RECP, HEADS * HD), BF16),
            v((2, RECP, 256), BF16), v((QDEV, HEADS * HD), BF16), v((2, QDEV, 128), BF16),
            v((4, 2, 4, 128, 256), BF16),
            v((NP, 2, 2, 4, TOK, 256), BF16),
            v((NP, 2, 2, 2, TOK, 256), BF16),
            v((NP, 2, 2, 2, TOK, 256), BF16),
            v((NP, 2, 4, 2, TOK, 128), BF16),
            (v((8, 2, TOK, 128), BF16),) * NP,
            v((4, 2, 128, 128), F32),
            v((4, 128, 128), F32),
            v((4, 2, 128, 256), F32),
            v((NP, 16, 8 * TOK + 32, 128), BF16),
            v((2, ROWS + QROWS, 128), BF16),
            v((2, 8, 128), F32),
            v((2, 128, 2 * CHUNK), BF16),
            v((3, ROWS, 128), F32), v((3, ROWS, 256), F32),
            v((2, ROWS + QROWS, 128), BF16),
            v((2, ROWS + QROWS, 128), BF16),
            v((2, 8, 128), F32),
            v((2, 8, 128), F32),
            dma((12,)),
            dma((2, 4)),
            dma((NP, 6)), dma((NP, 6)),
            dma((NP, 7)), dma((NP, 7)),
            dma((NP,)), dma((NP,)),
            dma((2,)), dma((2,)),
            dma((9, 4)), dma((9, 4)),
            dma((9, 4)), dma((9, 4)),
            dma((9, 8)), dma((9, 8)),
            dma((2,)), dma((2,)),
        ],
        compiler_params=pltpu.CompilerParams(
            collective_id=0, has_side_effects=True, vmem_limit_bytes=VMEM_LIMIT
        ),
        cost_estimate=pl.CostEstimate(
            flops=8_000_000_000, bytes_accessed=4_000_000, transcendentals=15_000_000
        ),
        name="blend_attend",
    )(
        pos_offset, owner_map, passage_ids, rec_count, rec_index, jnp.asarray(freq_table()),
        fresh_q, fresh_k, fresh_v, ques_q, ques_k, ques_v,
        k_store.reshape(4, 128, 1024), v_store.reshape(4, 128, 1024),
    )


def solution(mesh):
    return jax.shard_map(
        on_device,
        mesh=mesh,
        in_specs=(
            P(("bank", "blk"), None, None),
            P(("bank", "blk"), None, None),
            P(),
            P(),
            P(),
            P("blk", None),
            P("blk"),
            P("blk", "bank"),
            P("blk", None),
            P("blk", None),
            P("blk", "bank"),
            P("blk", None),
            P("blk", None),
        ),
        out_specs=(P("blk", "bank"), P("blk", "bank")),
        check_vma=False,
    )
```

```python
import functools

import jax
import jax.numpy as jnp
import numpy as np
from jax import lax
from jax.experimental import pallas as pl
from jax.experimental.pallas import tpu as pltpu
from jax.sharding import PartitionSpec as P

HD = 128
PT = 512
RECP = 128
QDEV = 16
PASS = 32
HEADS = 6
ROWS = HEADS * RECP
QROWS = HEADS * QDEV
QSTART = PASS * PT
CHUNK = 512
NP = 2
TOK = 64
VMEM_LIMIT = 62 * 1024 * 1024
FLOOR = -1e30
SCALE = float(1.0 / np.sqrt(128.0))
MESH = pl.DeviceIdType.MESH
F32 = jnp.float32
BF16 = jnp.bfloat16

INV_2PI = float(1.0 / (2.0 * np.pi))
PI_A = 6.28125
PI_B = 0.0019350051879882812
PI_C = 3.0199159795074593e-07
SIN_C = [float((-1.0) ** k / np.prod(np.arange(1, 2 * k + 2, dtype=np.float64))) for k in range(9)]
COS_C = [float((-1.0) ** k / np.prod(np.arange(1, 2 * k + 1, dtype=np.float64))) for k in range(10)]


def freq_table():
    half = HD // 2
    freqs = 1000000.0 ** (-np.arange(half, dtype=np.float64) * 2.0 / HD)
    return np.concatenate([freqs, freqs])[None, :].astype(np.float32)


def cos_sin(pos, freq):
    angle = pos * freq
    turns = jnp.floor(angle * INV_2PI + 0.5)
    r = ((angle - turns * PI_A) - turns * PI_B) - turns * PI_C
    r2 = r * r
    s = jnp.full_like(r, SIN_C[8])
    for k in range(7, -1, -1):
        s = s * r2 + SIN_C[k]
    s = s * r
    c = jnp.full_like(r, COS_C[9])
    for k in range(8, -1, -1):
        c = c * r2 + COS_C[k]
    lane = lax.broadcasted_iota(jnp.int32, s.shape, 1)
    return c, jnp.where(lane < HD // 2, -s, s)


def turn(x, c, s):
    return x * c + pltpu.roll(x, HD // 2, 1) * s


def eye_mask(n, m):
    row = lax.broadcasted_iota(jnp.int32, (n, m), 0)
    col = lax.broadcasted_iota(jnp.int32, (n, m), 1)
    return row == col


def to_col(row, n):
    full = jnp.broadcast_to(row, (n, 128))
    return jnp.sum(jnp.where(eye_mask(n, 128), full, 0.0), axis=1, keepdims=True)


def to_row(col, n):
    return jnp.sum(jnp.where(eye_mask(n, 128), col, 0.0), axis=0, keepdims=True)


def nt_dot(a, b):
    return lax.dot_general(a, b, (((1,), (1,)), ((), ())), preferred_element_type=F32)


def kernel(
    pos_off_h, owner_map_h, pids_h, rec_count_h, rec_index_h, freq_h, fresh_q_h, fresh_k_h,
    fresh_v_h, ques_q_h, ques_k_h, ques_v_h, k_store, v_store,
    rec_out, ques_out,
    pos_off, owner_map, pids, rec_count, rec_index, freq_ref, fresh_q, fresh_kv, ques_q, ques_kv,
    xfin0, xfin1, mb00, mb01, mb10, mb11, msend, zsend, zin0, zin1, tab, keep, repl, kvall, kvq,
    qall, qpos, kt, mst, ast,
    osend, orecv, lsend, lrecv,
    isem, lsem, xs, xr, zs, zr, bs, br, qs, qr, ps, pr, ns, nr, cs, cr, os_, or_,
):
    xfin = (xfin0, xfin1)
    mbuf = ((mb00, mb01), (mb10, mb11))
    zin = (zin0, zin1)
    bank = lax.axis_index("bank")
    blk = lax.axis_index("blk")
    x = lax.div(bank, 4)
    z_hi = lax.rem(bank, 4)
    zh = lax.div(z_hi, 2)
    b1 = lax.rem(z_hi, 2)
    z_lo = lax.div(blk, 16)
    g = lax.rem(blk, 16)
    y = lax.div(g, 2)
    core = lax.rem(g, 2)
    zc = 2 * z_hi + z_lo
    z4 = 2 * b1 + z_lo
    head = 2 * x + zh

    def dev(xx, zz, gg):
        return (xx * 4 + lax.div(zz, 2), lax.rem(zz, 2) * 16 + gg)

    x_up = dev(lax.rem(x + 1, 4), zc, g)
    x_dn = dev(lax.rem(x + 3, 4), zc, g)
    y_up = dev(x, zc, lax.rem(y + 1, 8) * 2 + core)
    y_dn = dev(x, zc, lax.rem(y + 7, 8) * 2 + core)
    y_up2 = dev(x, zc, lax.rem(y + 2, 8) * 2 + core)
    y_dn2 = dev(x, zc, lax.rem(y + 6, 8) * 2 + core)
    twin = dev(x, zc, y * 2 + 1 - core)

    def z_dev(i):
        return dev(x, lax.rem(zc + i, 8), g)

    partner = dev(x, 4 * zh + 2 * b1 + 1 - z_lo, g)
    other_b = dev(x, 4 * zh + 2 * (1 - b1) + z_lo, g)

    def rcopy(src, dst, ssem, rsem, where):
        return pltpu.make_async_remote_copy(
            src_ref=src, dst_ref=dst, send_sem=ssem, recv_sem=rsem,
            device_id=where, device_id_type=MESH,
        )

    def cols(xx):
        return pl.ds(pl.multiple_of(lax.rem(xx, 4) * 256, 256), 256)

    hcol = pl.ds(pl.multiple_of(head * 128, 128), 128)

    barrier = pltpu.get_barrier_semaphore()
    peers = [x_up, x_dn, y_up, y_dn, y_up2, y_dn2, twin] + [z_dev(i) for i in range(1, 8)]
    for peer in peers:
        pl.semaphore_signal(barrier, inc=1, device_id=peer, device_id_type=MESH)

    moves = [
        (fresh_q_h, fresh_q), (rec_index_h, rec_index), (freq_h, freq_ref), (ques_q_h, ques_q),
        (ques_k_h.at[:, hcol], ques_kv.at[0]), (ques_v_h.at[:, hcol], ques_kv.at[1]),
        (owner_map_h, owner_map), (pids_h, pids), (pos_off_h, pos_off), (rec_count_h, rec_count),
        (fresh_k_h.at[:, cols(x)], fresh_kv.at[0]), (fresh_v_h.at[:, cols(x)], fresh_kv.at[1]),
    ]
    moves = [pltpu.make_async_copy(a, b, isem.at[i]) for i, (a, b) in enumerate(moves)]
    for c in moves:
        c.start()

    stores = (k_store, v_store)
    top = pl.ds(0, 2)
    low = pl.ds(2, 2)

    def toks(part):
        return pl.ds(part * TOK, TOK)

    def x_local(part):
        copies = []
        for kv in range(2):
            st = stores[kv]
            for j, (src, dst) in enumerate((
                (st.at[top, toks(part), cols(x + 1)], mbuf[part][0].at[0, kv]),
                (st.at[low, toks(part), cols(x + 3)], mbuf[part][1].at[0, kv]),
                (st.at[top, toks(part), cols(x)], xfin[part].at[0, kv, 0]),
                (st.at[low, toks(part), cols(x)], xfin[part].at[0, kv, 1]),
            )):
                c = pltpu.make_async_copy(src, dst, lsem.at[part, kv, j])
                c.start()
                copies.append(c)
        return copies

    loc = [x_local(part) for part in range(NP)]
    pl.semaphore_wait(barrier, len(peers))

    def x_relay(part):
        copies = []
        for kv in range(2):
            st = stores[kv]
            copies += [
                rcopy(st.at[top, toks(part), cols(x + 2)], mbuf[part][0].at[1, kv],
                      xs.at[part, 0, kv], xr.at[part, 0, kv], x_up),
                rcopy(st.at[low, toks(part), cols(x + 2)], mbuf[part][1].at[1, kv],
                      xs.at[part, 1, kv], xr.at[part, 1, kv], x_dn),
            ]
        for c in copies:
            c.start()
        return copies

    def x_plain(part):
        copies = []
        for kv in range(2):
            st = stores[kv]
            copies += [
                rcopy(st.at[low, toks(part), cols(x + 1)], xfin[part].at[1, kv, 1],
                      xs.at[part, 2, kv], xr.at[part, 2, kv], x_up),
                rcopy(st.at[top, toks(part), cols(x + 3)], xfin[part].at[2, kv, 0],
                      xs.at[part, 3, kv], xr.at[part, 3, kv], x_dn),
            ]
        for c in copies:
            c.start()
        return copies

    def x_merge(part, relay, owner_x):
        copies = []
        for d in range(2):
            for kv in range(2):
                loc[part][kv * 4 + d].wait()
                relay[kv * 2 + d].wait_recv()
            near = lax.rem(x + (3 if d == 0 else 1), 4)
            pick = jnp.where(owner_x == near, 1, 0)
            msend[part, d] = mbuf[part][d][pick]
            c = rcopy(msend.at[part, d], xfin[part].at[1 + d, :, d],
                      xs.at[part, 4 + d, 0], xr.at[part, 4 + d, 0], x_up if d == 0 else x_dn)
            c.start()
            copies.append(c)
        return copies

    def x_finish(part, plain, merged, owner_x, between):
        for kv in range(2):
            loc[part][kv * 4 + 2].wait()
            loc[part][kv * 4 + 3].wait()
        for c in plain + merged:
            c.wait_recv()
        is_own = owner_x == x
        idx_a = jnp.where(is_own, 0, jnp.where(owner_x == lax.rem(x + 1, 4), 2, 1))
        idx_b = jnp.where(is_own, 0, jnp.where(owner_x == lax.rem(x + 3, 4), 1, 2))
        for kv in range(2):
            for quarter in range(4):
                half = quarter // 2
                idx = idx_a if half == 0 else idx_b
                data = xfin[part][idx, kv, half, quarter % 2].astype(F32)
                for hh in range(2):
                    lanes = slice(hh * 128, (hh + 1) * 128)
                    piece = data[:, lanes]
                    if kv == 0:
                        piece = turn(piece, tab[part, quarter, 0], tab[part, quarter, 1])
                    else:
                        piece = piece * keep[part, quarter]
                    piece = piece + repl[part, quarter, kv, :, lanes]
                    zsend[part, hh, quarter, kv] = piece.astype(BF16)
            if kv == 0 and between is not None:
                between()
        copies = []
        for i in (1, 7, 2, 6, 3, 5, 4):
            t = lax.rem(zc + i, 8)
            c = rcopy(
                zsend.at[part, lax.div(t, 4), lax.rem(t, 4)], zin[part].at[i],
                zs.at[part, i - 1], zr.at[part, i - 1], z_dev(i),
            )
            c.start()
            copies.append(c)
        zin[part][0] = zsend[part, zh, z4]
        return copies

    def g_rows(gg):
        return pl.ds(pl.multiple_of(gg * TOK, TOK), TOK)

    def swap_copy(part):
        piece = kvall.at[part, b1, :, :, g_rows(g), :]
        return rcopy(piece, piece, bs.at[part], br.at[part], other_b)

    def z_finish(part, copies):
        for c in copies:
            c.wait_recv()
        for c in range(2):
            owner_z = lax.rem(lax.div(owner_map[pids[c * 16 + g]], 32), 4)
            idx = lax.rem(zc + 8 - (2 * owner_z + c), 8)
            kvall[part, b1, 0, c, g_rows(g), :] = zin[part][idx, 0]
            kvall[part, b1, 1, c, g_rows(g), :] = zin[part][idx, 1]
        swap_copy(part).start()
        g_start(2 * part)

    def swap_finish(part):
        piece = kvall.at[part, 1 - b1, :, :, g_rows(g), :]
        rcopy(piece, piece, bs.at[part], br.at[part], other_b).wait_recv()
        g_start(2 * part + 1)

    def gather_slices(fam, gg):
        if fam < 4:
            return kvall.at[fam // 2, b1 if fam % 2 == 0 else 1 - b1, :, :, g_rows(gg), :]
        return kvq.at[:, pl.ds(pl.multiple_of(gg * 16, 16), 16), :]

    def reach(fam):
        return (4, 3) if fam % 2 == 0 else (3, 4)

    def at_y(dy):
        return lax.rem(y + 8 + dy, 8) * 2 + core

    def g_copy(fam, dy, which, hop):
        piece = gather_slices(fam, at_y(dy))
        if which == "up":
            return rcopy(piece, piece, ps.at[fam, hop], pr.at[fam, hop], y_up2 if hop % 2 else y_up)
        if which == "dn":
            return rcopy(piece, piece, ns.at[fam, hop], nr.at[fam, hop], y_dn2 if hop % 2 else y_dn)
        return rcopy(piece, piece, cs.at[fam, hop], cr.at[fam, hop], twin)

    def g_send(fam, dy, which, hop):
        g_copy(fam, dy, which, hop).start()

    def g_arrived(fam, dy, which, hop):
        g_copy(fam, dy, which, hop).wait_recv()

    def g_start(fam):
        for hop in range(2):
            g_send(fam, 0, "up", hop)
            g_send(fam, 0, "dn", hop)
        g_send(fam, 0, "twin", 0)

    def g_first(fam):
        n_up, n_dn = reach(fam)
        g_arrived(fam, -2, "up", 1)
        for hop in range(2, n_up):
            g_send(fam, -2, "up", hop)
        g_arrived(fam, 2, "dn", 1)
        for hop in range(2, n_dn):
            g_send(fam, 2, "dn", hop)
        g_send(fam, -2, "twin", 2)
        g_send(fam, 2, "twin", 6)
        g_arrived(fam, -1, "up", 0)
        g_send(fam, -1, "twin", 1)
        g_arrived(fam, 1, "dn", 0)
        g_send(fam, 1, "twin", 5)

    def g_second(fam):
        n_up, n_dn = reach(fam)
        for d in range(3, n_up + 1):
            g_arrived(fam, -d, "up", d - 1)
            g_send(fam, -d, "twin", d)
        for d in range(3, n_dn + 1):
            g_arrived(fam, d, "dn", d - 1)
            g_send(fam, d, "twin", d if d == 4 else 4 + d)

    def twin_hops(fam):
        n_up, n_dn = reach(fam)
        return [(0, 0)] + [(-d, d) for d in range(1, n_up + 1)] + [
            (d, d if d == 4 else 4 + d) for d in range(1, n_dn + 1)
        ]

    def g_end(fam):
        for dy, hop in twin_hops(fam):
            piece = gather_slices(fam, lax.rem(y + 8 + dy, 8) * 2 + 1 - core)
            rcopy(piece, piece, cs.at[fam, hop], cr.at[fam, hop], twin).wait_recv()

    def g_sent(fam):
        n_up, n_dn = reach(fam)
        for hop in range(n_up):
            g_copy(fam, 0 if hop < 2 else -2, "up", hop).wait_send()
        for hop in range(n_dn):
            g_copy(fam, 0 if hop < 2 else 2, "dn", hop).wait_send()
        for dy, hop in twin_hops(fam):
            g_copy(fam, dy, "twin", hop).wait_send()

    relay0 = x_relay(0)
    for c in moves:
        c.wait()
    slot = owner_map[pids[blk]]
    owner_x = lax.div(slot, 128)
    off = pos_off[slot]
    count = rec_count[0]

    freq = freq_ref[...]
    rec_row = rec_index[...].astype(F32)
    rec_pos_row = rec_row + (blk * PT).astype(F32)
    rec_pos = to_col(rec_pos_row, 128)
    c_rec, s_rec = cos_sin(rec_pos, freq)

    @pl.loop(0, HEADS)
    def _(hh):
        at = pl.ds(pl.multiple_of(hh * 128, 128), 128)
        q = turn(fresh_q[:, at].astype(F32), c_rec, s_rec) * SCALE
        qall[z_lo, at, :] = q.astype(BF16)

    qpos[z_lo] = jnp.broadcast_to(rec_pos_row, (8, 128))
    for c in relay0:
        c.wait_send()
    plain0 = x_plain(0)
    ques_pos = (
        lax.broadcasted_iota(jnp.int32, (QDEV, 1), 0) + (QSTART + blk * QDEV)
    ).astype(F32)
    c_q, s_q = cos_sin(ques_pos, freq)
    for hh in range(HEADS):
        lanes = slice(hh * 128, (hh + 1) * 128)
        q = turn(ques_q[:, lanes].astype(F32), c_q, s_q) * SCALE
        qall[z_lo, ROWS + hh * 16:ROWS + (hh + 1) * 16, :] = q.astype(BF16)
    q_copies = []
    for n, ref in enumerate((qall, qpos)):
        c = rcopy(ref.at[z_lo], ref.at[z_lo], qs.at[n], qr.at[n], partner)
        c.start()
        q_copies.append(c)

    my_rows = pl.ds(pl.multiple_of(g * 16, 16), 16)
    kvq[0, my_rows, :] = turn(ques_kv[0].astype(F32), c_q, s_q).astype(BF16)
    kvq[1, my_rows, :] = ques_kv[1]
    merged0 = x_merge(0, relay0, owner_x)
    g_start(4)

    off_f = off.astype(F32)
    base_f = (blk * PT).astype(F32)
    slot_lane = lax.broadcasted_iota(jnp.int32, (TOK, 128), 1)

    def tables(part):
        @pl.loop(0, 4)
        def _(quarter):
            first = quarter * 128 + part * TOK
            tok = lax.broadcasted_iota(jnp.int32, (TOK, 128), 0) + first
            match = (tok.astype(F32) == jnp.broadcast_to(rec_row, (TOK, 128))) & (slot_lane < count)
            onehot = jnp.where(match, 1.0, 0.0)
            found = jnp.sum(onehot, axis=1, keepdims=True) > 0.5
            onehot = onehot.astype(BF16)
            tpos = (lax.broadcasted_iota(jnp.int32, (TOK, 1), 0) + first).astype(F32) + base_f
            tpos = tpos - jnp.where(found, 0.0, off_f)
            c_t, s_t = cos_sin(tpos, freq)
            rk = jnp.dot(onehot, fresh_kv[0], preferred_element_type=F32)
            for hh in range(2):
                lanes = slice(hh * 128, (hh + 1) * 128)
                repl[part, quarter, 0, :, lanes] = turn(rk[:, lanes], c_t, s_t)
            repl[part, quarter, 1] = jnp.dot(onehot, fresh_kv[1], preferred_element_type=F32)
            stay = jnp.broadcast_to(jnp.where(found, 0.0, 1.0), (TOK, 128))
            keep[part, quarter] = stay
            tab[part, quarter, 0] = c_t * stay
            tab[part, quarter, 1] = s_t * stay

    tables(0)
    for c in merged0:
        c.wait_send()
    relay1 = x_relay(1)
    tables(1)
    plain1 = []

    def go_plain1():
        for c in relay1:
            c.wait_send()
        plain1.extend(x_plain(1))

    z0 = x_finish(0, plain0, merged0, owner_x, go_plain1)
    merged1 = x_merge(1, relay1, owner_x)
    g_first(4)
    g_second(4)
    z_finish(0, z0)
    z1 = x_finish(1, plain1, merged1, owner_x, None)
    swap_finish(0)
    g_first(0)
    z_finish(1, z1)
    g_first(1)
    swap_finish(1)
    g_second(0)
    g_second(1)
    g_end(4)
    g_end(0)
    g_end(1)
    for c in q_copies:
        c.wait_recv()

    key_lane = lax.broadcasted_iota(jnp.int32, (1, 2 * CHUNK), 1)
    key_in = lax.rem(key_lane, CHUNK)
    key_off = lax.div(key_in, TOK) * PT + lax.rem(key_in, TOK)
    key_off = (key_off + (2 * lax.div(key_lane, CHUNK) + z_lo) * 128).astype(F32)
    ones = jnp.ones((2 * CHUNK, 128), BF16)

    def chunk_of(part, b, kv, ch):
        rows = pl.ds(pl.multiple_of(lax.rem(ch, 2) * CHUNK, CHUNK), CHUNK)
        return kvall[part, b, kv, lax.div(ch, 2), rows, :]

    def transpose_keys(part):
        @pl.loop(0, 4)
        def _(ch):
            for b in range(2):
                kt[ch, :, b * CHUNK:(b + 1) * CHUNK] = jnp.transpose(chunk_of(part, b, 0, ch))

    def v_chunk(part, ch):
        v = jnp.concatenate([chunk_of(part, b, 1, ch) for b in range(2)], axis=0)
        return jnp.concatenate([v, ones], axis=1)

    def fold(s):
        m = s[:, 0:128]
        for j in range(1, s.shape[1] // 128):
            m = jnp.maximum(m, s[:, j * 128:(j + 1) * 128])
        return m

    def wide(m, n):
        return jnp.concatenate([m] * (n // 128), axis=1)

    def attend(n, rows_each, q_of, part, open_chunks, closing, m_ref, a_ref):
        blocks = [(b, slice(b * rows_each, (b + 1) * rows_each)) for b in range(n)]
        when, last_keys, last_values, mask = closing

        def step(b, rows, k, v, seen):
            s = jnp.dot(q_of(b), k, preferred_element_type=F32)
            if seen is not None:
                s = jnp.where(seen, s, FLOOR)
            old = m_ref[rows, :]
            new = jnp.maximum(old, jnp.max(fold(s), axis=1, keepdims=True))
            m_ref[rows, :] = new
            p = jnp.exp(s - wide(new, s.shape[1])).astype(BF16)
            scale = wide(jnp.exp(old - new), 256)
            a_ref[rows, :] = a_ref[rows, :] * scale + jnp.dot(p, v, preferred_element_type=F32)

        @pl.loop(0, open_chunks)
        def _(ch):
            k = kt[ch]
            v = v_chunk(part, ch)
            for b, rows in blocks:
                step(b, rows, k, v, None)

        def close():
            k = last_keys()
            v = last_values()
            seen = mask()
            for b, rows in blocks:
                step(b, rows, k, v, seen)

        if when is None:
            close()
        else:
            pl.when(when)(close)

    def log_sum(m, total, n):
        return to_row(m, n) + jnp.log(jnp.maximum(to_row(total, n), 1e-30))

    lsend[...] = jnp.zeros((2, 8, 128), F32)
    mst[...] = jnp.full((3, ROWS, 128), FLOOR, F32)
    ast[...] = jnp.zeros((3, ROWS, 256), F32)

    def out_copy(n):
        a, b = ((osend, orecv), (lsend, lrecv))[n]
        return rcopy(a.at[1 - z_lo], b.at[z_lo], os_.at[n], or_.at[n], partner)

    def ques_mask():
        row = lax.broadcasted_iota(jnp.int32, (2 * QROWS, 1), 0)
        row_pos = lax.div(row, QROWS) * 256 + g * 16 + lax.rem(row, 16)
        col = lax.broadcasted_iota(jnp.int32, (1, 256), 1)
        return z_lo * 256 + col <= row_pos

    def ques_pass(part):
        closing = (
            part == 0, lambda: jnp.transpose(kvq[0]),
            lambda: jnp.concatenate([kvq[1], ones[0:256]], axis=1), ques_mask,
        )
        attend(
            1, 2 * QROWS, lambda b: jnp.concatenate([qall[j, ROWS:, :] for j in range(2)], axis=0),
            part, 4, closing, mst.at[2], ast.at[2],
        )

        @pl.when(part == NP - 1)
        def _():
            for src in range(2):
                rows = slice(src * QROWS, (src + 1) * QROWS)
                total = ast[2, rows, 128:256]
                osend[src, ROWS:, :] = (ast[2, rows, 0:128] / total).astype(BF16)
                lsend[src, 6:7, :] = log_sum(mst[2, rows, :], total, QROWS)

    def rec_pass(part, c):
        n_open = 2 * c + lax.div(g, 8)
        pos_col = to_col(qpos[c, 0:1, :], 128)
        pos_col = jnp.concatenate([pos_col] * 3, axis=0)
        key_pos = key_off + (n_open * (8 * PT) + part * TOK).astype(F32)
        closing = (
            None, lambda: kt[n_open], lambda: v_chunk(part, n_open),
            lambda: key_pos <= pos_col,
        )
        attend(
            2, 384, lambda b: qall[c, b * 384:(b + 1) * 384, :],
            part, n_open, closing, mst.at[c], ast.at[c],
        )

    def rec_end(c):
        for hh in range(HEADS):
            rows = slice(hh * 128, (hh + 1) * 128)
            total = ast[c, rows, 128:256]
            osend[c, rows, :] = (ast[c, rows, 0:128] / total).astype(BF16)
            lsend[c, hh:hh + 1, :] = log_sum(mst[c, rows, :], total, 128)

    @pl.loop(0, NP)
    def _(part):
        transpose_keys(part)
        ques_pass(part)

        @pl.loop(0, 2)
        def _(t):
            @pl.when((part == 0) & (t == 0))
            def _():
                g_first(2)
                g_first(3)

            @pl.when((part == 0) & (t == 1))
            def _():
                g_second(2)
                g_second(3)

            c = lax.rem(z_lo + 1 + t, 2)
            rec_pass(part, c)

            @pl.when(part == NP - 1)
            def _():
                rec_end(c)

            @pl.when((part == NP - 1) & (t == 0))
            def _():
                for n in range(2):
                    out_copy(n).start()

        @pl.when(part == 0)
        def _():
            g_end(2)
            g_end(3)

    orecv[z_lo] = osend[z_lo]
    lrecv[z_lo] = lsend[z_lo]
    out_copies = [out_copy(n) for n in range(2)]
    for c in out_copies:
        c.wait_recv()

    def join(parts, lses, n):
        cols_ = [to_col(l, n) for l in lses]
        top_ = functools.reduce(jnp.maximum, cols_)
        ws = [jnp.exp(c - top_) for c in cols_]
        total = ws[0] + ws[1]
        acc = ws[0] * parts[0].astype(F32)
        for w, part in zip(ws[1:], parts[1:]):
            acc = acc + w * part.astype(F32)
        return acc / total

    used = lax.broadcasted_iota(jnp.int32, (128, 1), 0) < count

    @pl.loop(0, HEADS)
    def _(hh):
        rows = pl.ds(pl.multiple_of(hh * 128, 128), 128)
        o = join([orecv[j, rows, :] for j in range(2)], [lrecv[j, pl.ds(hh, 1), :] for j in range(2)], 128)
        rec_out[:, rows] = jnp.where(used, o, 0.0).astype(BF16)

    o = join([orecv[j, ROWS:, :] for j in range(2)], [lrecv[j, 6:7, :] for j in range(2)], QROWS)
    for hh in range(HEADS):
        ques_out[:, hh * 128:(hh + 1) * 128] = o[hh * 16:(hh + 1) * 16].astype(BF16)

    for c in plain0 + plain1 + merged1 + z0 + z1 + q_copies + out_copies:
        c.wait_send()
    for fam in range(5):
        g_sent(fam)
    for part in range(NP):
        swap_copy(part).wait_send()


def on_device(
    k_store, v_store, pos_offset, owner_map, passage_ids, rec_index, rec_count,
    fresh_q, fresh_k, fresh_v, ques_q, ques_k, ques_v,
):
    vmem = pl.BlockSpec(memory_space=pltpu.VMEM)
    anym = pl.BlockSpec(memory_space=pl.ANY)
    dma = pltpu.SemaphoreType.DMA
    v = pltpu.VMEM
    smem = pltpu.SMEM
    i32 = jnp.int32
    return pl.pallas_call(
        kernel,
        out_shape=(
            jax.ShapeDtypeStruct((RECP, HEADS * HD), BF16),
            jax.ShapeDtypeStruct((QDEV, HEADS * HD), BF16),
        ),
        in_specs=[anym] * 14,
        out_specs=(vmem, vmem),
        scratch_shapes=[
            smem((512,), i32), smem((512,), i32), smem((32,), i32), smem((1,), i32),
            v((1, 128), i32), v((1, 128), F32), v((RECP, HEADS * HD), BF16),
            v((2, RECP, 256), BF16), v((QDEV, HEADS * HD), BF16), v((2, QDEV, 128), BF16),
            v((3, 2, 2, 2, TOK, 256), BF16), v((3, 2, 2, 2, TOK, 256), BF16),
            v((2, 2, 2, TOK, 256), BF16), v((2, 2, 2, TOK, 256), BF16),
            v((2, 2, 2, TOK, 256), BF16), v((2, 2, 2, TOK, 256), BF16),
            v((NP, 2, 2, 2, TOK, 256), BF16),
            v((NP, 2, 4, 2, TOK, 128), BF16),
            v((8, 2, TOK, 128), BF16), v((8, 2, TOK, 128), BF16),
            v((NP, 4, 2, TOK, 128), F32),
            v((NP, 4, TOK, 128), F32),
            v((NP, 4, 2, TOK, 256), F32),
            v((NP, 2, 2, 2, 16 * TOK, 128), BF16),
            v((2, 256, 128), BF16),
            v((2, ROWS + QROWS, 128), BF16),
            v((2, 8, 128), F32),
            v((4, 128, 2 * CHUNK), BF16),
            v((3, ROWS, 128), F32), v((3, ROWS, 256), F32),
            v((2, ROWS + QROWS, 128), BF16),
            v((2, ROWS + QROWS, 128), BF16),
            v((2, 8, 128), F32),
            v((2, 8, 128), F32),
            dma((12,)),
            dma((NP, 2, 4)),
            dma((NP, 6, 2)), dma((NP, 6, 2)),
            dma((NP, 7)), dma((NP, 7)),
            dma((NP,)), dma((NP,)),
            dma((2,)), dma((2,)),
            dma((5, 4)), dma((5, 4)),
            dma((5, 4)), dma((5, 4)),
            dma((5, 8)), dma((5, 8)),
            dma((2,)), dma((2,)),
        ],
        compiler_params=pltpu.CompilerParams(
            collective_id=0, has_side_effects=True, vmem_limit_bytes=VMEM_LIMIT
        ),
        cost_estimate=pl.CostEstimate(
            flops=8_000_000_000, bytes_accessed=4_000_000, transcendentals=15_000_000
        ),
        name="blend_attend",
    )(
        pos_offset, owner_map, passage_ids, rec_count, rec_index, jnp.asarray(freq_table()),
        fresh_q, fresh_k, fresh_v, ques_q, ques_k, ques_v,
        k_store.reshape(4, 128, 1024), v_store.reshape(4, 128, 1024),
    )


def solution(mesh):
    return jax.shard_map(
        on_device,
        mesh=mesh,
        in_specs=(
            P(("bank", "blk"), None, None),
            P(("bank", "blk"), None, None),
            P(),
            P(),
            P(),
            P("blk", None),
            P("blk"),
            P("blk", "bank"),
            P("blk", None),
            P("blk", None),
            P("blk", "bank"),
            P("blk", None),
            P("blk", None),
        ),
        out_specs=(P("blk", "bank"), P("blk", "bank")),
        check_vma=False,
    )
```
